128 devices in a mesh: lat: 8 (over x, core), lon: 16 (over z, y).
Axes of the slice: x: 4, y: 4, z: 4, core: 2. Of those that a mesh axis runs over, the one named last changes fastest.
Arguments:
- grid_inputs: bfloat16 [384, 1024, 2, 227], P('lat', 'lon'), may hold values from -6 to 6
- mesh_latents: bfloat16 [4096, 512], P(('lat', 'lon')), may hold values from -6 to 6
- g2m_edges: bfloat16 [16384, 512], P(('lat', 'lon')), may hold values from -6 to 6
- g2m_sender: int32 [16384], P(('lat', 'lon')), may hold values from 0 to 393215, as said below
- g2m_receiver: int32 [16384], P(('lat', 'lon')), may hold values from 0 to 31
- mesh_edges: bfloat16 [32768, 512], P(('lat', 'lon')), may hold values from -6 to 6
- mesh_sender: int32 [32768], P(('lat', 'lon')), may hold values from 0 to 4095, as said below
- mesh_receiver: int32 [32768], P(('lat', 'lon')), may hold values from 0 to 31
- embed_w1: bfloat16 [227, 512], replicated, may hold values from -0.375 to 0.375
- embed_b1: float32 [512], replicated, may hold values from -3 to 3
- embed_w2: bfloat16 [512, 512], replicated, may hold values from -0.25 to 0.25
- embed_gain: float32 [512], replicated, may hold values from 0.5 to 1.5
- enc_edge_w1: bfloat16 [3, 512, 512], replicated, may hold values from -0.15625 to 0.15625
- enc_edge_b1: float32 [512], replicated, may hold values from -3 to 3
- enc_edge_w2: bfloat16 [512, 512], replicated, may hold values from -0.25 to 0.25
- enc_edge_gain: float32 [512], replicated, may hold values from 0.5 to 1.5
- enc_node_w1: bfloat16 [2, 512, 512], replicated, may hold values from -0.1875 to 0.1875
- enc_node_b1: float32 [512], replicated, may hold values from -3 to 3
- enc_node_w2: bfloat16 [512, 512], replicated, may hold values from -0.25 to 0.25
- enc_node_gain: float32 [512], replicated, may hold values from 0.5 to 1.5
- proc_edge_w1: bfloat16 [2, 3, 512, 512], replicated, may hold values from -0.15625 to 0.15625
- proc_edge_b1: float32 [2, 512], replicated, may hold values from -3 to 3
- proc_edge_w2: bfloat16 [2, 512, 512], replicated, may hold values from -0.25 to 0.25
- proc_edge_gain: float32 [2, 512], replicated, may hold values from 0.5 to 1.5
- proc_node_w1: bfloat16 [2, 2, 512, 512], replicated, may hold values from -0.1875 to 0.1875
- proc_node_b1: float32 [2, 512], replicated, may hold values from -3 to 3
- proc_node_w2: bfloat16 [2, 512, 512], replicated, may hold values from -0.25 to 0.25
- proc_node_gain: float32 [2, 512], replicated, may hold values from 0.5 to 1.5
Outputs:
- mesh_out: bfloat16 [4096, 2, 512], P(('lat', 'lon'))
The draws below stay inside these ranges and needn't reach their ends.
Inputs may be any that keep to these rules, and one draw needn't show every extreme that they name: `g2m_sender`: A grid id is row * 1024 + column. The edges of one device's block (128 rows; devices in mesh order, lat slowest) start at grid rows within 2 of that device's 48 rows (kept inside the grid) and at columns within 2 of its 64 columns, counted around the globe. `mesh_sender`: A mesh id is the owning device's index in mesh order (lat slowest) times 32 plus its row there. A device beside another is one whose lat index differs by at most one (no wrap) and whose lon index differs by at most one counted around. Among the senders named in one device's block of 256 edges, exactly 4 distinct ones belong to each device beside it; senders of devices not beside it come from exactly 16 such devices, exactly 1 distinct ones from each.
All inputs are finite; a program needn't handle non-finite values.
Results may differ from the reference program's by a relative error of at most 0.02.
Values may be sent and summed in bfloat16 or wider, within the bound.
A program may use at most 128 MiB of HBM per device.

```python
import jax
import jax.numpy as jnp
from jax import lax

D = 512
IN = 227
BATCH = 2
LAT_DEV = 48
LON_DEV = 64
HALO = 2
MESH_DEV = 32
DEGREE = 8
G2M_DEGREE = 4
STEPS = 2
FAR_PEERS = 16
CAP = 1
GLAT = 384
GLON = 1024
MESH = 4096
G2M_EDGES = 16384
MESH_EDGES = 32768
N_LAT = 8
N_LON = 16


def draw_g2m_sender(key, part):
    key = jax.random.fold_in(key, 11)
    devices = N_LAT * N_LON
    per_device = G2M_DEGREE * MESH_DEV
    row_key, col_key = jax.random.split(key)
    row_offsets = jax.random.randint(row_key, (devices, per_device), -HALO, LAT_DEV + HALO)
    col_offsets = jax.random.randint(col_key, (devices, per_device), -HALO, LON_DEV + HALO)
    row_offsets = row_offsets.at[:, 0].set(LAT_DEV + HALO - 1).at[:, 1].set(-HALO)
    col_offsets = col_offsets.at[:, 0].set(LON_DEV - 1).at[:, 1].set(0)
    device = jnp.arange(devices, dtype=jnp.int32)
    grid_rows = jnp.clip((device // N_LON)[:, None] * LAT_DEV + row_offsets, 0, LAT_DEV * N_LAT - 1)
    grid_cols = jnp.remainder((device % N_LON)[:, None] * LON_DEV + col_offsets, LON_DEV * N_LON)
    return (grid_rows * (LON_DEV * N_LON) + grid_cols).reshape(-1).astype(jnp.int32)


def shuffle_order(key):
    devices = N_LAT * N_LON
    per_device = DEGREE * MESH_DEV
    shuffle_key = jax.random.fold_in(key, 77)
    shuffle_scores = jax.random.randint(shuffle_key, (devices, per_device), 0, 2 ** 20) * per_device + jnp.arange(per_device, dtype=jnp.int32)
    return jnp.argsort(shuffle_scores, axis=1, stable=True)


def receiver_targets(key):
    target_key = jax.random.fold_in(key, 37)
    devices = N_LAT * N_LON
    per_device = DEGREE * MESH_DEV
    head_width = 8 * (MESH_DEV // 8) + FAR_PEERS * CAP
    targets = jax.random.randint(target_key, (devices, per_device), 0, MESH_DEV)
    targets = targets.at[:, head_width:head_width + DEGREE].set(0)
    targets = targets.at[:, head_width + DEGREE].set(MESH_DEV - 1)
    return targets


def draw_mesh_receiver(key, part):
    order = shuffle_order(key)
    targets = receiver_targets(key)
    targets = jnp.take_along_axis(targets, order, axis=1)
    return targets.reshape(-1).astype(jnp.int32)


def draw_mesh_sender(key, part):
    order = shuffle_order(key)
    targets = receiver_targets(key)
    key = jax.random.fold_in(key, 23)
    devices = N_LAT * N_LON
    per_device = DEGREE * MESH_DEV
    near_count = MESH_DEV // 8
    subkeys = jax.random.split(key, 5)
    device = jnp.arange(devices, dtype=jnp.int32)
    device_lat = device // N_LON
    device_lon = device % N_LON
    self_base = device[:, None] * MESH_DEV
    step_lat = jnp.array([-1, -1, -1, 0, 0, 1, 1, 1], dtype=jnp.int32)
    step_lon = jnp.array([-1, 0, 1, -1, 1, -1, 0, 1], dtype=jnp.int32)
    near_lat = device_lat[:, None] + step_lat[None, :]
    near_valid = (near_lat >= 0) & (near_lat < N_LAT)
    near_owner = jnp.clip(near_lat, 0, N_LAT - 1) * N_LON + jnp.remainder(device_lon[:, None] + step_lon[None, :], N_LON)
    near_scores = jax.random.randint(subkeys[0], (devices, 8, MESH_DEV), 0, 2 ** 20) * MESH_DEV + jnp.arange(MESH_DEV, dtype=jnp.int32)
    _, near_rows = lax.top_k(near_scores, near_count)
    near_ids = near_owner[:, :, None] * MESH_DEV + near_rows.astype(jnp.int32)
    self_fill = self_base[:, :, None] + jax.random.randint(subkeys[1], (devices, 8, near_count), 0, MESH_DEV)
    near_ids = jnp.where(near_valid[:, :, None], near_ids, self_fill).reshape(devices, 8 * near_count)
    lat_gap = jnp.abs(device_lat[:, None] - device_lat[None, :])
    lon_gap = jnp.remainder(device_lon[:, None] - device_lon[None, :] + 1, N_LON) - 1
    close = (lat_gap <= 1) & (lon_gap <= 1)
    far_scores = jax.random.randint(subkeys[2], (devices, devices), 0, 2 ** 20) * devices + device[None, :]
    opposite = jnp.remainder(device[:, None] + devices // 2, devices) == device[None, :]
    far_scores = jnp.where(opposite, 2 ** 30, far_scores)
    far_scores = jnp.where(close, -1, far_scores)
    _, far_owner = lax.top_k(far_scores, FAR_PEERS)
    far_row_scores = jax.random.randint(subkeys[3], (devices, FAR_PEERS, MESH_DEV), 0, 2 ** 20) * MESH_DEV + jnp.arange(MESH_DEV, dtype=jnp.int32)
    _, far_rows = lax.top_k(far_row_scores, CAP)
    far_ids = (far_owner.astype(jnp.int32)[:, :, None] * MESH_DEV + far_rows.astype(jnp.int32)).reshape(devices, FAR_PEERS * CAP)
    head = jnp.concatenate([near_ids, far_ids], axis=1)
    head_width = 8 * near_count + FAR_PEERS * CAP
    sources = self_base + jax.random.randint(subkeys[4], (devices, per_device), 0, MESH_DEV)
    sources = sources.at[:, :head_width].set(head)
    repeated = jnp.broadcast_to(far_ids[:, 0:1], (devices, DEGREE))
    sources = sources.at[:, head_width:head_width + DEGREE].set(repeated)
    tail_pick = 1 + jnp.remainder(targets, FAR_PEERS * CAP - 1)
    tail_ids = jnp.take_along_axis(far_ids, tail_pick, axis=1)
    position = jnp.arange(per_device, dtype=jnp.int32)
    in_tail = position >= head_width + DEGREE
    sources = jnp.where(in_tail[None, :], tail_ids, sources)
    sources = sources.at[:, per_device - 1].set(self_base[:, 0] + MESH_DEV - 1)
    sources = sources.at[:, per_device - 2].set(self_base[:, 0])
    sources = jnp.take_along_axis(sources, order, axis=1)
    return sources.reshape(-1).astype(jnp.int32)


def touch_ends(entries, key, smallest, largest):
    place = [jax.random.randint(jax.random.fold_in(key, axis), (), 0, length) for axis, length in enumerate(entries.shape)]
    longest = entries.shape.index(max(entries.shape))
    next_to = place[:longest] + [(place[longest] + 1) % entries.shape[longest]] + place[longest + 1:]
    return entries.at[tuple(place)].set(smallest).at[tuple(next_to)].set(largest)


def steps_of(rng, dims, shards, low, largest):
    def one(dim, shards_of):
        steps = jax.random.uniform(jax.random.fold_in(jax.random.fold_in(rng, 6), dim), (shards_of,), jnp.float32, low / len(shards), largest / len(shards))
        return jnp.repeat(jnp.exp(steps), dims[dim] // shards_of).reshape((-1,) + (1,) * (len(dims) - dim - 1))

    factor_of = one(*shards[0])
    for cut in shards[1:]:
        factor_of = factor_of * one(*cut)
    return factor_of


def noise(own_key, extent, width, bound, shards=(), held_as=jnp.bfloat16):
    drawn = jax.random.normal(own_key, extent, jnp.float32) * width
    if len(shards) > 0:
        drawn = steps_of(own_key, extent, shards, -0.22, 0.18) * drawn
    return jnp.clip(drawn, min=-bound, max=bound).astype(held_as)


def setup_inputs(seed: int = 0) -> dict:
    arg_keys = jax.random.split(jax.random.key(seed), 29)
    return {
        "grid_inputs": noise(arg_keys[0], (GLAT, GLON, BATCH, IN), 1.0, 6.0, ((0, 8), (1, 16))),
        "mesh_latents": noise(arg_keys[1], (MESH, D), 1.0, 6.0, ((0, 128),)),
        "g2m_edges": noise(arg_keys[2], (G2M_EDGES, D), 1.0, 6.0, ((0, 128),)),
        "g2m_sender": draw_g2m_sender(jax.random.fold_in(arg_keys[28], 71), 0),
        "g2m_receiver": touch_ends(jax.random.randint(arg_keys[4], (G2M_EDGES,), 0, MESH_DEV), jax.random.fold_in(arg_keys[4], 1), 0, MESH_DEV - 1).astype(jnp.int32),
        "mesh_edges": noise(arg_keys[5], (MESH_EDGES, D), 1.0, 6.0, ((0, 128),)),
        "mesh_sender": draw_mesh_sender(jax.random.fold_in(arg_keys[28], 71), 0),
        "mesh_receiver": draw_mesh_receiver(jax.random.fold_in(arg_keys[28], 71), 0),
        "embed_w1": noise(arg_keys[8], (IN, D), IN ** -0.5, 0.375),
        "embed_b1": noise(arg_keys[9], (D,), 0.5, 3.0, (), jnp.float32),
        "embed_w2": noise(arg_keys[10], (D, D), D ** -0.5, 0.25),
        "embed_gain": jnp.clip(1.0 + 0.1 * jax.random.normal(arg_keys[11], (D,), jnp.float32), 0.5, 1.5),
        "enc_edge_w1": noise(arg_keys[12], (3, D, D), (3 * D) ** -0.5, 0.15625),
        "enc_edge_b1": noise(arg_keys[13], (D,), 0.5, 3.0, (), jnp.float32),
        "enc_edge_w2": noise(arg_keys[14], (D, D), D ** -0.5, 0.25),
        "enc_edge_gain": jnp.clip(1.0 + 0.1 * jax.random.normal(arg_keys[15], (D,), jnp.float32), 0.5, 1.5),
        "enc_node_w1": noise(arg_keys[16], (2, D, D), (2 * D) ** -0.5, 0.1875),
        "enc_node_b1": noise(arg_keys[17], (D,), 0.5, 3.0, (), jnp.float32),
        "enc_node_w2": noise(arg_keys[18], (D, D), D ** -0.5, 0.25),
        "enc_node_gain": jnp.clip(1.0 + 0.1 * jax.random.normal(arg_keys[19], (D,), jnp.float32), 0.5, 1.5),
        "proc_edge_w1": noise(arg_keys[20], (STEPS, 3, D, D), (3 * D) ** -0.5, 0.15625),
        "proc_edge_b1": noise(arg_keys[21], (STEPS, D), 0.5, 3.0, (), jnp.float32),
        "proc_edge_w2": noise(arg_keys[22], (STEPS, D, D), D ** -0.5, 0.25),
        "proc_edge_gain": jnp.clip(1.0 + 0.1 * jax.random.normal(arg_keys[23], (STEPS, D), jnp.float32), 0.5, 1.5),
        "proc_node_w1": noise(arg_keys[24], (STEPS, 2, D, D), (2 * D) ** -0.5, 0.1875),
        "proc_node_b1": noise(arg_keys[25], (STEPS, D), 0.5, 3.0, (), jnp.float32),
        "proc_node_w2": noise(arg_keys[26], (STEPS, D, D), D ** -0.5, 0.25),
        "proc_node_gain": jnp.clip(1.0 + 0.1 * jax.random.normal(arg_keys[27], (STEPS, D), jnp.float32), 0.5, 1.5),
    }


def layer_norm(values, gain_vector):
    row_mean = lax.optimization_barrier(jnp.mean(values, axis=-1, keepdims=True))
    centered = values - row_mean
    variance = lax.optimization_barrier(jnp.mean(centered * centered, axis=-1, keepdims=True))
    return centered * lax.rsqrt(variance + 1e-05) * gain_vector

def embed_grid(inputs, embed_w1, embed_b1, embed_w2, embed_gain, send_weight):
    hidden = jax.nn.silu(jnp.dot(inputs, embed_w1, preferred_element_type=jnp.float32) + embed_b1).astype(jnp.bfloat16)
    latent = layer_norm(jnp.dot(hidden, embed_w2, preferred_element_type=jnp.float32), embed_gain).astype(jnp.bfloat16)
    return jnp.dot(latent, send_weight, preferred_element_type=jnp.float32).astype(jnp.bfloat16)

def edge_update(edge_rows, first_weight, senders, receivers, bias_vector, second_weight, gain_vector):
    preact = jnp.dot(edge_rows, first_weight, preferred_element_type=jnp.float32)
    preact = preact + senders.astype(jnp.float32) + receivers.astype(jnp.float32) + bias_vector
    hidden = jax.nn.silu(preact).astype(jnp.bfloat16)
    update = layer_norm(jnp.dot(hidden, second_weight, preferred_element_type=jnp.float32), gain_vector)
    return (edge_rows.astype(jnp.float32) + update).astype(jnp.bfloat16)

def node_update(state_rows, summed, first_weights, bias_vector, second_weight, gain_vector):
    preact = jnp.dot(state_rows, first_weights[0], preferred_element_type=jnp.float32)
    preact = preact + jnp.dot(summed, first_weights[1], preferred_element_type=jnp.float32) + bias_vector
    hidden = jax.nn.silu(preact).astype(jnp.bfloat16)
    update = layer_norm(jnp.dot(hidden, second_weight, preferred_element_type=jnp.float32), gain_vector)
    return (state_rows.astype(jnp.float32) + update).astype(jnp.bfloat16)

def segment_total(edge_rows, targets):
    summed = jax.ops.segment_sum(edge_rows.astype(jnp.float32), targets, num_segments=MESH_DEV)
    return summed.astype(jnp.bfloat16)

def reference(grid_inputs, mesh_latents, g2m_edges, g2m_sender, g2m_receiver, mesh_edges, mesh_sender, mesh_receiver, embed_w1, embed_b1, embed_w2, embed_gain, enc_edge_w1, enc_edge_b1, enc_edge_w2, enc_edge_gain, enc_node_w1, enc_node_b1, enc_node_w2, enc_node_gain, proc_edge_w1, proc_edge_b1, proc_edge_w2, proc_edge_gain, proc_node_w1, proc_node_b1, proc_node_w2, proc_node_gain):
    devices = N_LAT * N_LON

    def embed_row(row_inputs):
        return embed_grid(row_inputs, embed_w1, embed_b1, embed_w2, embed_gain, enc_edge_w1[1])
    grid_send = lax.map(embed_row, grid_inputs)
    grid_flat = grid_send.reshape(GLAT * GLON, BATCH, D)
    mesh_recv = jnp.dot(mesh_latents, enc_edge_w1[2], preferred_element_type=jnp.float32).astype(jnp.bfloat16)

    def encode_block(block_items):
        edge_rows, sources, targets, own_latent, own_recv = block_items
        senders = grid_flat[sources]
        receivers = own_recv[targets][:, None, :]
        new_edges = edge_update(edge_rows[:, None, :], enc_edge_w1[0], senders, receivers, enc_edge_b1, enc_edge_w2, enc_edge_gain)
        summed = segment_total(new_edges, targets)
        return node_update(own_latent[:, None, :], summed, enc_node_w1, enc_node_b1, enc_node_w2, enc_node_gain)
    mesh_state = lax.map(encode_block, (g2m_edges.reshape(devices, G2M_DEGREE * MESH_DEV, D), g2m_sender.reshape(devices, G2M_DEGREE * MESH_DEV), g2m_receiver.reshape(devices, G2M_DEGREE * MESH_DEV), mesh_latents.reshape(devices, MESH_DEV, D), mesh_recv.reshape(devices, MESH_DEV, D)))
    edge_state = mesh_edges.reshape(devices, DEGREE * MESH_DEV, 1, D)
    sources_all = mesh_sender.reshape(devices, DEGREE * MESH_DEV)
    targets_all = mesh_receiver.reshape(devices, DEGREE * MESH_DEV)
    for layer_index in range(STEPS):
        flat_state = mesh_state.reshape(MESH, BATCH, D)
        proc_send = jnp.dot(flat_state, proc_edge_w1[layer_index, 1], preferred_element_type=jnp.float32).astype(jnp.bfloat16)
        proc_recv = jnp.dot(mesh_state, proc_edge_w1[layer_index, 2], preferred_element_type=jnp.float32).astype(jnp.bfloat16)

        def process_block(block_items, layer_index=layer_index, proc_send=proc_send):
            edge_rows, sources, targets, own_state, own_recv = block_items
            new_edges = edge_update(edge_rows, proc_edge_w1[layer_index, 0], proc_send[sources], own_recv[targets], proc_edge_b1[layer_index], proc_edge_w2[layer_index], proc_edge_gain[layer_index])
            summed = segment_total(new_edges, targets)
            new_state = node_update(own_state, summed, proc_node_w1[layer_index], proc_node_b1[layer_index], proc_node_w2[layer_index], proc_node_gain[layer_index])
            return (new_edges, new_state)
        edge_state, mesh_state = lax.map(process_block, (edge_state, sources_all, targets_all, mesh_state, proc_recv))
    return mesh_state.reshape(MESH, BATCH, D)
```

```python
from typing import Any, NamedTuple

import jax
import jax.numpy as jnp
from jax import lax
from jax.experimental import pallas as pl
from jax.experimental.pallas import tpu as pltpu
from jax.sharding import PartitionSpec as P

BF = jnp.bfloat16
F32 = jnp.float32
I32 = jnp.int32
MESH = pl.DeviceIdType.MESH

BATCH = 2
D = 512
HALO = 2
STEPS = 2
LATS = 8
LONS = 16
PAIRS = LATS * LONS
NODES = 32
GRID_EDGES = 128
EDGES = 256
NEAR = (1, 15, 16, 17, 31, 112, 113, 127)
EXTRA = 3
SLOTS = PAIRS + EXTRA * len(NEAR)
DIRECTIONS = tuple((a, b) for a in (0, -1, 1) for b in (0, -1, 1) if (a, b) != (0, 0))


class Given(NamedTuple):
    grid_inputs: Any
    mesh_latents: Any
    g2m_edges: Any
    g2m_sender: Any
    g2m_receiver: Any
    mesh_edges: Any
    mesh_sender: Any
    mesh_receiver: Any
    embed_w1: Any
    embed_b1: Any
    embed_w2: Any
    embed_gain: Any
    enc_edge_w1: Any
    enc_edge_b1: Any
    enc_edge_w2: Any
    enc_edge_gain: Any
    enc_node_w1: Any
    enc_node_b1: Any
    enc_node_w2: Any
    enc_node_gain: Any
    proc_edge_w1: Any
    proc_edge_b1: Any
    proc_edge_w2: Any
    proc_edge_gain: Any
    proc_node_w1: Any
    proc_node_b1: Any
    proc_node_w2: Any
    proc_node_gain: Any


class Held(NamedTuple):
    g2m_receiver: Any
    mesh_sender: Any
    mesh_receiver: Any
    mesh_latents: Any
    g2m_edges: Any
    enc_edge_w1: Any
    enc_edge_b1: Any
    embed_w1: Any
    embed_b1: Any
    embed_w2: Any
    embed_gain: Any
    enc_edge_w2: Any
    enc_edge_gain: Any
    enc_node_w1: Any
    enc_node_b1: Any
    enc_node_w2: Any
    enc_node_gain: Any
    mesh_edges: Any
    proc_edge_w1: Any
    proc_edge_b1: Any
    proc_edge_w2: Any
    proc_edge_gain: Any
    proc_node_w1: Any
    proc_node_b1: Any
    proc_node_w2: Any
    proc_node_gain: Any


FETCHED = len(Held._fields)


def mm(a, b):
    return jnp.dot(a, b, preferred_element_type=F32)


def mm_nt(a, b):
    return lax.dot_general(a, b, (((1,), (1,)), ((), ())), preferred_element_type=F32)


def iota(shape, dim):
    return lax.broadcasted_iota(I32, shape, dim)


def hot(mask):
    return jnp.where(mask, 1.0, 0.0).astype(BF)


def silu(v):
    half = 0.5 * v
    return half + half * jnp.tanh(half)


def norm(v, gain):
    centered = v - jnp.mean(v, axis=-1, keepdims=True)
    variance = jnp.mean(centered * centered, axis=-1, keepdims=True)
    return centered * lax.rsqrt(variance + 1e-05) * gain


def doubled_column(row, count):
    shape = (2 * count, count)
    spread = jnp.where(iota(shape, 1) == (iota(shape, 0) >> 1), row.astype(F32), 0.0)
    return jnp.sum(spread, axis=1, keepdims=True).astype(I32)


def doubled_row(row, count):
    shape = (count, 2 * count)
    return mm(row.astype(F32).astype(BF), hot((iota(shape, 1) >> 1) == iota(shape, 0))).astype(I32)


def kernel(*refs):
    grid_hbm, sender_hbm = refs[:2]
    hbm = refs[2 : 2 + FETCHED]
    out_ref = refs[2 + FETCHED]
    refs = refs[3 + FETCHED :]
    held = Held(*refs[:FETCHED])
    (
        cells, sender, picked, pick_all, gather_far, gather_own, gather_recv, edge_base,
        req_out, req_in, out_rows, in_rows,
        fetch_sem, cells_sem, sender_sem,
        halo_send, halo_recv, req_send, req_recv, row_send, row_recv,
    ) = refs[FETCHED:]

    lat = lax.axis_index("lat")
    lon = lax.axis_index("lon")
    lat_rows, lon_cols = grid_hbm.shape[:2]

    sender_copy = pltpu.make_async_copy(sender_hbm, sender, sender_sem)
    sender_copy.start()
    fetches = [
        pltpu.make_async_copy(hbm[n], held[n], fetch_sem.at[n]) for n in range(FETCHED)
    ]
    fetch = Held(*fetches)

    def ready(*copies):
        for copy in copies:
            copy.wait()

    for copy in fetches[:3]:
        copy.start()
    cells_copy = pltpu.make_async_copy(
        grid_hbm, cells.at[pl.ds(HALO, lat_rows), pl.ds(HALO, lon_cols)], cells_sem
    )
    cells_copy.start()
    for copy in fetches[3:]:
        copy.start()

    def place(step_lat, step_lon, sign):
        return (
            (lat + sign * step_lat + LATS) & (LATS - 1),
            (lon + sign * step_lon + LONS) & (LONS - 1),
        )

    def for_all_others(act):
        for step_lon in range(1, LONS):
            act(0, step_lon)

        def band(step_lat, carry):
            for step_lon in range(LONS):
                act(step_lat, step_lon)
            return carry

        lax.fori_loop(1, LATS, band, 0)

    barrier = pltpu.get_barrier_semaphore()

    def greet(step_lat, step_lon):
        pl.semaphore_signal(
            barrier, inc=1, device_id=place(step_lat, step_lon, 1), device_id_type=MESH
        )

    for_all_others(greet)

    ready(fetch.g2m_receiver, fetch.mesh_sender, fetch.mesh_receiver)
    senders = held.mesh_sender[...]
    owner = senders >> 5
    row = senders & (NODES - 1)
    rel = ((((owner >> 4) - lat) & (LATS - 1)) << 4) | (((owner & 15) - lon) & (LONS - 1))
    owner2 = hot((iota((2 * PAIRS, EDGES), 0) >> 1) == rel)
    row2 = hot((iota((128, EDGES), 0) >> 1) == row)
    asked = mm_nt(owner2, row2)
    shape = (2 * PAIRS, 128)
    same = (iota(shape, 0) & 1) == (iota(shape, 1) & 1)
    asked = hot((asked > 0.5) & same & (iota(shape, 0) >= 2))
    req_out[...] = asked.reshape(PAIRS, 2, 128)
    req_in[0] = jnp.zeros((2, 128), BF)
    for t in range(STEPS):
        in_rows[t, 0] = jnp.zeros((2, D), BF)

    pl.semaphore_wait(barrier, PAIRS - 1)

    spans = {0: (0, lat_rows, HALO), -1: (0, HALO, HALO + lat_rows), 1: (lat_rows - HALO, HALO, 0)}
    spans_lon = {
        0: (0, lon_cols, HALO), -1: (0, HALO, HALO + lon_cols), 1: (lon_cols - HALO, HALO, 0)
    }
    halo = []
    for n, (a, b) in enumerate(DIRECTIONS):
        row0, rows, to_row = spans[a]
        col0, cols, to_col = spans_lon[b]
        halo.append(
            pltpu.make_async_remote_copy(
                src_ref=grid_hbm.at[pl.ds(row0, rows), pl.ds(col0, cols)],
                dst_ref=cells.at[pl.ds(to_row, rows), pl.ds(to_col, cols)],
                send_sem=halo_send.at[n],
                recv_sem=halo_recv.at[n],
                device_id=((lat + a + LATS) & (LATS - 1), (lon + b + LONS) & (LONS - 1)),
                device_id_type=MESH,
            )
        )
    groups = [
        [copy for copy, (a, _) in zip(halo, DIRECTIONS) if a == which] for which in (0, -1, 1)
    ]
    has_before = lat > 0
    has_after = lat < LATS - 1

    for copy in groups[0]:
        copy.start()

    @pl.when(has_before)
    def _():
        for copy in groups[1]:
            copy.start()

    @pl.when(has_after)
    def _():
        for copy in groups[2]:
            copy.start()

    def ask(step_lat, step_lon):
        i = step_lat * LONS + step_lon
        pltpu.make_async_remote_copy(
            src_ref=req_out.at[i], dst_ref=req_in.at[i], send_sem=req_send, recv_sem=req_recv,
            device_id=place(step_lat, step_lon, 1), device_id_type=MESH,
        ).start()

    for_all_others(ask)

    owner1 = hot(iota((PAIRS, EDGES), 0) == rel)
    row1 = iota((NODES, EDGES), 0) == row
    needed = hot(mm_nt(hot(row1), owner1) > 0.5)
    below = hot(iota((NODES, NODES), 1) < iota((NODES, NODES), 0))
    order = mm(below, needed).astype(BF)
    rank = jnp.sum(jnp.where(row1, mm(order, owner1), 0.0), axis=0, keepdims=True).astype(I32)
    near = jnp.zeros_like(rel)
    for n, i in enumerate(NEAR):
        near = jnp.where(rel == i, n, near)
    slot = jnp.where(rank == 0, rel, PAIRS + EXTRA * near + rank - 1)
    slot = jnp.where(rel == 0, SLOTS + row, slot)
    slot_column = doubled_column(slot, EDGES)
    shape = (2 * EDGES, 2 * (SLOTS + NODES))
    gather = hot(iota(shape, 1) == 2 * slot_column + (iota(shape, 0) & 1))
    gather_far[...] = gather[:, : 2 * SLOTS]
    gather_own[...] = gather[:, 2 * SLOTS :]
    receivers = held.mesh_receiver[...]
    shape = (2 * EDGES, 2 * NODES)
    gather_recv[...] = hot(
        iota(shape, 1) == 2 * doubled_column(receivers, EDGES) + (iota(shape, 0) & 1)
    )
    shape = (2 * NODES, 2 * EDGES)
    total_mesh = hot(iota(shape, 0) == 2 * doubled_row(receivers, EDGES) + (iota(shape, 1) & 1))

    grid_receivers = held.g2m_receiver[...]
    shape = (2 * NODES, 2 * GRID_EDGES)
    total_grid = hot(
        iota(shape, 0) == 2 * doubled_row(grid_receivers, GRID_EDGES) + (iota(shape, 1) & 1)
    )
    shape = (2 * GRID_EDGES, NODES)
    gather_grid_recv = hot(iota(shape, 1) == doubled_column(grid_receivers, GRID_EDGES))

    ready(fetch.mesh_latents, fetch.g2m_edges, fetch.enc_edge_w1, fetch.enc_edge_b1)
    latents = held.mesh_latents[...]
    shape = (2 * GRID_EDGES, GRID_EDGES)
    grid_edges = mm(hot(iota(shape, 1) == (iota(shape, 0) >> 1)), held.g2m_edges[...]).astype(BF)
    mesh_recv = mm(latents, held.enc_edge_w1[2]).astype(BF)
    grid_base = (
        mm(grid_edges, held.enc_edge_w1[0])
        + mm(gather_grid_recv, mesh_recv)
        + held.enc_edge_b1[...]
    )
    shape = (2 * NODES, NODES)
    state = mm(hot(iota(shape, 1) == (iota(shape, 0) >> 1)), latents).astype(BF)
    ready(fetch.mesh_edges)
    shape = (2 * EDGES, EDGES)
    edge_state = mm(
        hot(iota(shape, 1) == (iota(shape, 0) >> 1)), held.mesh_edges[...]
    ).astype(BF)

    sender_copy.wait()
    cells_copy.wait()
    for copy in groups[0]:
        copy.wait_recv()

    @pl.when(has_after)
    def _():
        for copy in groups[1]:
            copy.wait_recv()

    @pl.when(has_before)
    def _():
        for copy in groups[2]:
            copy.wait_recv()

    width = lon_cols * LONS

    def pick(k, carry):
        cell = sender[k]
        cell_row = (cell // width) - lat * lat_rows + HALO
        cell_col = ((cell & (width - 1)) - lon * lon_cols + HALO + width) & (width - 1)
        cell_row = jnp.clip(cell_row, 0, cells.shape[0] - 1)
        cell_col = jnp.clip(cell_col, 0, cells.shape[1] - 1)
        picked[k] = cells[cell_row, cell_col]
        return carry

    lax.fori_loop(0, GRID_EDGES, pick, 0, unroll=8)

    ready(fetch.embed_w1, fetch.embed_b1, fetch.embed_w2, fetch.embed_gain)
    inputs = picked[...].reshape(2 * GRID_EDGES, picked.shape[2])
    hidden = silu(mm(inputs, held.embed_w1[...]) + held.embed_b1[...]).astype(BF)
    latent = norm(mm(hidden, held.embed_w2[...]), held.embed_gain[...]).astype(BF)
    preact = mm(latent, held.enc_edge_w1[1]) + grid_base
    hidden = silu(preact).astype(BF)
    ready(fetch.enc_edge_w2, fetch.enc_edge_gain)
    update = norm(mm(hidden, held.enc_edge_w2[...]), held.enc_edge_gain[...])
    new_edges = (grid_edges.astype(F32) + update).astype(BF)
    summed = mm(total_grid, new_edges).astype(BF)
    ready(fetch.enc_node_w1, fetch.enc_node_b1, fetch.enc_node_w2, fetch.enc_node_gain)
    preact = (
        mm(state, held.enc_node_w1[0])
        + mm(summed, held.enc_node_w1[1])
        + held.enc_node_b1[...]
    )
    hidden = silu(preact).astype(BF)
    update = norm(mm(hidden, held.enc_node_w2[...]), held.enc_node_gain[...])
    state = (state.astype(F32) + update).astype(BF)

    pltpu.make_async_copy(
        req_in.at[pl.ds(1, PAIRS - 1)], req_in.at[pl.ds(1, PAIRS - 1)], req_recv
    ).wait()
    wanted = req_in[...].reshape(2 * PAIRS, 128)[:, : 2 * NODES]
    shape = (2 * NODES, 2 * NODES)
    before = hot(
        (iota(shape, 0) < iota(shape, 1)) & ((iota(shape, 0) & 1) == (iota(shape, 1) & 1))
    )
    place_of = mm(wanted, before).astype(BF)
    first = jnp.where(place_of.astype(F32) < 0.5, wanted.astype(F32), 0.0).astype(BF)
    shape = (2 * EXTRA * len(NEAR), 2 * PAIRS)
    line = iota(shape, 0)
    which = jnp.zeros_like(line)
    target = jnp.full_like(line, NEAR[0])
    for n in range(1, len(NEAR)):
        later = line >= 2 * EXTRA * n
        which = jnp.where(later, n, which)
        target = jnp.where(later, NEAR[n], target)
    choose = hot(iota(shape, 1) == 2 * target + (line & 1))
    kth = ((line >> 1) - EXTRA * which + 1).astype(F32)[:, : 2 * NODES]
    more = jnp.where(mm(choose, place_of) == kth, mm(choose, wanted), 0.0).astype(BF)
    pick_all[: 2 * PAIRS] = first
    pick_all[2 * PAIRS :] = more

    ready(fetch.proc_edge_w1, fetch.proc_edge_b1, fetch.proc_edge_w2, fetch.proc_edge_gain)
    ready(fetch.proc_node_w1, fetch.proc_node_b1, fetch.proc_node_w2, fetch.proc_node_gain)
    for t in range(STEPS):
        outgoing = mm(state, held.proc_edge_w1[t, 1]).astype(BF)
        out_rows[t] = mm(pick_all[...], outgoing).astype(BF).reshape(SLOTS, 2, D)

        def give(step_lat, step_lon, t=t):
            i = step_lat * LONS + step_lon
            pltpu.make_async_remote_copy(
                src_ref=out_rows.at[t, i], dst_ref=in_rows.at[t, i],
                send_sem=row_send.at[t], recv_sem=row_recv.at[t],
                device_id=place(step_lat, step_lon, -1), device_id_type=MESH,
            ).start()

        for_all_others(give)
        for n, i in enumerate(NEAR):
            span = pl.ds(PAIRS + EXTRA * n, EXTRA)
            pltpu.make_async_remote_copy(
                src_ref=out_rows.at[t, span], dst_ref=in_rows.at[t, span],
                send_sem=row_send.at[t], recv_sem=row_recv.at[t],
                device_id=place(i // LONS, i % LONS, -1), device_id_type=MESH,
            ).start()

        incoming = mm(state, held.proc_edge_w1[t, 2]).astype(BF)
        edge_base[...] = (
            mm(edge_state, held.proc_edge_w1[t, 0])
            + mm(gather_recv[...], incoming)
            + mm(gather_own[...], outgoing)
            + held.proc_edge_b1[t : t + 1]
        )
        node_base = mm(state, held.proc_node_w1[t, 0]) + held.proc_node_b1[t : t + 1]

        arrived = in_rows.at[t, pl.ds(1, SLOTS - 1)]
        pltpu.make_async_copy(arrived, arrived, row_recv.at[t]).wait()
        table = in_rows[t].reshape(2 * SLOTS, D)
        hidden = silu(edge_base[...] + mm(gather_far[...], table)).astype(BF)
        update = norm(mm(hidden, held.proc_edge_w2[t]), held.proc_edge_gain[t : t + 1])
        edge_state = (edge_state.astype(F32) + update).astype(BF)
        summed = mm(total_mesh, edge_state).astype(BF)
        hidden = silu(node_base + mm(summed, held.proc_node_w1[t, 1])).astype(BF)
        update = norm(mm(hidden, held.proc_node_w2[t]), held.proc_node_gain[t : t + 1])
        state = (state.astype(F32) + update).astype(BF)

    out_ref[...] = state.reshape(NODES, 2, D)

    for copy in groups[0]:
        copy.wait_send()

    @pl.when(has_before)
    def _():
        for copy in groups[1]:
            copy.wait_send()

    @pl.when(has_after)
    def _():
        for copy in groups[2]:
            copy.wait_send()

    asked_all = req_out.at[pl.ds(1, PAIRS - 1)]
    pltpu.make_async_copy(asked_all, asked_all, req_send).wait()
    for t in range(STEPS):
        sent = out_rows.at[t, pl.ds(1, SLOTS - 1)]
        pltpu.make_async_copy(sent, sent, row_send.at[t]).wait()


def on_device(*args):
    given = Given(*args)
    lat_rows, lon_cols, batch, width = given.grid_inputs.shape

    def flat(row):
        return row.reshape(1, row.shape[0])

    wanted = Held(
        flat(given.g2m_receiver),
        flat(given.mesh_sender),
        flat(given.mesh_receiver),
        given.mesh_latents,
        given.g2m_edges,
        given.enc_edge_w1,
        flat(given.enc_edge_b1),
        given.embed_w1,
        flat(given.embed_b1),
        given.embed_w2,
        flat(given.embed_gain),
        given.enc_edge_w2,
        flat(given.enc_edge_gain),
        given.enc_node_w1,
        flat(given.enc_node_b1),
        given.enc_node_w2,
        flat(given.enc_node_gain),
        given.mesh_edges,
        given.proc_edge_w1,
        given.proc_edge_b1,
        given.proc_edge_w2,
        given.proc_edge_gain,
        given.proc_node_w1,
        given.proc_node_b1,
        given.proc_node_w2,
        given.proc_node_gain,
    )
    operands = [given.grid_inputs, given.g2m_sender, *wanted]
    dma = pltpu.SemaphoreType.DMA
    scratch = [pltpu.VMEM(part.shape, part.dtype) for part in wanted]
    scratch += [
        pltpu.VMEM((lat_rows + 2 * HALO, lon_cols + 2 * HALO, batch, width), BF),
        pltpu.SMEM((GRID_EDGES,), I32),
        pltpu.VMEM((GRID_EDGES, batch, width), BF),
        pltpu.VMEM((2 * SLOTS, 2 * NODES), BF),
        pltpu.VMEM((2 * EDGES, 2 * SLOTS), BF),
        pltpu.VMEM((2 * EDGES, 2 * NODES), BF),
        pltpu.VMEM((2 * EDGES, 2 * NODES), BF),
        pltpu.VMEM((2 * EDGES, D), F32),
        pltpu.VMEM((PAIRS, 2, 128), BF),
        pltpu.VMEM((PAIRS, 2, 128), BF),
        pltpu.VMEM((STEPS, SLOTS, 2, D), BF),
        pltpu.VMEM((STEPS, SLOTS, 2, D), BF),
        dma((FETCHED,)),
        dma,
        dma,
        dma((len(DIRECTIONS),)),
        dma((len(DIRECTIONS),)),
        dma,
        dma,
        dma((STEPS,)),
        dma((STEPS,)),
    ]
    return pl.pallas_call(
        kernel,
        out_shape=jax.ShapeDtypeStruct((NODES, batch, D), BF),
        in_specs=[pl.BlockSpec(memory_space=pl.ANY)] * len(operands),
        out_specs=pl.BlockSpec(memory_space=pltpu.VMEM),
        scratch_shapes=scratch,
        cost_estimate=pl.CostEstimate(
            flops=4 * 10**9, bytes_accessed=15 * 10**6, transcendentals=10**6
        ),
        compiler_params=pltpu.CompilerParams(
            collective_id=0, has_side_effects=True, vmem_limit_bytes=64 * 2**20
        ),
    )(*operands)


def solution(mesh):
    nodes = P(("lat", "lon"), None)
    edges = P(("lat", "lon"))
    split = [P("lat", "lon", None, None), nodes, nodes, edges, edges, nodes, edges, edges]
    split += [P()] * (len(Given._fields) - len(split))
    return jax.shard_map(
        on_device,
        mesh=mesh,
        in_specs=tuple(split),
        out_specs=P(("lat", "lon"), None, None),
        check_vma=False,
    )
```

```python
from typing import Any, NamedTuple

import jax
import jax.numpy as jnp
from jax import lax
from jax.experimental import pallas as pl
from jax.experimental.pallas import tpu as pltpu
from jax.sharding import PartitionSpec as P

BF = jnp.bfloat16
F32 = jnp.float32
I32 = jnp.int32
MESH = pl.DeviceIdType.MESH

BATCH = 2
D = 512
HALO = 2
STEPS = 2
LATS = 8
LONS = 16
PAIRS = LATS * LONS
NODES = 32
GRID_EDGES = 128
EDGES = 256
NEAR = (1, 15, 16, 17, 31, 112, 113, 127)
EXTRA = 3
SLOTS = PAIRS + EXTRA * len(NEAR)
DIRECTIONS = tuple((a, b) for a in (0, -1, 1) for b in (0, -1, 1) if (a, b) != (0, 0))


class Given(NamedTuple):
    grid_inputs: Any
    mesh_latents: Any
    g2m_edges: Any
    g2m_sender: Any
    g2m_receiver: Any
    mesh_edges: Any
    mesh_sender: Any
    mesh_receiver: Any
    embed_w1: Any
    embed_b1: Any
    embed_w2: Any
    embed_gain: Any
    enc_edge_w1: Any
    enc_edge_b1: Any
    enc_edge_w2: Any
    enc_edge_gain: Any
    enc_node_w1: Any
    enc_node_b1: Any
    enc_node_w2: Any
    enc_node_gain: Any
    proc_edge_w1: Any
    proc_edge_b1: Any
    proc_edge_w2: Any
    proc_edge_gain: Any
    proc_node_w1: Any
    proc_node_b1: Any
    proc_node_w2: Any
    proc_node_gain: Any


class Held(NamedTuple):
    g2m_receiver: Any
    mesh_sender: Any
    mesh_receiver: Any
    mesh_latents: Any
    g2m_edges: Any
    enc_edge_w1: Any
    enc_edge_b1: Any
    embed_w1: Any
    embed_b1: Any
    embed_w2: Any
    embed_gain: Any
    enc_edge_w2: Any
    enc_edge_gain: Any
    enc_node_w1: Any
    enc_node_b1: Any
    enc_node_w2: Any
    enc_node_gain: Any
    mesh_edges: Any
    proc_edge_w1: Any
    proc_edge_b1: Any
    proc_edge_w2: Any
    proc_edge_gain: Any
    proc_node_w1: Any
    proc_node_b1: Any
    proc_node_w2: Any
    proc_node_gain: Any


FETCHED = len(Held._fields)


def mm(a, b):
    return jnp.dot(a, b, preferred_element_type=F32)


def mm_nt(a, b):
    return lax.dot_general(a, b, (((1,), (1,)), ((), ())), preferred_element_type=F32)


def iota(shape, dim):
    return lax.broadcasted_iota(I32, shape, dim)


def hot(mask):
    return jnp.where(mask, 1.0, 0.0).astype(BF)


def silu(v):
    half = 0.5 * v
    return half + half * jnp.tanh(half)


def norm(v, gain):
    centered = v - jnp.mean(v, axis=-1, keepdims=True)
    variance = jnp.mean(centered * centered, axis=-1, keepdims=True)
    return centered * lax.rsqrt(variance + 1e-05) * gain


def doubled_column(row, count):
    shape = (2 * count, count)
    spread = jnp.where(iota(shape, 1) == (iota(shape, 0) >> 1), row.astype(F32), 0.0)
    return jnp.sum(spread, axis=1, keepdims=True).astype(I32)


def doubled_row(row, count):
    shape = (count, 2 * count)
    return mm(row.astype(F32).astype(BF), hot((iota(shape, 1) >> 1) == iota(shape, 0))).astype(I32)


def kernel(*refs):
    grid_hbm, sender_hbm = refs[:2]
    hbm = refs[2 : 2 + FETCHED]
    out_ref = refs[2 + FETCHED]
    refs = refs[3 + FETCHED :]
    held = Held(*refs[:FETCHED])
    (
        cells, sender, picked, pick_all, gather_far, gather_own, gather_recv, edge_base,
        req_out, req_in, out_rows, in_rows,
        fetch_sem, cells_sem, sender_sem,
        halo_send, halo_recv, req_send, req_recv, row_send, row_recv,
    ) = refs[FETCHED:]

    lat = lax.axis_index("lat")
    lon = lax.axis_index("lon")
    lat_rows, lon_cols = grid_hbm.shape[:2]

    def place(step_lat, step_lon, sign):
        return (
            (lat + sign * step_lat + LATS) & (LATS - 1),
            (lon + sign * step_lon + LONS) & (LONS - 1),
        )

    def for_all_others(act):
        for step_lon in range(1, LONS):
            act(0, step_lon)

        def band(step_lat, carry):
            for step_lon in range(LONS):
                act(step_lat, step_lon)
            return carry

        lax.fori_loop(1, LATS, band, 0)

    barrier = pltpu.get_barrier_semaphore()
    for i in NEAR:
        pl.semaphore_signal(
            barrier, inc=1, device_id=place(i // LONS, i % LONS, 1), device_id_type=MESH
        )

    def greet(step_lat, step_lon):
        pl.semaphore_signal(
            barrier, inc=1, device_id=place(step_lat, step_lon, 1), device_id_type=MESH
        )

    for step_lat in (0, 1, LATS - 1):
        for step_lon in range(2, LONS - 1):
            greet(step_lat, step_lon)

    def greet_band(step_lat, carry):
        for step_lon in range(LONS):
            greet(step_lat, step_lon)
        return carry

    lax.fori_loop(2, LATS - 1, greet_band, 0)

    sender_copy = pltpu.make_async_copy(sender_hbm, sender, sender_sem)
    sender_copy.start()
    fetches = [
        pltpu.make_async_copy(hbm[n], held[n], fetch_sem.at[n]) for n in range(FETCHED)
    ]
    fetch = Held(*fetches)

    def ready(*copies):
        for copy in copies:
            copy.wait()

    for copy in fetches[:3]:
        copy.start()
    cells_copy = pltpu.make_async_copy(
        grid_hbm, cells.at[pl.ds(HALO, lat_rows), pl.ds(HALO, lon_cols)], cells_sem
    )
    cells_copy.start()
    for copy in fetches[3:]:
        copy.start()

    ready(fetch.g2m_receiver, fetch.mesh_sender, fetch.mesh_receiver)
    senders = held.mesh_sender[...]
    owner = senders >> 5
    row = senders & (NODES - 1)
    rel = ((((owner >> 4) - lat) & (LATS - 1)) << 4) | (((owner & 15) - lon) & (LONS - 1))
    owner2 = hot((iota((2 * PAIRS, EDGES), 0) >> 1) == rel)
    row2 = hot((iota((128, EDGES), 0) >> 1) == row)
    asked = mm_nt(owner2, row2)
    shape = (2 * PAIRS, 128)
    same = (iota(shape, 0) & 1) == (iota(shape, 1) & 1)
    asked = hot((asked > 0.5) & same & (iota(shape, 0) >= 2))
    req_out[...] = asked.reshape(PAIRS, 2, 128)
    req_in[0] = jnp.zeros((2, 128), BF)
    for t in range(STEPS):
        in_rows[t, 0] = jnp.zeros((2, D), BF)

    pl.semaphore_wait(barrier, PAIRS - 1)

    spans = {0: (0, lat_rows, HALO), -1: (0, HALO, HALO + lat_rows), 1: (lat_rows - HALO, HALO, 0)}
    spans_lon = {
        0: (0, lon_cols, HALO), -1: (0, HALO, HALO + lon_cols), 1: (lon_cols - HALO, HALO, 0)
    }
    halo = []
    for n, (a, b) in enumerate(DIRECTIONS):
        row0, rows, to_row = spans[a]
        col0, cols, to_col = spans_lon[b]
        halo.append(
            pltpu.make_async_remote_copy(
                src_ref=grid_hbm.at[pl.ds(row0, rows), pl.ds(col0, cols)],
                dst_ref=cells.at[pl.ds(to_row, rows), pl.ds(to_col, cols)],
                send_sem=halo_send.at[n],
                recv_sem=halo_recv.at[n],
                device_id=((lat + a + LATS) & (LATS - 1), (lon + b + LONS) & (LONS - 1)),
                device_id_type=MESH,
            )
        )
    groups = [
        [copy for copy, (a, _) in zip(halo, DIRECTIONS) if a == which] for which in (0, -1, 1)
    ]
    has_before = lat > 0
    has_after = lat < LATS - 1

    for copy in groups[0]:
        copy.start()

    @pl.when(has_before)
    def _():
        for copy in groups[1]:
            copy.start()

    @pl.when(has_after)
    def _():
        for copy in groups[2]:
            copy.start()

    def ask(step_lat, step_lon):
        i = step_lat * LONS + step_lon
        pltpu.make_async_remote_copy(
            src_ref=req_out.at[i], dst_ref=req_in.at[i], send_sem=req_send, recv_sem=req_recv,
            device_id=place(step_lat, step_lon, 1), device_id_type=MESH,
        ).start()

    for_all_others(ask)

    grid_receivers = held.g2m_receiver[...]
    shape = (2 * NODES, 2 * GRID_EDGES)
    total_grid = hot(
        iota(shape, 0) == 2 * doubled_row(grid_receivers, GRID_EDGES) + (iota(shape, 1) & 1)
    )
    shape = (2 * GRID_EDGES, NODES)
    gather_grid_recv = hot(iota(shape, 1) == doubled_column(grid_receivers, GRID_EDGES))

    ready(fetch.mesh_latents, fetch.g2m_edges, fetch.enc_edge_w1, fetch.enc_edge_b1)
    latents = held.mesh_latents[...]
    shape = (2 * GRID_EDGES, GRID_EDGES)
    grid_edges = mm(hot(iota(shape, 1) == (iota(shape, 0) >> 1)), held.g2m_edges[...]).astype(BF)
    mesh_recv = mm(latents, held.enc_edge_w1[2]).astype(BF)
    grid_base = (
        mm(grid_edges, held.enc_edge_w1[0])
        + mm(gather_grid_recv, mesh_recv)
        + held.enc_edge_b1[...]
    )
    shape = (2 * NODES, NODES)
    state = mm(hot(iota(shape, 1) == (iota(shape, 0) >> 1)), latents).astype(BF)

    sender_copy.wait()
    cells_copy.wait()
    for copy in groups[0]:
        copy.wait_recv()

    @pl.when(has_after)
    def _():
        for copy in groups[1]:
            copy.wait_recv()

    @pl.when(has_before)
    def _():
        for copy in groups[2]:
            copy.wait_recv()

    width = lon_cols * LONS

    def pick(k, carry):
        cell = sender[k]
        cell_row = (cell // width) - lat * lat_rows + HALO
        cell_col = ((cell & (width - 1)) - lon * lon_cols + HALO + width) & (width - 1)
        cell_row = jnp.clip(cell_row, 0, cells.shape[0] - 1)
        cell_col = jnp.clip(cell_col, 0, cells.shape[1] - 1)
        picked[k] = cells[cell_row, cell_col]
        return carry

    lax.fori_loop(0, GRID_EDGES, pick, 0, unroll=8)

    ready(fetch.embed_w1, fetch.embed_b1, fetch.embed_w2, fetch.embed_gain)
    inputs = picked[...].reshape(2 * GRID_EDGES, picked.shape[2])
    hidden = silu(mm(inputs, held.embed_w1[...]) + held.embed_b1[...]).astype(BF)
    latent = norm(mm(hidden, held.embed_w2[...]), held.embed_gain[...]).astype(BF)
    preact = mm(latent, held.enc_edge_w1[1]) + grid_base
    hidden = silu(preact).astype(BF)
    pltpu.make_async_copy(
        req_in.at[pl.ds(1, PAIRS - 1)], req_in.at[pl.ds(1, PAIRS - 1)], req_recv
    ).wait()
    wanted = req_in[...].reshape(2 * PAIRS, 128)[:, : 2 * NODES]
    shape = (2 * NODES, 2 * NODES)
    before = hot(
        (iota(shape, 0) < iota(shape, 1)) & ((iota(shape, 0) & 1) == (iota(shape, 1) & 1))
    )
    place_of = mm(wanted, before).astype(BF)
    first = jnp.where(place_of.astype(F32) < 0.5, wanted.astype(F32), 0.0).astype(BF)
    shape = (2 * EXTRA * len(NEAR), 2 * PAIRS)
    line = iota(shape, 0)
    which = jnp.zeros_like(line)
    target = jnp.full_like(line, NEAR[0])
    for n in range(1, len(NEAR)):
        later = line >= 2 * EXTRA * n
        which = jnp.where(later, n, which)
        target = jnp.where(later, NEAR[n], target)
    choose = hot(iota(shape, 1) == 2 * target + (line & 1))
    kth = ((line >> 1) - EXTRA * which + 1).astype(F32)[:, : 2 * NODES]
    more = jnp.where(mm(choose, place_of) == kth, mm(choose, wanted), 0.0).astype(BF)
    pick_all[: 2 * PAIRS] = first
    pick_all[2 * PAIRS :] = more

    ready(fetch.enc_edge_w2, fetch.enc_edge_gain)
    update = norm(mm(hidden, held.enc_edge_w2[...]), held.enc_edge_gain[...])
    new_edges = (grid_edges.astype(F32) + update).astype(BF)
    summed = mm(total_grid, new_edges).astype(BF)
    ready(fetch.enc_node_w1, fetch.enc_node_b1, fetch.enc_node_w2, fetch.enc_node_gain)
    preact = (
        mm(state, held.enc_node_w1[0])
        + mm(summed, held.enc_node_w1[1])
        + held.enc_node_b1[...]
    )
    hidden = silu(preact).astype(BF)
    update = norm(mm(hidden, held.enc_node_w2[...]), held.enc_node_gain[...])
    state = (state.astype(F32) + update).astype(BF)

    ready(fetch.proc_edge_w1, fetch.proc_edge_b1, fetch.proc_edge_w2, fetch.proc_edge_gain)
    ready(fetch.proc_node_w1, fetch.proc_node_b1, fetch.proc_node_w2, fetch.proc_node_gain)
    for t in range(STEPS):
        outgoing = mm(state, held.proc_edge_w1[t, 1]).astype(BF)
        out_rows[t] = mm(pick_all[...], outgoing).astype(BF).reshape(SLOTS, 2, D)

        def give(step_lat, step_lon, t=t):
            i = step_lat * LONS + step_lon
            pltpu.make_async_remote_copy(
                src_ref=out_rows.at[t, i], dst_ref=in_rows.at[t, i],
                send_sem=row_send.at[t], recv_sem=row_recv.at[t],
                device_id=place(step_lat, step_lon, -1), device_id_type=MESH,
            ).start()

        for_all_others(give)
        for n, i in enumerate(NEAR):
            span = pl.ds(PAIRS + EXTRA * n, EXTRA)
            pltpu.make_async_remote_copy(
                src_ref=out_rows.at[t, span], dst_ref=in_rows.at[t, span],
                send_sem=row_send.at[t], recv_sem=row_recv.at[t],
                device_id=place(i // LONS, i % LONS, -1), device_id_type=MESH,
            ).start()

        if t == 0:
            owner1 = hot(iota((PAIRS, EDGES), 0) == rel)
            row1 = iota((NODES, EDGES), 0) == row
            needed = hot(mm_nt(hot(row1), owner1) > 0.5)
            below = hot(iota((NODES, NODES), 1) < iota((NODES, NODES), 0))
            order = mm(below, needed).astype(BF)
            rank = jnp.sum(jnp.where(row1, mm(order, owner1), 0.0), axis=0, keepdims=True).astype(I32)
            near = jnp.zeros_like(rel)
            for n, i in enumerate(NEAR):
                near = jnp.where(rel == i, n, near)
            slot = jnp.where(rank == 0, rel, PAIRS + EXTRA * near + rank - 1)
            slot = jnp.where(rel == 0, SLOTS + row, slot)
            slot_column = doubled_column(slot, EDGES)
            shape = (2 * EDGES, 2 * (SLOTS + NODES))
            gather = hot(iota(shape, 1) == 2 * slot_column + (iota(shape, 0) & 1))
            gather_far[...] = gather[:, : 2 * SLOTS]
            gather_own[...] = gather[:, 2 * SLOTS :]
            receivers = held.mesh_receiver[...]
            shape = (2 * EDGES, 2 * NODES)
            gather_recv[...] = hot(
                iota(shape, 1) == 2 * doubled_column(receivers, EDGES) + (iota(shape, 0) & 1)
            )
            shape = (2 * NODES, 2 * EDGES)
            total_mesh = hot(iota(shape, 0) == 2 * doubled_row(receivers, EDGES) + (iota(shape, 1) & 1))

            ready(fetch.mesh_edges)
            shape = (2 * EDGES, EDGES)
            edge_state = mm(
                hot(iota(shape, 1) == (iota(shape, 0) >> 1)), held.mesh_edges[...]
            ).astype(BF)

        incoming = mm(state, held.proc_edge_w1[t, 2]).astype(BF)
        edge_base[...] = (
            mm(edge_state, held.proc_edge_w1[t, 0])
            + mm(gather_recv[...], incoming)
            + mm(gather_own[...], outgoing)
            + held.proc_edge_b1[t : t + 1]
        )
        node_base = mm(state, held.proc_node_w1[t, 0]) + held.proc_node_b1[t : t + 1]

        arrived = in_rows.at[t, pl.ds(1, SLOTS - 1)]
        pltpu.make_async_copy(arrived, arrived, row_recv.at[t]).wait()
        table = in_rows[t].reshape(2 * SLOTS, D)
        hidden = silu(edge_base[...] + mm(gather_far[...], table)).astype(BF)
        update = norm(mm(hidden, held.proc_edge_w2[t]), held.proc_edge_gain[t : t + 1])
        edge_state = (edge_state.astype(F32) + update).astype(BF)
        summed = mm(total_mesh, edge_state).astype(BF)
        hidden = silu(node_base + mm(summed, held.proc_node_w1[t, 1])).astype(BF)
        update = norm(mm(hidden, held.proc_node_w2[t]), held.proc_node_gain[t : t + 1])
        state = (state.astype(F32) + update).astype(BF)

    out_ref[...] = state

    for copy in groups[0]:
        copy.wait_send()

    @pl.when(has_before)
    def _():
        for copy in groups[1]:
            copy.wait_send()

    @pl.when(has_after)
    def _():
        for copy in groups[2]:
            copy.wait_send()

    asked_all = req_out.at[pl.ds(1, PAIRS - 1)]
    pltpu.make_async_copy(asked_all, asked_all, req_send).wait()
    for t in range(STEPS):
        sent = out_rows.at[t, pl.ds(1, SLOTS - 1)]
        pltpu.make_async_copy(sent, sent, row_send.at[t]).wait()


def on_device(*args):
    given = Given(*args)
    lat_rows, lon_cols, batch, width = given.grid_inputs.shape

    def flat(row):
        return row.reshape(1, row.shape[0])

    wanted = Held(
        flat(given.g2m_receiver),
        flat(given.mesh_sender),
        flat(given.mesh_receiver),
        given.mesh_latents,
        given.g2m_edges,
        given.enc_edge_w1,
        flat(given.enc_edge_b1),
        given.embed_w1,
        flat(given.embed_b1),
        given.embed_w2,
        flat(given.embed_gain),
        given.enc_edge_w2,
        flat(given.enc_edge_gain),
        given.enc_node_w1,
        flat(given.enc_node_b1),
        given.enc_node_w2,
        flat(given.enc_node_gain),
        given.mesh_edges,
        given.proc_edge_w1,
        given.proc_edge_b1,
        given.proc_edge_w2,
        given.proc_edge_gain,
        given.proc_node_w1,
        given.proc_node_b1,
        given.proc_node_w2,
        given.proc_node_gain,
    )
    operands = [given.grid_inputs, given.g2m_sender, *wanted]
    dma = pltpu.SemaphoreType.DMA
    scratch = [pltpu.VMEM(part.shape, part.dtype) for part in wanted]
    scratch += [
        pltpu.VMEM((lat_rows + 2 * HALO, lon_cols + 2 * HALO, batch, width), BF),
        pltpu.SMEM((GRID_EDGES,), I32),
        pltpu.VMEM((GRID_EDGES, batch, width), BF),
        pltpu.VMEM((2 * SLOTS, 2 * NODES), BF),
        pltpu.VMEM((2 * EDGES, 2 * SLOTS), BF),
        pltpu.VMEM((2 * EDGES, 2 * NODES), BF),
        pltpu.VMEM((2 * EDGES, 2 * NODES), BF),
        pltpu.VMEM((2 * EDGES, D), F32),
        pltpu.VMEM((PAIRS, 2, 128), BF),
        pltpu.VMEM((PAIRS, 2, 128), BF),
        pltpu.VMEM((STEPS, SLOTS, 2, D), BF),
        pltpu.VMEM((STEPS, SLOTS, 2, D), BF),
        dma((FETCHED,)),
        dma,
        dma,
        dma((len(DIRECTIONS),)),
        dma((len(DIRECTIONS),)),
        dma,
        dma,
        dma((STEPS,)),
        dma((STEPS,)),
    ]
    return pl.pallas_call(
        kernel,
        out_shape=jax.ShapeDtypeStruct((NODES * batch, D), BF),
        in_specs=[pl.BlockSpec(memory_space=pl.ANY)] * len(operands),
        out_specs=pl.BlockSpec(memory_space=pltpu.VMEM),
        scratch_shapes=scratch,
        cost_estimate=pl.CostEstimate(
            flops=4 * 10**9, bytes_accessed=15 * 10**6, transcendentals=10**6
        ),
        compiler_params=pltpu.CompilerParams(
            collective_id=0, has_side_effects=True, vmem_limit_bytes=64 * 2**20
        ),
    )(*operands).reshape(NODES, batch, D)


def solution(mesh):
    nodes = P(("lat", "lon"), None)
    edges = P(("lat", "lon"))
    split = [P("lat", "lon", None, None), nodes, nodes, edges, edges, nodes, edges, edges]
    split += [P()] * (len(Given._fields) - len(split))
    return jax.shard_map(
        on_device,
        mesh=mesh,
        in_specs=tuple(split),
        out_specs=P(("lat", "lon"), None, None),
        check_vma=False,
    )
```

```python
from typing import Any, NamedTuple

import jax
import jax.numpy as jnp
from jax import lax
from jax.experimental import pallas as pl
from jax.experimental.pallas import tpu as pltpu
from jax.sharding import PartitionSpec as P

BF = jnp.bfloat16
F32 = jnp.float32
I32 = jnp.int32
MESH = pl.DeviceIdType.MESH

BATCH = 2
D = 512
HALO = 2
STEPS = 2
LATS = 8
LONS = 16
CORES = 2
XS = LATS // CORES
CHIPS = XS * LONS
NODES = 32
CHIP_NODES = CORES * NODES
GRID_EDGES = 128
EDGES = 256
PLAIN = 2 * CHIPS
NEAR = (1, 15, 16, 17, 31, 48, 49, 63)
EXTRA = (6, 6, 3, 3, 3, 3, 3, 3)
START = (0, 6, 12, 15, 18, 21, 24, 27)
SLOTS = PLAIN + sum(EXTRA)
DIRECTIONS = tuple((a, b) for a in (0, -1, 1) for b in (0, -1, 1) if (a, b) != (0, 0))


class Given(NamedTuple):
    grid_inputs: Any
    mesh_latents: Any
    g2m_edges: Any
    g2m_sender: Any
    g2m_receiver: Any
    mesh_edges: Any
    mesh_sender: Any
    mesh_receiver: Any
    embed_w1: Any
    embed_b1: Any
    embed_w2: Any
    embed_gain: Any
    enc_edge_w1: Any
    enc_edge_b1: Any
    enc_edge_w2: Any
    enc_edge_gain: Any
    enc_node_w1: Any
    enc_node_b1: Any
    enc_node_w2: Any
    enc_node_gain: Any
    proc_edge_w1: Any
    proc_edge_b1: Any
    proc_edge_w2: Any
    proc_edge_gain: Any
    proc_node_w1: Any
    proc_node_b1: Any
    proc_node_w2: Any
    proc_node_gain: Any


class Held(NamedTuple):
    g2m_receiver: Any
    mesh_sender: Any
    mesh_receiver: Any
    mesh_latents: Any
    g2m_edges: Any
    enc_edge_w1: Any
    enc_edge_b1: Any
    embed_w1: Any
    embed_b1: Any
    embed_w2: Any
    embed_gain: Any
    enc_edge_w2: Any
    enc_edge_gain: Any
    enc_node_w1: Any
    enc_node_b1: Any
    enc_node_w2: Any
    enc_node_gain: Any
    mesh_edges: Any
    proc_edge_w1: Any
    proc_edge_b1: Any
    proc_edge_w2: Any
    proc_edge_gain: Any
    proc_node_w1: Any
    proc_node_b1: Any
    proc_node_w2: Any
    proc_node_gain: Any


FETCHED = len(Held._fields)


def mm(a, b):
    return jnp.dot(a, b, preferred_element_type=F32)


def mm_nt(a, b):
    return lax.dot_general(a, b, (((1,), (1,)), ((), ())), preferred_element_type=F32)


def iota(shape, dim):
    return lax.broadcasted_iota(I32, shape, dim)


def hot(mask):
    return jnp.where(mask, 1.0, 0.0).astype(BF)


def silu(v):
    half = 0.5 * v
    return half + half * jnp.tanh(half)


def norm(v, gain):
    centered = v - jnp.mean(v, axis=-1, keepdims=True)
    variance = jnp.mean(centered * centered, axis=-1, keepdims=True)
    return centered * lax.rsqrt(variance + 1e-05) * gain


def doubled_column(row, count):
    shape = (2 * count, count)
    spread = jnp.where(iota(shape, 1) == (iota(shape, 0) >> 1), row.astype(F32), 0.0)
    return jnp.sum(spread, axis=1, keepdims=True).astype(I32)


def doubled_row(row, count):
    shape = (count, 2 * count)
    return mm(row.astype(F32).astype(BF), hot((iota(shape, 1) >> 1) == iota(shape, 0))).astype(I32)


def kernel(*refs):
    grid_hbm, sender_hbm = refs[:2]
    hbm = refs[2 : 2 + FETCHED]
    out_ref = refs[2 + FETCHED]
    refs = refs[3 + FETCHED :]
    held = Held(*refs[:FETCHED])
    (
        cells, sender, picked, pick_all, gather_far, gather_own, gather_recv, edge_base,
        req_out, req_in, chip_rows, out_rows, in_rows,
        fetch_sem, cells_sem, sender_sem,
        halo_send, halo_recv, req_send, req_recv, share_send, share_recv,
        row_send, row_recv,
    ) = refs[FETCHED:]

    lat = lax.axis_index("lat")
    lon = lax.axis_index("lon")
    lat_rows, lon_cols = grid_hbm.shape[:2]

    core = lat & 1
    beside = lat ^ 1

    def place(step_x, step_lon, sign):
        return (
            (lat + sign * CORES * step_x + LATS) & (LATS - 1),
            (lon + sign * step_lon + LONS) & (LONS - 1),
        )

    def for_all_chips(act):
        for step_lon in range(1, LONS):
            act(0, step_lon)

        def band(step_x, carry):
            for step_lon in range(LONS):
                act(step_x, step_lon)
            return carry

        lax.fori_loop(1, XS, band, 0)

    barrier = pltpu.get_barrier_semaphore()
    others = [(a, b) for a in (-1, 1) for b in (0, -1, 1)]
    for a, b in others:
        pl.semaphore_signal(
            barrier, inc=1, device_id_type=MESH,
            device_id=((lat + a + LATS) & (LATS - 1), (lon + b + LONS) & (LONS - 1)),
        )

    def greet(step_x, step_lon):
        pl.semaphore_signal(
            barrier, inc=1, device_id=place(step_x, step_lon, 1), device_id_type=MESH
        )

    for_all_chips(greet)

    sender_copy = pltpu.make_async_copy(sender_hbm, sender, sender_sem)
    sender_copy.start()
    fetches = [
        pltpu.make_async_copy(hbm[n], held[n], fetch_sem.at[n]) for n in range(FETCHED)
    ]
    fetch = Held(*fetches)

    def ready(*copies):
        for copy in copies:
            copy.wait()

    for copy in fetches[:3]:
        copy.start()
    ready(fetch.g2m_receiver, fetch.mesh_sender, fetch.mesh_receiver)
    senders = held.mesh_sender[...]
    owner = senders >> 5
    step_x = ((owner >> 5) - (lat >> 1)) & (XS - 1)
    rel = (step_x << 4) | (((owner & 15) - lon) & (LONS - 1))
    row = (((owner >> 4) & 1) << 5) | (senders & (NODES - 1))
    shape = (2 * CHIPS, EDGES)
    chip2 = hot((iota(shape, 0) >> 1) == rel)
    row2 = hot((iota(shape, 0) >> 1) == row)
    shape = (2 * CHIPS, 2 * CHIP_NODES)
    same = (iota(shape, 0) & 1) == (iota(shape, 1) & 1)
    asked = hot((mm_nt(chip2, row2) > 0.5) & same & (iota(shape, 0) >= 2))
    req_out[...] = asked.reshape(CHIPS, 2, 2 * CHIP_NODES)
    req_in[0] = jnp.zeros((2, 2 * CHIP_NODES), BF)
    for t in range(STEPS):
        in_rows[t, 0] = jnp.zeros((2, D), BF)
        in_rows[t, 1] = jnp.zeros((2, D), BF)

    pl.semaphore_wait(barrier, CHIPS - 1 + len(others))

    spans = {0: (0, lat_rows, HALO), -1: (0, HALO, HALO + lat_rows), 1: (lat_rows - HALO, HALO, 0)}
    spans_lon = {
        0: (0, lon_cols, HALO), -1: (0, HALO, HALO + lon_cols), 1: (lon_cols - HALO, HALO, 0)
    }
    halo = []
    for n, (a, b) in enumerate(DIRECTIONS):
        row0, rows, to_row = spans[a]
        col0, cols, to_col = spans_lon[b]
        halo.append(
            pltpu.make_async_remote_copy(
                src_ref=grid_hbm.at[pl.ds(row0, rows), pl.ds(col0, cols)],
                dst_ref=cells.at[pl.ds(to_row, rows), pl.ds(to_col, cols)],
                send_sem=halo_send.at[n],
                recv_sem=halo_recv.at[n],
                device_id=((lat + a + LATS) & (LATS - 1), (lon + b + LONS) & (LONS - 1)),
                device_id_type=MESH,
            )
        )
    groups = [
        [copy for copy, (a, _) in zip(halo, DIRECTIONS) if a == which] for which in (0, -1, 1)
    ]
    has_before = lat > 0
    has_after = lat < LATS - 1

    for copy in groups[0]:
        copy.start()

    @pl.when(has_before)
    def _():
        for copy in groups[1]:
            copy.start()

    @pl.when(has_after)
    def _():
        for copy in groups[2]:
            copy.start()

    cells_copy = pltpu.make_async_copy(
        grid_hbm, cells.at[pl.ds(HALO, lat_rows), pl.ds(HALO, lon_cols)], cells_sem
    )
    cells_copy.start()
    for copy in fetches[3:]:
        copy.start()

    def ask(step_x, step_lon):
        i = step_x * LONS + step_lon
        pltpu.make_async_remote_copy(
            src_ref=req_out.at[i], dst_ref=req_in.at[i], send_sem=req_send, recv_sem=req_recv,
            device_id=place(step_x, step_lon, 1), device_id_type=MESH,
        ).start()

    for_all_chips(ask)

    grid_receivers = held.g2m_receiver[...]
    shape = (2 * NODES, 2 * GRID_EDGES)
    total_grid = hot(
        iota(shape, 0) == 2 * doubled_row(grid_receivers, GRID_EDGES) + (iota(shape, 1) & 1)
    )
    shape = (2 * GRID_EDGES, NODES)
    gather_grid_recv = hot(iota(shape, 1) == doubled_column(grid_receivers, GRID_EDGES))

    ready(fetch.mesh_latents, fetch.g2m_edges, fetch.enc_edge_w1, fetch.enc_edge_b1)
    latents = held.mesh_latents[...]
    shape = (2 * GRID_EDGES, GRID_EDGES)
    grid_edges = mm(hot(iota(shape, 1) == (iota(shape, 0) >> 1)), held.g2m_edges[...]).astype(BF)
    mesh_recv = mm(latents, held.enc_edge_w1[2]).astype(BF)
    grid_base = (
        mm(grid_edges, held.enc_edge_w1[0])
        + mm(gather_grid_recv, mesh_recv)
        + held.enc_edge_b1[...]
    )
    shape = (2 * NODES, NODES)
    state = mm(hot(iota(shape, 1) == (iota(shape, 0) >> 1)), latents).astype(BF)

    sender_copy.wait()
    cells_copy.wait()
    for copy in groups[0]:
        copy.wait_recv()

    @pl.when(has_after)
    def _():
        for copy in groups[1]:
            copy.wait_recv()

    @pl.when(has_before)
    def _():
        for copy in groups[2]:
            copy.wait_recv()

    width = lon_cols * LONS

    def pick(k, carry):
        cell = sender[k]
        cell_row = (cell // width) - lat * lat_rows + HALO
        cell_col = ((cell & (width - 1)) - lon * lon_cols + HALO + width) & (width - 1)
        cell_row = jnp.clip(cell_row, 0, cells.shape[0] - 1)
        cell_col = jnp.clip(cell_col, 0, cells.shape[1] - 1)
        picked[k] = cells[cell_row, cell_col]
        return carry

    lax.fori_loop(0, GRID_EDGES, pick, 0, unroll=8)

    ready(fetch.embed_w1, fetch.embed_b1, fetch.embed_w2, fetch.embed_gain)
    inputs = picked[...].reshape(2 * GRID_EDGES, picked.shape[2])
    hidden = silu(mm(inputs, held.embed_w1[...]) + held.embed_b1[...]).astype(BF)
    latent = norm(mm(hidden, held.embed_w2[...]), held.embed_gain[...]).astype(BF)
    preact = mm(latent, held.enc_edge_w1[1]) + grid_base
    hidden = silu(preact).astype(BF)
    asked_all = req_in.at[pl.ds(1, CHIPS - 1)]
    pltpu.make_async_copy(asked_all, asked_all, req_recv).wait()
    wanted = req_in[...].reshape(2 * CHIPS, 2 * CHIP_NODES)
    shape = (2 * CHIP_NODES, 2 * CHIP_NODES)
    before = hot(
        (iota(shape, 0) < iota(shape, 1)) & ((iota(shape, 0) & 1) == (iota(shape, 1) & 1))
    )
    place_of = mm(wanted, before).astype(BF)
    shape = (2 * SLOTS, 2 * CHIPS)
    line = iota(shape, 0)
    number = line >> 1
    chip = number >> 1
    kth = number & 1
    for i, start in zip(NEAR, START):
        later = number >= PLAIN + start
        chip = jnp.where(later, i, chip)
        kth = jnp.where(later, number - (PLAIN + start - 2), kth)
    choose = hot(iota(shape, 1) == 2 * chip + (line & 1))
    kth = kth.astype(F32)
    pick_all[...] = jnp.where(mm(choose, place_of) == kth, mm(choose, wanted), 0.0).astype(BF)

    ready(fetch.enc_edge_w2, fetch.enc_edge_gain)
    update = norm(mm(hidden, held.enc_edge_w2[...]), held.enc_edge_gain[...])
    new_edges = (grid_edges.astype(F32) + update).astype(BF)
    summed = mm(total_grid, new_edges).astype(BF)
    ready(fetch.enc_node_w1, fetch.enc_node_b1, fetch.enc_node_w2, fetch.enc_node_gain)
    preact = (
        mm(state, held.enc_node_w1[0])
        + mm(summed, held.enc_node_w1[1])
        + held.enc_node_b1[...]
    )
    hidden = silu(preact).astype(BF)
    update = norm(mm(hidden, held.enc_node_w2[...]), held.enc_node_gain[...])
    state = (state.astype(F32) + update).astype(BF)

    ready(fetch.proc_edge_w1, fetch.proc_edge_b1, fetch.proc_edge_w2, fetch.proc_edge_gain)
    ready(fetch.proc_node_w1, fetch.proc_node_b1, fetch.proc_node_w2, fetch.proc_node_gain)
    for t in range(STEPS):
        chip_rows[t, core] = mm(state, held.proc_edge_w1[t, 1]).astype(BF)
        share = pltpu.make_async_remote_copy(
            src_ref=chip_rows.at[t, core], dst_ref=chip_rows.at[t, core],
            send_sem=share_send.at[t], recv_sem=share_recv.at[t],
            device_id=(beside, lon), device_id_type=MESH,
        )
        share.start()
        incoming = mm(state, held.proc_edge_w1[t, 2]).astype(BF)
        node_base = mm(state, held.proc_node_w1[t, 0]) + held.proc_node_b1[t : t + 1]
        share.wait()
        outgoing = chip_rows[t].reshape(2 * CHIP_NODES, D)
        out_rows[t] = mm(pick_all[...], outgoing).astype(BF).reshape(SLOTS, 2, D)

        for n, i in enumerate(NEAR):
            span = pl.ds(PLAIN + START[n], EXTRA[n])
            pltpu.make_async_remote_copy(
                src_ref=out_rows.at[t, span], dst_ref=in_rows.at[t, span],
                send_sem=row_send.at[t], recv_sem=row_recv.at[t],
                device_id=place(i // LONS, i % LONS, -1), device_id_type=MESH,
            ).start()

        def give(step_x, step_lon, t=t):
            span = pl.ds(2 * (step_x * LONS + step_lon), 2)
            pltpu.make_async_remote_copy(
                src_ref=out_rows.at[t, span], dst_ref=in_rows.at[t, span],
                send_sem=row_send.at[t], recv_sem=row_recv.at[t],
                device_id=place(step_x, step_lon, -1), device_id_type=MESH,
            ).start()

        for_all_chips(give)

        if t == 0:
            chip1 = hot(iota((CHIPS, EDGES), 0) == rel)
            row1 = iota((CHIP_NODES, EDGES), 0) == row
            needed = hot(mm_nt(hot(row1), chip1) > 0.5)
            shape = (CHIP_NODES, CHIP_NODES)
            order = mm(hot(iota(shape, 1) < iota(shape, 0)), needed).astype(BF)
            rank = jnp.where(row1, mm(order, chip1), 0.0)
            rank = jnp.sum(rank, axis=0, keepdims=True).astype(I32)
            extra = jnp.zeros_like(rel)
            for i, start in zip(NEAR, START):
                extra = jnp.where(rel == i, start, extra)
            slot = jnp.where(rank < 2, 2 * rel + rank, PLAIN + extra + rank - 2)
            slot = jnp.where(rel == 0, SLOTS + row, slot)
            slot_column = doubled_column(slot, EDGES)
            shape = (2 * EDGES, 2 * (SLOTS + CHIP_NODES))
            gather = hot(iota(shape, 1) == 2 * slot_column + (iota(shape, 0) & 1))
            gather_far[...] = gather[:, : 2 * SLOTS]
            gather_own[...] = gather[:, 2 * SLOTS :]
            receivers = held.mesh_receiver[...]
            shape = (2 * EDGES, 2 * NODES)
            gather_recv[...] = hot(
                iota(shape, 1) == 2 * doubled_column(receivers, EDGES) + (iota(shape, 0) & 1)
            )
            shape = (2 * NODES, 2 * EDGES)
            total_mesh = hot(iota(shape, 0) == 2 * doubled_row(receivers, EDGES) + (iota(shape, 1) & 1))

            ready(fetch.mesh_edges)
            shape = (2 * EDGES, EDGES)
            edge_state = mm(
                hot(iota(shape, 1) == (iota(shape, 0) >> 1)), held.mesh_edges[...]
            ).astype(BF)

        edge_base[...] = (
            mm(edge_state, held.proc_edge_w1[t, 0])
            + mm(gather_recv[...], incoming)
            + mm(gather_own[...], outgoing)
            + held.proc_edge_b1[t : t + 1]
        )
        arrived = in_rows.at[t, pl.ds(2, SLOTS - 2)]
        pltpu.make_async_copy(arrived, arrived, row_recv.at[t]).wait()
        table = in_rows[t].reshape(2 * SLOTS, D)
        hidden = silu(edge_base[...] + mm(gather_far[...], table)).astype(BF)
        update = norm(mm(hidden, held.proc_edge_w2[t]), held.proc_edge_gain[t : t + 1])
        edge_state = (edge_state.astype(F32) + update).astype(BF)
        summed = mm(total_mesh, edge_state).astype(BF)
        hidden = silu(node_base + mm(summed, held.proc_node_w1[t, 1])).astype(BF)
        update = norm(mm(hidden, held.proc_node_w2[t]), held.proc_node_gain[t : t + 1])
        state = (state.astype(F32) + update).astype(BF)

    out_ref[...] = state

    for copy in groups[0]:
        copy.wait_send()

    @pl.when(has_before)
    def _():
        for copy in groups[1]:
            copy.wait_send()

    @pl.when(has_after)
    def _():
        for copy in groups[2]:
            copy.wait_send()

    asked_all = req_out.at[pl.ds(1, CHIPS - 1)]
    pltpu.make_async_copy(asked_all, asked_all, req_send).wait()
    for t in range(STEPS):
        sent = out_rows.at[t, pl.ds(2, SLOTS - 2)]
        pltpu.make_async_copy(sent, sent, row_send.at[t]).wait()


def on_device(*args):
    given = Given(*args)
    lat_rows, lon_cols, batch, width = given.grid_inputs.shape

    def flat(row):
        return row.reshape(1, row.shape[0])

    wanted = Held(
        flat(given.g2m_receiver),
        flat(given.mesh_sender),
        flat(given.mesh_receiver),
        given.mesh_latents,
        given.g2m_edges,
        given.enc_edge_w1,
        flat(given.enc_edge_b1),
        given.embed_w1,
        flat(given.embed_b1),
        given.embed_w2,
        flat(given.embed_gain),
        given.enc_edge_w2,
        flat(given.enc_edge_gain),
        given.enc_node_w1,
        flat(given.enc_node_b1),
        given.enc_node_w2,
        flat(given.enc_node_gain),
        given.mesh_edges,
        given.proc_edge_w1,
        given.proc_edge_b1,
        given.proc_edge_w2,
        given.proc_edge_gain,
        given.proc_node_w1,
        given.proc_node_b1,
        given.proc_node_w2,
        given.proc_node_gain,
    )
    operands = [given.grid_inputs, given.g2m_sender, *wanted]
    dma = pltpu.SemaphoreType.DMA
    scratch = [pltpu.VMEM(part.shape, part.dtype) for part in wanted]
    scratch += [
        pltpu.VMEM((lat_rows + 2 * HALO, lon_cols + 2 * HALO, batch, width), BF),
        pltpu.SMEM((GRID_EDGES,), I32),
        pltpu.VMEM((GRID_EDGES, batch, width), BF),
        pltpu.VMEM((2 * SLOTS, 2 * CHIP_NODES), BF),
        pltpu.VMEM((2 * EDGES, 2 * SLOTS), BF),
        pltpu.VMEM((2 * EDGES, 2 * CHIP_NODES), BF),
        pltpu.VMEM((2 * EDGES, 2 * NODES), BF),
        pltpu.VMEM((2 * EDGES, D), F32),
        pltpu.VMEM((CHIPS, 2, 2 * CHIP_NODES), BF),
        pltpu.VMEM((CHIPS, 2, 2 * CHIP_NODES), BF),
        pltpu.VMEM((STEPS, CORES, 2 * NODES, D), BF),
        pltpu.VMEM((STEPS, SLOTS, 2, D), BF),
        pltpu.VMEM((STEPS, SLOTS, 2, D), BF),
        dma((FETCHED,)),
        dma,
        dma,
        dma((len(DIRECTIONS),)),
        dma((len(DIRECTIONS),)),
        dma,
        dma,
        dma((STEPS,)),
        dma((STEPS,)),
        dma((STEPS,)),
        dma((STEPS,)),
    ]
    return pl.pallas_call(
        kernel,
        out_shape=jax.ShapeDtypeStruct((NODES * batch, D), BF),
        in_specs=[pl.BlockSpec(memory_space=pl.ANY)] * len(operands),
        out_specs=pl.BlockSpec(memory_space=pltpu.VMEM),
        scratch_shapes=scratch,
        cost_estimate=pl.CostEstimate(
            flops=4 * 10**9, bytes_accessed=15 * 10**6, transcendentals=10**6
        ),
        compiler_params=pltpu.CompilerParams(
            collective_id=0, has_side_effects=True, vmem_limit_bytes=64 * 2**20
        ),
    )(*operands).reshape(NODES, batch, D)


def solution(mesh):
    nodes = P(("lat", "lon"), None)
    edges = P(("lat", "lon"))
    split = [P("lat", "lon", None, None), nodes, nodes, edges, edges, nodes, edges, edges]
    split += [P()] * (len(Given._fields) - len(split))
    return jax.shard_map(
        on_device,
        mesh=mesh,
        in_specs=tuple(split),
        out_specs=P(("lat", "lon"), None, None),
        check_vma=False,
    )
```

```python
from typing import Any, NamedTuple

import jax
import jax.numpy as jnp
from jax import lax
from jax.experimental import pallas as pl
from jax.experimental.pallas import tpu as pltpu
from jax.sharding import PartitionSpec as P

BF = jnp.bfloat16
F32 = jnp.float32
I32 = jnp.int32
MESH = pl.DeviceIdType.MESH

BATCH = 2
D = 512
HALO = 2
STEPS = 2
CHUNK = 64
LATS = 8
LONS = 16
PAIRS = LATS * LONS
NODES = 32
GRID_EDGES = 128
EDGES = 256
NEAR = (1, 15, 16, 17, 31, 112, 113, 127)
EXTRA = 3
SLOTS = PAIRS + EXTRA * len(NEAR)
DIRECTIONS = tuple((a, b) for a in (0, -1, 1) for b in (0, -1, 1) if (a, b) != (0, 0))


class Given(NamedTuple):
    grid_inputs: Any
    mesh_latents: Any
    g2m_edges: Any
    g2m_sender: Any
    g2m_receiver: Any
    mesh_edges: Any
    mesh_sender: Any
    mesh_receiver: Any
    embed_w1: Any
    embed_b1: Any
    embed_w2: Any
    embed_gain: Any
    enc_edge_w1: Any
    enc_edge_b1: Any
    enc_edge_w2: Any
    enc_edge_gain: Any
    enc_node_w1: Any
    enc_node_b1: Any
    enc_node_w2: Any
    enc_node_gain: Any
    proc_edge_w1: Any
    proc_edge_b1: Any
    proc_edge_w2: Any
    proc_edge_gain: Any
    proc_node_w1: Any
    proc_node_b1: Any
    proc_node_w2: Any
    proc_node_gain: Any


class Held(NamedTuple):
    g2m_receiver: Any
    mesh_sender: Any
    mesh_receiver: Any
    mesh_latents: Any
    g2m_edges: Any
    enc_edge_w1: Any
    enc_edge_b1: Any
    embed_w1: Any
    embed_b1: Any
    embed_w2: Any
    embed_gain: Any
    enc_edge_w2: Any
    enc_edge_gain: Any
    enc_node_w1: Any
    enc_node_b1: Any
    enc_node_w2: Any
    enc_node_gain: Any
    mesh_edges: Any
    proc_edge_w1: Any
    proc_edge_b1: Any
    proc_edge_w2: Any
    proc_edge_gain: Any
    proc_node_w1: Any
    proc_node_b1: Any
    proc_node_w2: Any
    proc_node_gain: Any


FETCHED = len(Held._fields)


def mm(a, b):
    return jnp.dot(a, b, preferred_element_type=F32)


def mm_nt(a, b):
    return lax.dot_general(a, b, (((1,), (1,)), ((), ())), preferred_element_type=F32)


def iota(shape, dim):
    return lax.broadcasted_iota(I32, shape, dim)


def hot(mask):
    return jnp.where(mask, 1.0, 0.0).astype(BF)


def silu(v):
    half = 0.5 * v
    return half + half * jnp.tanh(half)


def norm(v, gain):
    centered = v - jnp.mean(v, axis=-1, keepdims=True)
    variance = jnp.mean(centered * centered, axis=-1, keepdims=True)
    return centered * lax.rsqrt(variance + 1e-05) * gain


def by_rows(act, *arrays):
    count = arrays[0].shape[0]
    pieces = [act(*(v[c : c + CHUNK] for v in arrays)) for c in range(0, count, CHUNK)]
    return jnp.concatenate(pieces, axis=0)


def silu_rows(*terms):
    return by_rows(lambda *parts: silu(sum(parts[1:], parts[0])).astype(BF), *terms)


def updated_rows(rows, v, gain):
    return by_rows(lambda r, part: (r.astype(F32) + norm(part, gain)).astype(BF), rows, v)


def doubled_column(row, count):
    shape = (2 * count, count)
    spread = jnp.where(iota(shape, 1) == (iota(shape, 0) >> 1), row.astype(F32), 0.0)
    return jnp.sum(spread, axis=1, keepdims=True).astype(I32)


def doubled_row(row, count):
    shape = (count, 2 * count)
    return mm(row.astype(F32).astype(BF), hot((iota(shape, 1) >> 1) == iota(shape, 0))).astype(I32)


def kernel(*refs):
    grid_hbm, sender_hbm = refs[:2]
    hbm = refs[2 : 2 + FETCHED]
    out_ref = refs[2 + FETCHED]
    refs = refs[3 + FETCHED :]
    held = Held(*refs[:FETCHED])
    (
        cells, sender, picked, pick_all, gather_far, gather_own, gather_recv, edge_base,
        req_out, req_in, out_rows, in_rows,
        fetch_sem, cells_sem, sender_sem,
        halo_send, halo_recv, req_send, req_recv, row_send, row_recv,
    ) = refs[FETCHED:]

    lat = lax.axis_index("lat")
    lon = lax.axis_index("lon")
    lat_rows, lon_cols = grid_hbm.shape[:2]

    def place(step_lat, step_lon, sign):
        return (
            (lat + sign * step_lat + LATS) & (LATS - 1),
            (lon + sign * step_lon + LONS) & (LONS - 1),
        )

    def for_all_others(act):
        for step_lon in range(1, LONS):
            act(0, step_lon)

        def band(step_lat, carry):
            for step_lon in range(LONS):
                act(step_lat, step_lon)
            return carry

        lax.fori_loop(1, LATS, band, 0)

    barrier = pltpu.get_barrier_semaphore()
    for i in NEAR:
        pl.semaphore_signal(
            barrier, inc=1, device_id=place(i // LONS, i % LONS, 1), device_id_type=MESH
        )

    def greet(step_lat, step_lon):
        pl.semaphore_signal(
            barrier, inc=1, device_id=place(step_lat, step_lon, 1), device_id_type=MESH
        )

    for step_lat in (0, 1, LATS - 1):
        for step_lon in range(2, LONS - 1):
            greet(step_lat, step_lon)

    def greet_band(step_lat, carry):
        for step_lon in range(LONS):
            greet(step_lat, step_lon)
        return carry

    lax.fori_loop(2, LATS - 1, greet_band, 0)

    sender_copy = pltpu.make_async_copy(sender_hbm, sender, sender_sem)
    sender_copy.start()
    fetches = [
        pltpu.make_async_copy(hbm[n], held[n], fetch_sem.at[n]) for n in range(FETCHED)
    ]
    fetch = Held(*fetches)

    def ready(*copies):
        for copy in copies:
            copy.wait()

    for copy in fetches[:3]:
        copy.start()
    cells_copy = pltpu.make_async_copy(
        grid_hbm, cells.at[pl.ds(HALO, lat_rows), pl.ds(HALO, lon_cols)], cells_sem
    )
    cells_copy.start()
    for copy in fetches[3:]:
        copy.start()

    ready(fetch.g2m_receiver, fetch.mesh_sender, fetch.mesh_receiver)
    senders = held.mesh_sender[...]
    owner = senders >> 5
    row = senders & (NODES - 1)
    rel = ((((owner >> 4) - lat) & (LATS - 1)) << 4) | (((owner & 15) - lon) & (LONS - 1))
    owner2 = hot((iota((2 * PAIRS, EDGES), 0) >> 1) == rel)
    row2 = hot((iota((128, EDGES), 0) >> 1) == row)
    asked = mm_nt(owner2, row2)
    shape = (2 * PAIRS, 128)
    same = (iota(shape, 0) & 1) == (iota(shape, 1) & 1)
    asked = hot((asked > 0.5) & same & (iota(shape, 0) >= 2))
    req_out[...] = asked.reshape(PAIRS, 2, 128)
    req_in[0] = jnp.zeros((2, 128), BF)
    for t in range(STEPS):
        in_rows[t, 0] = jnp.zeros((2, D), BF)

    pl.semaphore_wait(barrier, PAIRS - 1)

    spans = {0: (0, lat_rows, HALO), -1: (0, HALO, HALO + lat_rows), 1: (lat_rows - HALO, HALO, 0)}
    spans_lon = {
        0: (0, lon_cols, HALO), -1: (0, HALO, HALO + lon_cols), 1: (lon_cols - HALO, HALO, 0)
    }
    halo = []
    for n, (a, b) in enumerate(DIRECTIONS):
        row0, rows, to_row = spans[a]
        col0, cols, to_col = spans_lon[b]
        halo.append(
            pltpu.make_async_remote_copy(
                src_ref=grid_hbm.at[pl.ds(row0, rows), pl.ds(col0, cols)],
                dst_ref=cells.at[pl.ds(to_row, rows), pl.ds(to_col, cols)],
                send_sem=halo_send.at[n],
                recv_sem=halo_recv.at[n],
                device_id=((lat + a + LATS) & (LATS - 1), (lon + b + LONS) & (LONS - 1)),
                device_id_type=MESH,
            )
        )
    groups = [
        [copy for copy, (a, _) in zip(halo, DIRECTIONS) if a == which] for which in (0, -1, 1)
    ]
    has_before = lat > 0
    has_after = lat < LATS - 1

    for copy in groups[0]:
        copy.start()

    @pl.when(has_before)
    def _():
        for copy in groups[1]:
            copy.start()

    @pl.when(has_after)
    def _():
        for copy in groups[2]:
            copy.start()

    def ask(step_lat, step_lon):
        i = step_lat * LONS + step_lon
        pltpu.make_async_remote_copy(
            src_ref=req_out.at[i], dst_ref=req_in.at[i], send_sem=req_send, recv_sem=req_recv,
            device_id=place(step_lat, step_lon, 1), device_id_type=MESH,
        ).start()

    for_all_others(ask)

    grid_receivers = held.g2m_receiver[...]
    shape = (2 * NODES, 2 * GRID_EDGES)
    total_grid = hot(
        iota(shape, 0) == 2 * doubled_row(grid_receivers, GRID_EDGES) + (iota(shape, 1) & 1)
    )
    shape = (2 * GRID_EDGES, NODES)
    gather_grid_recv = hot(iota(shape, 1) == doubled_column(grid_receivers, GRID_EDGES))

    ready(fetch.mesh_latents, fetch.g2m_edges, fetch.enc_edge_w1, fetch.enc_edge_b1)
    latents = held.mesh_latents[...]
    shape = (2 * GRID_EDGES, GRID_EDGES)
    grid_edges = mm(hot(iota(shape, 1) == (iota(shape, 0) >> 1)), held.g2m_edges[...]).astype(BF)
    mesh_recv = mm(latents, held.enc_edge_w1[2]).astype(BF)
    grid_base = (
        mm(grid_edges, held.enc_edge_w1[0])
        + mm(gather_grid_recv, mesh_recv)
        + held.enc_edge_b1[...]
    )
    shape = (2 * NODES, NODES)
    state = mm(hot(iota(shape, 1) == (iota(shape, 0) >> 1)), latents).astype(BF)

    sender_copy.wait()
    cells_copy.wait()
    for copy in groups[0]:
        copy.wait_recv()

    @pl.when(has_after)
    def _():
        for copy in groups[1]:
            copy.wait_recv()

    @pl.when(has_before)
    def _():
        for copy in groups[2]:
            copy.wait_recv()

    width = lon_cols * LONS

    def pick(k, carry):
        cell = sender[k]
        cell_row = (cell >> 10) - lat * lat_rows + HALO
        cell_col = ((cell & (width - 1)) - lon * lon_cols + HALO + width) & (width - 1)
        cell_row = jnp.clip(cell_row, 0, cells.shape[0] - 1)
        cell_col = jnp.clip(cell_col, 0, cells.shape[1] - 1)
        picked[k] = cells[cell_row, cell_col]
        return carry

    lax.fori_loop(0, GRID_EDGES, pick, 0, unroll=16)

    ready(fetch.embed_w1, fetch.embed_b1, fetch.embed_w2, fetch.embed_gain)
    inputs = picked[...].reshape(2 * GRID_EDGES, picked.shape[2])
    bias = held.embed_b1[...]
    hidden = by_rows(lambda v: silu(v + bias).astype(BF), mm(inputs, held.embed_w1[...]))
    gain = held.embed_gain[...]
    latent = by_rows(lambda v: norm(v, gain).astype(BF), mm(hidden, held.embed_w2[...]))
    hidden = silu_rows(mm(latent, held.enc_edge_w1[1]), grid_base)
    pltpu.make_async_copy(
        req_in.at[pl.ds(1, PAIRS - 1)], req_in.at[pl.ds(1, PAIRS - 1)], req_recv
    ).wait()
    wanted = req_in[...].reshape(2 * PAIRS, 128)[:, : 2 * NODES]
    shape = (2 * NODES, 2 * NODES)
    before = hot(
        (iota(shape, 0) < iota(shape, 1)) & ((iota(shape, 0) & 1) == (iota(shape, 1) & 1))
    )
    place_of = mm(wanted, before).astype(BF)
    first = jnp.where(place_of.astype(F32) < 0.5, wanted.astype(F32), 0.0).astype(BF)
    shape = (2 * EXTRA * len(NEAR), 2 * PAIRS)
    line = iota(shape, 0)
    which = jnp.zeros_like(line)
    target = jnp.full_like(line, NEAR[0])
    for n in range(1, len(NEAR)):
        later = line >= 2 * EXTRA * n
        which = jnp.where(later, n, which)
        target = jnp.where(later, NEAR[n], target)
    choose = hot(iota(shape, 1) == 2 * target + (line & 1))
    kth = ((line >> 1) - EXTRA * which + 1).astype(F32)[:, : 2 * NODES]
    more = jnp.where(mm(choose, place_of) == kth, mm(choose, wanted), 0.0).astype(BF)
    pick_all[: 2 * PAIRS] = first
    pick_all[2 * PAIRS :] = more

    ready(fetch.enc_edge_w2, fetch.enc_edge_gain)
    new_edges = updated_rows(grid_edges, mm(hidden, held.enc_edge_w2[...]), held.enc_edge_gain[...])
    summed = mm(total_grid, new_edges).astype(BF)
    ready(fetch.enc_node_w1, fetch.enc_node_b1, fetch.enc_node_w2, fetch.enc_node_gain)
    preact = (
        mm(state, held.enc_node_w1[0])
        + mm(summed, held.enc_node_w1[1])
        + held.enc_node_b1[...]
    )
    hidden = silu(preact).astype(BF)
    update = norm(mm(hidden, held.enc_node_w2[...]), held.enc_node_gain[...])
    state = (state.astype(F32) + update).astype(BF)

    ready(fetch.proc_edge_w1, fetch.proc_edge_b1, fetch.proc_edge_w2, fetch.proc_edge_gain)
    ready(fetch.proc_node_w1, fetch.proc_node_b1, fetch.proc_node_w2, fetch.proc_node_gain)
    for t in range(STEPS):
        outgoing = mm(state, held.proc_edge_w1[t, 1]).astype(BF)
        out_rows[t] = mm(pick_all[...], outgoing).astype(BF).reshape(SLOTS, 2, D)

        def give(step_lat, step_lon, t=t):
            i = step_lat * LONS + step_lon
            pltpu.make_async_remote_copy(
                src_ref=out_rows.at[t, i], dst_ref=in_rows.at[t, i],
                send_sem=row_send.at[t], recv_sem=row_recv.at[t],
                device_id=place(step_lat, step_lon, -1), device_id_type=MESH,
            ).start()

        for_all_others(give)
        for n, i in enumerate(NEAR):
            span = pl.ds(PAIRS + EXTRA * n, EXTRA)
            pltpu.make_async_remote_copy(
                src_ref=out_rows.at[t, span], dst_ref=in_rows.at[t, span],
                send_sem=row_send.at[t], recv_sem=row_recv.at[t],
                device_id=place(i // LONS, i % LONS, -1), device_id_type=MESH,
            ).start()

        if t == 0:
            owner1 = hot(iota((PAIRS, EDGES), 0) == rel)
            row1 = iota((NODES, EDGES), 0) == row
            needed = hot(mm_nt(hot(row1), owner1) > 0.5)
            below = hot(iota((NODES, NODES), 1) < iota((NODES, NODES), 0))
            order = mm(below, needed).astype(BF)
            rank = jnp.sum(jnp.where(row1, mm(order, owner1), 0.0), axis=0, keepdims=True).astype(I32)
            near = jnp.zeros_like(rel)
            for n, i in enumerate(NEAR):
                near = jnp.where(rel == i, n, near)
            slot = jnp.where(rank == 0, rel, PAIRS + EXTRA * near + rank - 1)
            slot = jnp.where(rel == 0, SLOTS + row, slot)
            slot_column = doubled_column(slot, EDGES)
            shape = (2 * EDGES, 2 * (SLOTS + NODES))
            gather = hot(iota(shape, 1) == 2 * slot_column + (iota(shape, 0) & 1))
            gather_far[...] = gather[:, : 2 * SLOTS]
            gather_own[...] = gather[:, 2 * SLOTS :]
            receivers = held.mesh_receiver[...]
            shape = (2 * EDGES, 2 * NODES)
            gather_recv[...] = hot(
                iota(shape, 1) == 2 * doubled_column(receivers, EDGES) + (iota(shape, 0) & 1)
            )
            shape = (2 * NODES, 2 * EDGES)
            total_mesh = hot(iota(shape, 0) == 2 * doubled_row(receivers, EDGES) + (iota(shape, 1) & 1))

            ready(fetch.mesh_edges)
            shape = (2 * EDGES, EDGES)
            edge_state = mm(
                hot(iota(shape, 1) == (iota(shape, 0) >> 1)), held.mesh_edges[...]
            ).astype(BF)

        incoming = mm(state, held.proc_edge_w1[t, 2]).astype(BF)
        edge_base[...] = (
            mm(edge_state, held.proc_edge_w1[t, 0])
            + mm(gather_recv[...], incoming)
            + mm(gather_own[...], outgoing)
            + held.proc_edge_b1[t : t + 1]
        )
        node_base = mm(state, held.proc_node_w1[t, 0]) + held.proc_node_b1[t : t + 1]

        arrived = in_rows.at[t, pl.ds(1, SLOTS - 1)]
        pltpu.make_async_copy(arrived, arrived, row_recv.at[t]).wait()
        table = in_rows[t].reshape(2 * SLOTS, D)
        gain = held.proc_edge_gain[t : t + 1]
        halves = []
        for span in (slice(0, EDGES), slice(EDGES, 2 * EDGES)):
            hidden = silu_rows(mm(gather_far[span], table), edge_base[span])
            halves.append(updated_rows(edge_state[span], mm(hidden, held.proc_edge_w2[t]), gain))
        edge_state = jnp.concatenate(halves, axis=0)
        summed = mm(total_mesh, edge_state).astype(BF)
        hidden = silu(node_base + mm(summed, held.proc_node_w1[t, 1])).astype(BF)
        update = norm(mm(hidden, held.proc_node_w2[t]), held.proc_node_gain[t : t + 1])
        state = (state.astype(F32) + update).astype(BF)

    out_ref[...] = state

    for copy in groups[0]:
        copy.wait_send()

    @pl.when(has_before)
    def _():
        for copy in groups[1]:
            copy.wait_send()

    @pl.when(has_after)
    def _():
        for copy in groups[2]:
            copy.wait_send()

    asked_all = req_out.at[pl.ds(1, PAIRS - 1)]
    pltpu.make_async_copy(asked_all, asked_all, req_send).wait()
    for t in range(STEPS):
        sent = out_rows.at[t, pl.ds(1, SLOTS - 1)]
        pltpu.make_async_copy(sent, sent, row_send.at[t]).wait()


def on_device(*args):
    given = Given(*args)
    lat_rows, lon_cols, batch, width = given.grid_inputs.shape

    def flat(row):
        return row.reshape(1, row.shape[0])

    wanted = Held(
        flat(given.g2m_receiver),
        flat(given.mesh_sender),
        flat(given.mesh_receiver),
        given.mesh_latents,
        given.g2m_edges,
        given.enc_edge_w1,
        flat(given.enc_edge_b1),
        given.embed_w1,
        flat(given.embed_b1),
        given.embed_w2,
        flat(given.embed_gain),
        given.enc_edge_w2,
        flat(given.enc_edge_gain),
        given.enc_node_w1,
        flat(given.enc_node_b1),
        given.enc_node_w2,
        flat(given.enc_node_gain),
        given.mesh_edges,
        given.proc_edge_w1,
        given.proc_edge_b1,
        given.proc_edge_w2,
        given.proc_edge_gain,
        given.proc_node_w1,
        given.proc_node_b1,
        given.proc_node_w2,
        given.proc_node_gain,
    )
    operands = [given.grid_inputs, given.g2m_sender, *wanted]
    dma = pltpu.SemaphoreType.DMA
    scratch = [pltpu.VMEM(part.shape, part.dtype) for part in wanted]
    scratch += [
        pltpu.VMEM((lat_rows + 2 * HALO, lon_cols + 2 * HALO, batch, width), BF),
        pltpu.SMEM((GRID_EDGES,), I32),
        pltpu.VMEM((GRID_EDGES, batch, width), BF),
        pltpu.VMEM((2 * SLOTS, 2 * NODES), BF),
        pltpu.VMEM((2 * EDGES, 2 * SLOTS), BF),
        pltpu.VMEM((2 * EDGES, 2 * NODES), BF),
        pltpu.VMEM((2 * EDGES, 2 * NODES), BF),
        pltpu.VMEM((2 * EDGES, D), F32),
        pltpu.VMEM((PAIRS, 2, 128), BF),
        pltpu.VMEM((PAIRS, 2, 128), BF),
        pltpu.VMEM((STEPS, SLOTS, 2, D), BF),
        pltpu.VMEM((STEPS, SLOTS, 2, D), BF),
        dma((FETCHED,)),
        dma,
        dma,
        dma((len(DIRECTIONS),)),
        dma((len(DIRECTIONS),)),
        dma,
        dma,
        dma((STEPS,)),
        dma((STEPS,)),
    ]
    return pl.pallas_call(
        kernel,
        out_shape=jax.ShapeDtypeStruct((NODES * batch, D), BF),
        in_specs=[pl.BlockSpec(memory_space=pl.ANY)] * len(operands),
        out_specs=pl.BlockSpec(memory_space=pltpu.VMEM),
        scratch_shapes=scratch,
        cost_estimate=pl.CostEstimate(
            flops=4 * 10**9, bytes_accessed=15 * 10**6, transcendentals=10**6
        ),
        compiler_params=pltpu.CompilerParams(
            collective_id=0, has_side_effects=True, vmem_limit_bytes=64 * 2**20
        ),
    )(*operands).reshape(NODES, batch, D)


def solution(mesh):
    nodes = P(("lat", "lon"), None)
    edges = P(("lat", "lon"))
    split = [P("lat", "lon", None, None), nodes, nodes, edges, edges, nodes, edges, edges]
    split += [P()] * (len(Given._fields) - len(split))
    return jax.shard_map(
        on_device,
        mesh=mesh,
        in_specs=tuple(split),
        out_specs=P(("lat", "lon"), None, None),
        check_vma=False,
    )
```

```python
from typing import Any, NamedTuple

import jax
import jax.numpy as jnp
from jax import lax
from jax.experimental import pallas as pl
from jax.experimental.pallas import tpu as pltpu
from jax.sharding import PartitionSpec as P

BF = jnp.bfloat16
F32 = jnp.float32
I32 = jnp.int32
MESH = pl.DeviceIdType.MESH

BATCH = 2
D = 512
HALO = 2
STEPS = 2
CHUNK = 64
LATS = 8
LONS = 16
PAIRS = LATS * LONS
NODES = 32
GRID_EDGES = 128
EDGES = 256
NEAR = (1, 15, 16, 17, 31, 112, 113, 127)
EXTRA = 3
SLOTS = PAIRS + EXTRA * len(NEAR)
DIRECTIONS = tuple((a, b) for a in (0, -1, 1) for b in (0, -1, 1) if (a, b) != (0, 0))


class Given(NamedTuple):
    grid_inputs: Any
    mesh_latents: Any
    g2m_edges: Any
    g2m_sender: Any
    g2m_receiver: Any
    mesh_edges: Any
    mesh_sender: Any
    mesh_receiver: Any
    embed_w1: Any
    embed_b1: Any
    embed_w2: Any
    embed_gain: Any
    enc_edge_w1: Any
    enc_edge_b1: Any
    enc_edge_w2: Any
    enc_edge_gain: Any
    enc_node_w1: Any
    enc_node_b1: Any
    enc_node_w2: Any
    enc_node_gain: Any
    proc_edge_w1: Any
    proc_edge_b1: Any
    proc_edge_w2: Any
    proc_edge_gain: Any
    proc_node_w1: Any
    proc_node_b1: Any
    proc_node_w2: Any
    proc_node_gain: Any


class Held(NamedTuple):
    g2m_receiver: Any
    mesh_sender: Any
    mesh_receiver: Any
    mesh_latents: Any
    g2m_edges: Any
    enc_edge_w1: Any
    enc_edge_b1: Any
    embed_w1: Any
    embed_b1: Any
    embed_w2: Any
    embed_gain: Any
    enc_edge_w2: Any
    enc_edge_gain: Any
    enc_node_w1: Any
    enc_node_b1: Any
    enc_node_w2: Any
    enc_node_gain: Any
    mesh_edges: Any
    proc_edge_w1: Any
    proc_edge_b1: Any
    proc_edge_w2: Any
    proc_edge_gain: Any
    proc_node_w1: Any
    proc_node_b1: Any
    proc_node_w2: Any
    proc_node_gain: Any


FETCHED = len(Held._fields)


def mm(a, b):
    return jnp.dot(a, b, preferred_element_type=F32)


def mm_nt(a, b):
    return lax.dot_general(a, b, (((1,), (1,)), ((), ())), preferred_element_type=F32)


def iota(shape, dim):
    return lax.broadcasted_iota(I32, shape, dim)


def hot(mask):
    return jnp.where(mask, 1.0, 0.0).astype(BF)


def silu(v):
    half = 0.5 * v
    return half + half * jnp.tanh(half)


def norm(v, gain):
    centered = v - jnp.mean(v, axis=-1, keepdims=True)
    variance = jnp.mean(centered * centered, axis=-1, keepdims=True)
    return centered * lax.rsqrt(variance + 1e-05) * gain


def by_rows(act, *arrays):
    count = arrays[0].shape[0]
    pieces = [act(*(v[c : c + CHUNK] for v in arrays)) for c in range(0, count, CHUNK)]
    return jnp.concatenate(pieces, axis=0)


def silu_rows(*terms):
    return by_rows(lambda *parts: silu(sum(parts[1:], parts[0])).astype(BF), *terms)


def updated_rows(rows, v, gain):
    return by_rows(lambda r, part: (r.astype(F32) + norm(part, gain)).astype(BF), rows, v)


def doubled_column(row, count):
    shape = (2 * count, count)
    spread = jnp.where(iota(shape, 1) == (iota(shape, 0) >> 1), row.astype(F32), 0.0)
    return jnp.sum(spread, axis=1, keepdims=True).astype(I32)


def doubled_row(row, count):
    shape = (count, 2 * count)
    return mm(row.astype(F32).astype(BF), hot((iota(shape, 1) >> 1) == iota(shape, 0))).astype(I32)


def kernel(*refs):
    grid_hbm, sender_hbm = refs[:2]
    hbm = refs[2 : 2 + FETCHED]
    out_ref = refs[2 + FETCHED]
    refs = refs[3 + FETCHED :]
    held = Held(*refs[:FETCHED])
    (
        cells, sender, picked, pick_all, gather_far, gather_own, gather_recv, edge_base,
        req_out, req_in, out_rows, in_rows,
        fetch_sem, cells_sem, sender_sem,
        halo_send, halo_recv, req_send, req_recv, row_send, row_recv,
    ) = refs[FETCHED:]

    lat = lax.axis_index("lat")
    lon = lax.axis_index("lon")
    lat_rows, lon_cols = grid_hbm.shape[:2]

    def place(step_lat, step_lon, sign):
        return (
            (lat + sign * step_lat + LATS) & (LATS - 1),
            (lon + sign * step_lon + LONS) & (LONS - 1),
        )

    def for_all_others(act):
        steps_lat = (0, 4, 1, 7, 2, 6, 3, 5)
        for step_lat in steps_lat:
            act(step_lat, 8)
        for step_lat in steps_lat[1:]:
            act(step_lat, 0)

        def pair(step_lon, carry):
            for step_lat in steps_lat:
                act(step_lat, step_lon)
                act(step_lat, LONS - step_lon)
            return carry

        lax.fori_loop(1, LONS // 2, pair, 0)

    barrier = pltpu.get_barrier_semaphore()
    for i in NEAR:
        pl.semaphore_signal(
            barrier, inc=1, device_id=place(i // LONS, i % LONS, 1), device_id_type=MESH
        )

    def greet(step_lat, step_lon):
        pl.semaphore_signal(
            barrier, inc=1, device_id=place(step_lat, step_lon, 1), device_id_type=MESH
        )

    for step_lat in (0, 1, LATS - 1):
        for step_lon in range(2, LONS - 1):
            greet(step_lat, step_lon)

    def greet_band(step_lat, carry):
        for step_lon in range(LONS):
            greet(step_lat, step_lon)
        return carry

    lax.fori_loop(2, LATS - 1, greet_band, 0)

    sender_copy = pltpu.make_async_copy(sender_hbm, sender, sender_sem)
    sender_copy.start()
    fetches = [
        pltpu.make_async_copy(hbm[n], held[n], fetch_sem.at[n]) for n in range(FETCHED)
    ]
    fetch = Held(*fetches)

    def ready(*copies):
        for copy in copies:
            copy.wait()

    for copy in fetches[:3]:
        copy.start()
    cells_copy = pltpu.make_async_copy(
        grid_hbm, cells.at[pl.ds(HALO, lat_rows), pl.ds(HALO, lon_cols)], cells_sem
    )
    cells_copy.start()
    for copy in fetches[3:]:
        copy.start()

    ready(fetch.g2m_receiver, fetch.mesh_sender, fetch.mesh_receiver)
    senders = held.mesh_sender[...]
    owner = senders >> 5
    row = senders & (NODES - 1)
    rel = ((((owner >> 4) - lat) & (LATS - 1)) << 4) | (((owner & 15) - lon) & (LONS - 1))
    owner2 = hot((iota((2 * PAIRS, EDGES), 0) >> 1) == rel)
    row2 = hot((iota((128, EDGES), 0) >> 1) == row)
    asked = mm_nt(owner2, row2)
    shape = (2 * PAIRS, 128)
    same = (iota(shape, 0) & 1) == (iota(shape, 1) & 1)
    asked = hot((asked > 0.5) & same & (iota(shape, 0) >= 2))
    req_out[...] = asked.reshape(PAIRS, 2, 128)
    req_in[0] = jnp.zeros((2, 128), BF)
    for t in range(STEPS):
        in_rows[t, 0] = jnp.zeros((2, D), BF)

    pl.semaphore_wait(barrier, PAIRS - 1)

    spans = {0: (0, lat_rows, HALO), -1: (0, HALO, HALO + lat_rows), 1: (lat_rows - HALO, HALO, 0)}
    spans_lon = {
        0: (0, lon_cols, HALO), -1: (0, HALO, HALO + lon_cols), 1: (lon_cols - HALO, HALO, 0)
    }
    halo = []
    for n, (a, b) in enumerate(DIRECTIONS):
        row0, rows, to_row = spans[a]
        col0, cols, to_col = spans_lon[b]
        halo.append(
            pltpu.make_async_remote_copy(
                src_ref=grid_hbm.at[pl.ds(row0, rows), pl.ds(col0, cols)],
                dst_ref=cells.at[pl.ds(to_row, rows), pl.ds(to_col, cols)],
                send_sem=halo_send.at[n],
                recv_sem=halo_recv.at[n],
                device_id=((lat + a + LATS) & (LATS - 1), (lon + b + LONS) & (LONS - 1)),
                device_id_type=MESH,
            )
        )
    groups = [
        [copy for copy, (a, _) in zip(halo, DIRECTIONS) if a == which] for which in (0, -1, 1)
    ]
    has_before = lat > 0
    has_after = lat < LATS - 1

    for copy in groups[0]:
        copy.start()

    @pl.when(has_before)
    def _():
        for copy in groups[1]:
            copy.start()

    @pl.when(has_after)
    def _():
        for copy in groups[2]:
            copy.start()

    def ask(step_lat, step_lon):
        i = step_lat * LONS + step_lon
        pltpu.make_async_remote_copy(
            src_ref=req_out.at[i], dst_ref=req_in.at[i], send_sem=req_send, recv_sem=req_recv,
            device_id=place(step_lat, step_lon, 1), device_id_type=MESH,
        ).start()

    for_all_others(ask)

    grid_receivers = held.g2m_receiver[...]
    shape = (2 * NODES, 2 * GRID_EDGES)
    total_grid = hot(
        iota(shape, 0) == 2 * doubled_row(grid_receivers, GRID_EDGES) + (iota(shape, 1) & 1)
    )
    shape = (2 * GRID_EDGES, NODES)
    gather_grid_recv = hot(iota(shape, 1) == doubled_column(grid_receivers, GRID_EDGES))

    ready(fetch.mesh_latents, fetch.g2m_edges, fetch.enc_edge_w1, fetch.enc_edge_b1)
    latents = held.mesh_latents[...]
    shape = (2 * GRID_EDGES, GRID_EDGES)
    grid_edges = mm(hot(iota(shape, 1) == (iota(shape, 0) >> 1)), held.g2m_edges[...]).astype(BF)
    mesh_recv = mm(latents, held.enc_edge_w1[2]).astype(BF)
    grid_base = (
        mm(grid_edges, held.enc_edge_w1[0])
        + mm(gather_grid_recv, mesh_recv)
        + held.enc_edge_b1[...]
    )
    shape = (2 * NODES, NODES)
    state = mm(hot(iota(shape, 1) == (iota(shape, 0) >> 1)), latents).astype(BF)

    sender_copy.wait()
    cells_copy.wait()
    for copy in groups[0]:
        copy.wait_recv()

    @pl.when(has_after)
    def _():
        for copy in groups[1]:
            copy.wait_recv()

    @pl.when(has_before)
    def _():
        for copy in groups[2]:
            copy.wait_recv()

    width = lon_cols * LONS

    def pick(k, carry):
        cell = sender[k]
        cell_row = (cell >> 10) - lat * lat_rows + HALO
        cell_col = ((cell & (width - 1)) - lon * lon_cols + HALO + width) & (width - 1)
        cell_row = jnp.clip(cell_row, 0, cells.shape[0] - 1)
        cell_col = jnp.clip(cell_col, 0, cells.shape[1] - 1)
        picked[k] = cells[cell_row, cell_col]
        return carry

    lax.fori_loop(0, GRID_EDGES, pick, 0, unroll=16)

    ready(fetch.embed_w1, fetch.embed_b1, fetch.embed_w2, fetch.embed_gain)
    inputs = picked[...].reshape(2 * GRID_EDGES, picked.shape[2])
    bias = held.embed_b1[...]
    hidden = by_rows(lambda v: silu(v + bias).astype(BF), mm(inputs, held.embed_w1[...]))
    gain = held.embed_gain[...]
    latent = by_rows(lambda v: norm(v, gain).astype(BF), mm(hidden, held.embed_w2[...]))
    hidden = silu_rows(mm(latent, held.enc_edge_w1[1]), grid_base)
    pltpu.make_async_copy(
        req_in.at[pl.ds(1, PAIRS - 1)], req_in.at[pl.ds(1, PAIRS - 1)], req_recv
    ).wait()
    wanted = req_in[...].reshape(2 * PAIRS, 128)[:, : 2 * NODES]
    shape = (2 * NODES, 2 * NODES)
    before = hot(
        (iota(shape, 0) < iota(shape, 1)) & ((iota(shape, 0) & 1) == (iota(shape, 1) & 1))
    )
    place_of = mm(wanted, before).astype(BF)
    first = jnp.where(place_of.astype(F32) < 0.5, wanted.astype(F32), 0.0).astype(BF)
    shape = (2 * EXTRA * len(NEAR), 2 * PAIRS)
    line = iota(shape, 0)
    which = jnp.zeros_like(line)
    target = jnp.full_like(line, NEAR[0])
    for n in range(1, len(NEAR)):
        later = line >= 2 * EXTRA * n
        which = jnp.where(later, n, which)
        target = jnp.where(later, NEAR[n], target)
    choose = hot(iota(shape, 1) == 2 * target + (line & 1))
    kth = ((line >> 1) - EXTRA * which + 1).astype(F32)[:, : 2 * NODES]
    more = jnp.where(mm(choose, place_of) == kth, mm(choose, wanted), 0.0).astype(BF)
    pick_all[: 2 * PAIRS] = first
    pick_all[2 * PAIRS :] = more

    ready(fetch.enc_edge_w2, fetch.enc_edge_gain)
    new_edges = updated_rows(grid_edges, mm(hidden, held.enc_edge_w2[...]), held.enc_edge_gain[...])
    summed = mm(total_grid, new_edges).astype(BF)
    ready(fetch.enc_node_w1, fetch.enc_node_b1, fetch.enc_node_w2, fetch.enc_node_gain)
    preact = (
        mm(state, held.enc_node_w1[0])
        + mm(summed, held.enc_node_w1[1])
        + held.enc_node_b1[...]
    )
    hidden = silu(preact).astype(BF)
    update = norm(mm(hidden, held.enc_node_w2[...]), held.enc_node_gain[...])
    state = (state.astype(F32) + update).astype(BF)

    ready(fetch.proc_edge_w1, fetch.proc_edge_b1, fetch.proc_edge_w2, fetch.proc_edge_gain)
    ready(fetch.proc_node_w1, fetch.proc_node_b1, fetch.proc_node_w2, fetch.proc_node_gain)
    for t in range(STEPS):
        outgoing = mm(state, held.proc_edge_w1[t, 1]).astype(BF)
        out_rows[t] = mm(pick_all[...], outgoing).astype(BF).reshape(SLOTS, 2, D)

        def give(step_lat, step_lon, t=t):
            i = step_lat * LONS + step_lon
            pltpu.make_async_remote_copy(
                src_ref=out_rows.at[t, i], dst_ref=in_rows.at[t, i],
                send_sem=row_send.at[t], recv_sem=row_recv.at[t],
                device_id=place(step_lat, step_lon, -1), device_id_type=MESH,
            ).start()

        for_all_others(give)
        for n, i in enumerate(NEAR):
            span = pl.ds(PAIRS + EXTRA * n, EXTRA)
            pltpu.make_async_remote_copy(
                src_ref=out_rows.at[t, span], dst_ref=in_rows.at[t, span],
                send_sem=row_send.at[t], recv_sem=row_recv.at[t],
                device_id=place(i // LONS, i % LONS, -1), device_id_type=MESH,
            ).start()

        if t == 0:
            owner1 = hot(iota((PAIRS, EDGES), 0) == rel)
            row1 = iota((NODES, EDGES), 0) == row
            needed = hot(mm_nt(hot(row1), owner1) > 0.5)
            below = hot(iota((NODES, NODES), 1) < iota((NODES, NODES), 0))
            order = mm(below, needed).astype(BF)
            rank = jnp.sum(jnp.where(row1, mm(order, owner1), 0.0), axis=0, keepdims=True).astype(I32)
            near = jnp.zeros_like(rel)
            for n, i in enumerate(NEAR):
                near = jnp.where(rel == i, n, near)
            slot = jnp.where(rank == 0, rel, PAIRS + EXTRA * near + rank - 1)
            slot = jnp.where(rel == 0, SLOTS + row, slot)
            slot_column = doubled_column(slot, EDGES)
            shape = (2 * EDGES, 2 * (SLOTS + NODES))
            gather = hot(iota(shape, 1) == 2 * slot_column + (iota(shape, 0) & 1))
            gather_far[...] = gather[:, : 2 * SLOTS]
            gather_own[...] = gather[:, 2 * SLOTS :]
            receivers = held.mesh_receiver[...]
            shape = (2 * EDGES, 2 * NODES)
            gather_recv[...] = hot(
                iota(shape, 1) == 2 * doubled_column(receivers, EDGES) + (iota(shape, 0) & 1)
            )
            shape = (2 * NODES, 2 * EDGES)
            total_mesh = hot(iota(shape, 0) == 2 * doubled_row(receivers, EDGES) + (iota(shape, 1) & 1))

            ready(fetch.mesh_edges)
            shape = (2 * EDGES, EDGES)
            edge_state = mm(
                hot(iota(shape, 1) == (iota(shape, 0) >> 1)), held.mesh_edges[...]
            ).astype(BF)

        incoming = mm(state, held.proc_edge_w1[t, 2]).astype(BF)
        edge_base[...] = (
            mm(edge_state, held.proc_edge_w1[t, 0])
            + mm(gather_recv[...], incoming)
            + mm(gather_own[...], outgoing)
            + held.proc_edge_b1[t : t + 1]
        )
        node_base = mm(state, held.proc_node_w1[t, 0]) + held.proc_node_b1[t : t + 1]

        arrived = in_rows.at[t, pl.ds(1, SLOTS - 1)]
        pltpu.make_async_copy(arrived, arrived, row_recv.at[t]).wait()
        table = in_rows[t].reshape(2 * SLOTS, D)
        gain = held.proc_edge_gain[t : t + 1]
        halves = []
        for span in (slice(0, EDGES), slice(EDGES, 2 * EDGES)):
            hidden = silu_rows(mm(gather_far[span], table), edge_base[span])
            halves.append(updated_rows(edge_state[span], mm(hidden, held.proc_edge_w2[t]), gain))
        edge_state = jnp.concatenate(halves, axis=0)
        summed = mm(total_mesh, edge_state).astype(BF)
        hidden = silu(node_base + mm(summed, held.proc_node_w1[t, 1])).astype(BF)
        update = norm(mm(hidden, held.proc_node_w2[t]), held.proc_node_gain[t : t + 1])
        state = (state.astype(F32) + update).astype(BF)

    out_ref[...] = state

    for copy in groups[0]:
        copy.wait_send()

    @pl.when(has_before)
    def _():
        for copy in groups[1]:
            copy.wait_send()

    @pl.when(has_after)
    def _():
        for copy in groups[2]:
            copy.wait_send()

    asked_all = req_out.at[pl.ds(1, PAIRS - 1)]
    pltpu.make_async_copy(asked_all, asked_all, req_send).wait()
    for t in range(STEPS):
        sent = out_rows.at[t, pl.ds(1, SLOTS - 1)]
        pltpu.make_async_copy(sent, sent, row_send.at[t]).wait()


def on_device(*args):
    given = Given(*args)
    lat_rows, lon_cols, batch, width = given.grid_inputs.shape

    def flat(row):
        return row.reshape(1, row.shape[0])

    wanted = Held(
        flat(given.g2m_receiver),
        flat(given.mesh_sender),
        flat(given.mesh_receiver),
        given.mesh_latents,
        given.g2m_edges,
        given.enc_edge_w1,
        flat(given.enc_edge_b1),
        given.embed_w1,
        flat(given.embed_b1),
        given.embed_w2,
        flat(given.embed_gain),
        given.enc_edge_w2,
        flat(given.enc_edge_gain),
        given.enc_node_w1,
        flat(given.enc_node_b1),
        given.enc_node_w2,
        flat(given.enc_node_gain),
        given.mesh_edges,
        given.proc_edge_w1,
        given.proc_edge_b1,
        given.proc_edge_w2,
        given.proc_edge_gain,
        given.proc_node_w1,
        given.proc_node_b1,
        given.proc_node_w2,
        given.proc_node_gain,
    )
    operands = [given.grid_inputs, given.g2m_sender, *wanted]
    dma = pltpu.SemaphoreType.DMA
    scratch = [pltpu.VMEM(part.shape, part.dtype) for part in wanted]
    scratch += [
        pltpu.VMEM((lat_rows + 2 * HALO, lon_cols + 2 * HALO, batch, width), BF),
        pltpu.SMEM((GRID_EDGES,), I32),
        pltpu.VMEM((GRID_EDGES, batch, width), BF),
        pltpu.VMEM((2 * SLOTS, 2 * NODES), BF),
        pltpu.VMEM((2 * EDGES, 2 * SLOTS), BF),
        pltpu.VMEM((2 * EDGES, 2 * NODES), BF),
        pltpu.VMEM((2 * EDGES, 2 * NODES), BF),
        pltpu.VMEM((2 * EDGES, D), F32),
        pltpu.VMEM((PAIRS, 2, 128), BF),
        pltpu.VMEM((PAIRS, 2, 128), BF),
        pltpu.VMEM((STEPS, SLOTS, 2, D), BF),
        pltpu.VMEM((STEPS, SLOTS, 2, D), BF),
        dma((FETCHED,)),
        dma,
        dma,
        dma((len(DIRECTIONS),)),
        dma((len(DIRECTIONS),)),
        dma,
        dma,
        dma((STEPS,)),
        dma((STEPS,)),
    ]
    return pl.pallas_call(
        kernel,
        out_shape=jax.ShapeDtypeStruct((NODES * batch, D), BF),
        in_specs=[pl.BlockSpec(memory_space=pl.ANY)] * len(operands),
        out_specs=pl.BlockSpec(memory_space=pltpu.VMEM),
        scratch_shapes=scratch,
        cost_estimate=pl.CostEstimate(
            flops=4 * 10**9, bytes_accessed=15 * 10**6, transcendentals=10**6
        ),
        compiler_params=pltpu.CompilerParams(
            collective_id=0, has_side_effects=True, vmem_limit_bytes=64 * 2**20
        ),
    )(*operands).reshape(NODES, batch, D)


def solution(mesh):
    nodes = P(("lat", "lon"), None)
    edges = P(("lat", "lon"))
    split = [P("lat", "lon", None, None), nodes, nodes, edges, edges, nodes, edges, edges]
    split += [P()] * (len(Given._fields) - len(split))
    return jax.shard_map(
        on_device,
        mesh=mesh,
        in_specs=tuple(split),
        out_specs=P(("lat", "lon"), None, None),
        check_vma=False,
    )
```

```python
from typing import Any, NamedTuple

import jax
import jax.numpy as jnp
from jax import lax
from jax.experimental import pallas as pl
from jax.experimental.pallas import tpu as pltpu
from jax.sharding import PartitionSpec as P

BF = jnp.bfloat16
F32 = jnp.float32
I32 = jnp.int32
MESH = pl.DeviceIdType.MESH

BATCH = 2
D = 512
HALO = 2
STEPS = 2
CHUNK = 64
LATS = 8
LONS = 16
PAIRS = LATS * LONS
NODES = 32
GRID_EDGES = 128
EDGES = 256
NEAR = (1, 15, 16, 17, 31, 112, 113, 127)
EXTRA = 3
SLOTS = PAIRS + EXTRA * len(NEAR)
CLOSE = 4 * NODES + 2 * EXTRA * len(NEAR)
DIRECTIONS = tuple((a, b) for a in (0, -1, 1) for b in (0, -1, 1) if (a, b) != (0, 0))


class Given(NamedTuple):
    grid_inputs: Any
    mesh_latents: Any
    g2m_edges: Any
    g2m_sender: Any
    g2m_receiver: Any
    mesh_edges: Any
    mesh_sender: Any
    mesh_receiver: Any
    embed_w1: Any
    embed_b1: Any
    embed_w2: Any
    embed_gain: Any
    enc_edge_w1: Any
    enc_edge_b1: Any
    enc_edge_w2: Any
    enc_edge_gain: Any
    enc_node_w1: Any
    enc_node_b1: Any
    enc_node_w2: Any
    enc_node_gain: Any
    proc_edge_w1: Any
    proc_edge_b1: Any
    proc_edge_w2: Any
    proc_edge_gain: Any
    proc_node_w1: Any
    proc_node_b1: Any
    proc_node_w2: Any
    proc_node_gain: Any


class Held(NamedTuple):
    g2m_sender: Any
    g2m_receiver: Any
    mesh_sender: Any
    mesh_receiver: Any
    mesh_latents: Any
    g2m_edges: Any
    enc_edge_w1: Any
    enc_edge_b1: Any
    embed_w1: Any
    embed_b1: Any
    embed_w2: Any
    embed_gain: Any
    enc_edge_w2: Any
    enc_edge_gain: Any
    enc_node_w1: Any
    enc_node_b1: Any
    enc_node_w2: Any
    enc_node_gain: Any
    mesh_edges: Any
    proc_edge_w1: Any
    proc_edge_b1: Any
    proc_edge_w2: Any
    proc_edge_gain: Any
    proc_node_w1: Any
    proc_node_b1: Any
    proc_node_w2: Any
    proc_node_gain: Any


FETCHED = len(Held._fields)
FIRST = FETCHED - 9
PIECES = 4


def mm(a, b):
    return jnp.dot(a, b, preferred_element_type=F32)


def mm_nt(a, b):
    return lax.dot_general(a, b, (((1,), (1,)), ((), ())), preferred_element_type=F32)


def iota(shape, dim):
    return lax.broadcasted_iota(I32, shape, dim)


def hot(mask):
    return jnp.where(mask, 1.0, 0.0).astype(BF)


def silu(v):
    half = 0.5 * v
    return half + half * jnp.tanh(half)


def norm(v, gain):
    centered = v - jnp.mean(v, axis=-1, keepdims=True)
    variance = jnp.mean(centered * centered, axis=-1, keepdims=True)
    return centered * lax.rsqrt(variance + 1e-05) * gain


def by_rows(act, *arrays):
    count = arrays[0].shape[0]
    pieces = [act(*(v[c : c + CHUNK] for v in arrays)) for c in range(0, count, CHUNK)]
    return jnp.concatenate(pieces, axis=0)


def silu_rows(*terms):
    return by_rows(lambda *parts: silu(sum(parts[1:], parts[0])).astype(BF), *terms)


def updated_rows(rows, v, gain):
    return by_rows(lambda r, part: (r.astype(F32) + norm(part, gain)).astype(BF), rows, v)


def doubled_column(row, count):
    shape = (2 * count, count)
    spread = jnp.where(iota(shape, 1) == (iota(shape, 0) >> 1), row.astype(F32), 0.0)
    return jnp.sum(spread, axis=1, keepdims=True).astype(I32)


def doubled_row(row, count):
    shape = (count, 2 * count)
    return mm(row.astype(F32).astype(BF), hot((iota(shape, 1) >> 1) == iota(shape, 0))).astype(I32)


def kernel(*refs):
    grid_hbm = refs[0]
    hbm = refs[1 : 1 + FETCHED]
    out_ref = refs[1 + FETCHED]
    refs = refs[2 + FETCHED :]
    held = Held(*refs[:FETCHED])
    (
        cells, found, sender, picked, pick_all, gather_far, gather_close, close_rows, edge_base,
        req_out, req_in, out_rows, in_rows,
        fetch_sem, cells_sem, sender_sem,
        halo_send, halo_recv, req_send, req_recv, row_send, row_recv,
        more_send, more_recv,
    ) = refs[FETCHED:]

    lat = lax.axis_index("lat")
    lon = lax.axis_index("lon")
    lat_rows, lon_cols = grid_hbm.shape[:2]

    def place(step_lat, step_lon, sign):
        return (
            (lat + sign * step_lat + LATS) & (LATS - 1),
            (lon + sign * step_lon + LONS) & (LONS - 1),
        )

    def for_all_others(act):
        for step_lon in range(1, LONS):
            act(0, step_lon)

        def band(step_lat, carry):
            for step_lon in range(LONS):
                act(step_lat, step_lon)
            return carry

        lax.fori_loop(1, LATS, band, 0)

    fetches = [
        pltpu.make_async_copy(hbm[n], held[n], fetch_sem.at[n]) for n in range(FETCHED)
    ]
    fetch = Held(*fetches)

    def ready(*copies):
        for copy in copies:
            copy.wait()

    for copy in fetches[:4]:
        copy.start()
    cells_copies = []
    for n in range(PIECES):
        rows = lat_rows // PIECES
        cells_copies.append(
            pltpu.make_async_copy(
                grid_hbm.at[pl.ds(n * rows, rows)],
                cells.at[pl.ds(HALO + n * rows, rows), pl.ds(HALO, lon_cols)],
                cells_sem.at[n],
            )
        )
    for copy in cells_copies:
        copy.start()

    barrier = pltpu.get_barrier_semaphore()
    for i in NEAR:
        pl.semaphore_signal(
            barrier, inc=1, device_id=place(i // LONS, i % LONS, 1), device_id_type=MESH
        )

    for copy in fetches[4:FIRST]:
        copy.start()

    def greet(step_lat, step_lon):
        pl.semaphore_signal(
            barrier, inc=1, device_id=place(step_lat, step_lon, 1), device_id_type=MESH
        )

    for step_lat in (0, 1, LATS - 1):
        for step_lon in range(2, LONS - 1):
            greet(step_lat, step_lon)

    def greet_band(step_lat, carry):
        for step_lon in range(LONS):
            greet(step_lat, step_lon)
        return carry

    lax.fori_loop(2, LATS - 1, greet_band, 0)

    ready(fetch.g2m_sender, fetch.g2m_receiver, fetch.mesh_sender, fetch.mesh_receiver)
    cell = held.g2m_sender[...]
    cell_row = (cell >> 10) - lat * lat_rows + HALO
    cell_col = ((cell & (LONS * lon_cols - 1)) - lon * lon_cols + HALO) & (LONS * lon_cols - 1)
    found[0:1] = jnp.clip(cell_row, 0, cells.shape[0] - 1)
    found[1:2] = jnp.clip(cell_col, 0, cells.shape[1] - 1)
    sender_copy = pltpu.make_async_copy(found, sender, sender_sem)
    sender_copy.start()
    senders = held.mesh_sender[...]
    owner = senders >> 5
    row = senders & (NODES - 1)
    rel = ((((owner >> 4) - lat) & (LATS - 1)) << 4) | (((owner & 15) - lon) & (LONS - 1))
    owner2 = hot((iota((2 * PAIRS, EDGES), 0) >> 1) == rel)
    row2 = hot((iota((128, EDGES), 0) >> 1) == row)
    asked = mm_nt(owner2, row2)
    shape = (2 * PAIRS, 128)
    same = (iota(shape, 0) & 1) == (iota(shape, 1) & 1)
    asked = hot((asked > 0.5) & same & (iota(shape, 0) >= 2))
    req_out[...] = asked.reshape(PAIRS, 2, 128)
    req_in[0] = jnp.zeros((2, 128), BF)
    for t in range(STEPS):
        in_rows[t, 0] = jnp.zeros((2, D), BF)

    pl.semaphore_wait(barrier, PAIRS - 1)

    spans = {0: (0, lat_rows, HALO), -1: (0, HALO, HALO + lat_rows), 1: (lat_rows - HALO, HALO, 0)}
    spans_lon = {
        0: (0, lon_cols, HALO), -1: (0, HALO, HALO + lon_cols), 1: (lon_cols - HALO, HALO, 0)
    }
    halo = []
    for n, (a, b) in enumerate(DIRECTIONS):
        row0, rows, to_row = spans[a]
        col0, cols, to_col = spans_lon[b]
        halo.append(
            pltpu.make_async_remote_copy(
                src_ref=grid_hbm.at[pl.ds(row0, rows), pl.ds(col0, cols)],
                dst_ref=cells.at[pl.ds(to_row, rows), pl.ds(to_col, cols)],
                send_sem=halo_send.at[n],
                recv_sem=halo_recv.at[n],
                device_id=((lat + a + LATS) & (LATS - 1), (lon + b + LONS) & (LONS - 1)),
                device_id_type=MESH,
            )
        )
    groups = [
        [copy for copy, (a, _) in zip(halo, DIRECTIONS) if a == which] for which in (0, -1, 1)
    ]
    has_before = lat > 0
    has_after = lat < LATS - 1

    for copy in groups[0]:
        copy.start()

    @pl.when(has_before)
    def _():
        for copy in groups[1]:
            copy.start()

    @pl.when(has_after)
    def _():
        for copy in groups[2]:
            copy.start()

    def ask(step_lat, step_lon):
        i = step_lat * LONS + step_lon
        pltpu.make_async_remote_copy(
            src_ref=req_out.at[i], dst_ref=req_in.at[i], send_sem=req_send, recv_sem=req_recv,
            device_id=place(step_lat, step_lon, 1), device_id_type=MESH,
        ).start()

    for_all_others(ask)

    for copy in fetches[FIRST:]:
        copy.start()

    grid_receivers = held.g2m_receiver[...]
    shape = (2 * NODES, 2 * GRID_EDGES)
    total_grid = hot(
        iota(shape, 0) == 2 * doubled_row(grid_receivers, GRID_EDGES) + (iota(shape, 1) & 1)
    )
    shape = (2 * GRID_EDGES, NODES)
    gather_grid_recv = hot(iota(shape, 1) == doubled_column(grid_receivers, GRID_EDGES))

    ready(fetch.mesh_latents, fetch.g2m_edges, fetch.enc_edge_w1, fetch.enc_edge_b1)
    latents = held.mesh_latents[...]
    shape = (2 * GRID_EDGES, GRID_EDGES)
    grid_edges = mm(hot(iota(shape, 1) == (iota(shape, 0) >> 1)), held.g2m_edges[...]).astype(BF)
    mesh_recv = mm(latents, held.enc_edge_w1[2]).astype(BF)
    grid_base = (
        mm(grid_edges, held.enc_edge_w1[0])
        + mm(gather_grid_recv, mesh_recv)
        + held.enc_edge_b1[...]
    )
    shape = (2 * NODES, NODES)
    state = mm(hot(iota(shape, 1) == (iota(shape, 0) >> 1)), latents).astype(BF)

    sender_copy.wait()
    for copy in cells_copies:
        copy.wait()
    for copy in groups[0]:
        copy.wait_recv()

    @pl.when(has_after)
    def _():
        for copy in groups[1]:
            copy.wait_recv()

    @pl.when(has_before)
    def _():
        for copy in groups[2]:
            copy.wait_recv()

    def pick(k, carry):
        picked[k] = cells[sender[0, k], sender[1, k]]
        return carry

    lax.fori_loop(0, GRID_EDGES, pick, 0, unroll=32)

    ready(fetch.embed_w1, fetch.embed_b1, fetch.embed_w2, fetch.embed_gain)
    inputs = picked[...].reshape(2 * GRID_EDGES, picked.shape[2])
    bias = held.embed_b1[...]
    hidden = by_rows(lambda v: silu(v + bias).astype(BF), mm(inputs, held.embed_w1[...]))
    gain = held.embed_gain[...]
    latent = by_rows(lambda v: norm(v, gain).astype(BF), mm(hidden, held.embed_w2[...]))
    hidden = silu_rows(mm(latent, held.enc_edge_w1[1]), grid_base)
    pltpu.make_async_copy(
        req_in.at[pl.ds(1, PAIRS - 1)], req_in.at[pl.ds(1, PAIRS - 1)], req_recv
    ).wait()
    wanted = req_in[...].reshape(2 * PAIRS, 128)[:, : 2 * NODES]
    shape = (2 * NODES, 2 * NODES)
    before = hot(
        (iota(shape, 0) < iota(shape, 1)) & ((iota(shape, 0) & 1) == (iota(shape, 1) & 1))
    )
    place_of = mm(wanted, before).astype(BF)
    first = jnp.where(place_of.astype(F32) < 0.5, wanted.astype(F32), 0.0).astype(BF)
    shape = (2 * EXTRA * len(NEAR), 2 * PAIRS)
    line = iota(shape, 0)
    which = jnp.zeros_like(line)
    target = jnp.full_like(line, NEAR[0])
    for n in range(1, len(NEAR)):
        later = line >= 2 * EXTRA * n
        which = jnp.where(later, n, which)
        target = jnp.where(later, NEAR[n], target)
    choose = hot(iota(shape, 1) == 2 * target + (line & 1))
    kth = ((line >> 1) - EXTRA * which + 1).astype(F32)[:, : 2 * NODES]
    more = jnp.where(mm(choose, place_of) == kth, mm(choose, wanted), 0.0).astype(BF)
    pick_all[: 2 * PAIRS] = first
    pick_all[2 * PAIRS :] = more

    ready(fetch.enc_edge_w2, fetch.enc_edge_gain)
    new_edges = updated_rows(grid_edges, mm(hidden, held.enc_edge_w2[...]), held.enc_edge_gain[...])
    summed = mm(total_grid, new_edges).astype(BF)
    ready(fetch.enc_node_w1, fetch.enc_node_b1, fetch.enc_node_w2, fetch.enc_node_gain)
    preact = (
        mm(state, held.enc_node_w1[0])
        + mm(summed, held.enc_node_w1[1])
        + held.enc_node_b1[...]
    )
    hidden = silu(preact).astype(BF)
    update = norm(mm(hidden, held.enc_node_w2[...]), held.enc_node_gain[...])
    state = (state.astype(F32) + update).astype(BF)

    ready(fetch.proc_edge_w1, fetch.proc_edge_b1, fetch.proc_edge_w2, fetch.proc_edge_gain)
    ready(fetch.proc_node_w1, fetch.proc_node_b1, fetch.proc_node_w2, fetch.proc_node_gain)
    for t in range(STEPS):
        outgoing = mm(state, held.proc_edge_w1[t, 1]).astype(BF)
        out_rows[t] = mm(pick_all[...], outgoing).astype(BF).reshape(SLOTS, 2, D)

        for n, i in enumerate(NEAR):
            span = pl.ds(PAIRS + EXTRA * n, EXTRA)
            pltpu.make_async_remote_copy(
                src_ref=out_rows.at[t, span], dst_ref=in_rows.at[t, span],
                send_sem=more_send.at[t], recv_sem=more_recv.at[t],
                device_id=place(i // LONS, i % LONS, -1), device_id_type=MESH,
            ).start()

        def give(step_lat, step_lon, t=t):
            i = step_lat * LONS + step_lon
            pltpu.make_async_remote_copy(
                src_ref=out_rows.at[t, i], dst_ref=in_rows.at[t, i],
                send_sem=row_send.at[t], recv_sem=row_recv.at[t],
                device_id=place(step_lat, step_lon, -1), device_id_type=MESH,
            ).start()

        for_all_others(give)

        if t == 0:
            owner1 = hot(iota((PAIRS, EDGES), 0) == rel)
            row1 = iota((NODES, EDGES), 0) == row
            needed = hot(mm_nt(hot(row1), owner1) > 0.5)
            below = hot(iota((NODES, NODES), 1) < iota((NODES, NODES), 0))
            order = mm(below, needed).astype(BF)
            rank = jnp.sum(jnp.where(row1, mm(order, owner1), 0.0), axis=0, keepdims=True).astype(I32)
            near = jnp.zeros_like(rel)
            for n, i in enumerate(NEAR):
                near = jnp.where(rel == i, n, near)
            nowhere = -PAIRS
            far = jnp.where((rank == 0) & (rel > 0), rel, nowhere)
            close = jnp.where(rank == 0, nowhere, 2 * NODES + EXTRA * near + rank - 1)
            close = jnp.where(rel == 0, NODES + row, close)
            shape = (2 * EDGES, 2 * PAIRS)
            gather_far[...] = hot(
                iota(shape, 1) == 2 * doubled_column(far, EDGES) + (iota(shape, 0) & 1)
            )
            receivers = held.mesh_receiver[...]
            shape = (2 * EDGES, CLOSE)
            lane = iota(shape, 1) - (iota(shape, 0) & 1)
            gather_close[...] = hot(
                (lane == 2 * doubled_column(receivers, EDGES))
                | (lane == 2 * doubled_column(close, EDGES))
            )
            shape = (2 * NODES, 2 * EDGES)
            total_mesh = hot(iota(shape, 0) == 2 * doubled_row(receivers, EDGES) + (iota(shape, 1) & 1))

            ready(fetch.mesh_edges)
            shape = (2 * EDGES, EDGES)
            edge_state = mm(
                hot(iota(shape, 1) == (iota(shape, 0) >> 1)), held.mesh_edges[...]
            ).astype(BF)

        close_rows[: 2 * NODES] = mm(state, held.proc_edge_w1[t, 2]).astype(BF)
        close_rows[2 * NODES : 4 * NODES] = outgoing
        node_base = mm(state, held.proc_node_w1[t, 0]) + held.proc_node_b1[t : t + 1]
        arrived = in_rows.at[t, pl.ds(PAIRS, SLOTS - PAIRS)]
        pltpu.make_async_copy(arrived, arrived, more_recv.at[t]).wait()
        close_rows[4 * NODES :] = in_rows[t, PAIRS:].reshape(2 * (SLOTS - PAIRS), D)
        edge_base[...] = (
            mm(edge_state, held.proc_edge_w1[t, 0])
            + mm(gather_close[...], close_rows[...])
            + held.proc_edge_b1[t : t + 1]
        )

        arrived = in_rows.at[t, pl.ds(1, PAIRS - 1)]
        pltpu.make_async_copy(arrived, arrived, row_recv.at[t]).wait()
        table = in_rows[t, :PAIRS].reshape(2 * PAIRS, D)
        gain = held.proc_edge_gain[t : t + 1]
        halves = []
        for span in (slice(0, EDGES), slice(EDGES, 2 * EDGES)):
            hidden = silu_rows(mm(gather_far[span], table), edge_base[span])
            halves.append(updated_rows(edge_state[span], mm(hidden, held.proc_edge_w2[t]), gain))
        edge_state = jnp.concatenate(halves, axis=0)
        summed = mm(total_mesh, edge_state).astype(BF)
        hidden = silu(node_base + mm(summed, held.proc_node_w1[t, 1])).astype(BF)
        update = norm(mm(hidden, held.proc_node_w2[t]), held.proc_node_gain[t : t + 1])
        state = (state.astype(F32) + update).astype(BF)

    out_ref[...] = state

    for copy in groups[0]:
        copy.wait_send()

    @pl.when(has_before)
    def _():
        for copy in groups[1]:
            copy.wait_send()

    @pl.when(has_after)
    def _():
        for copy in groups[2]:
            copy.wait_send()

    asked_all = req_out.at[pl.ds(1, PAIRS - 1)]
    pltpu.make_async_copy(asked_all, asked_all, req_send).wait()
    for t in range(STEPS):
        sent = out_rows.at[t, pl.ds(1, PAIRS - 1)]
        pltpu.make_async_copy(sent, sent, row_send.at[t]).wait()
        sent = out_rows.at[t, pl.ds(PAIRS, SLOTS - PAIRS)]
        pltpu.make_async_copy(sent, sent, more_send.at[t]).wait()


def on_device(*args):
    given = Given(*args)
    lat_rows, lon_cols, batch, width = given.grid_inputs.shape

    def flat(row):
        return row.reshape(1, row.shape[0])

    wanted = Held(
        flat(given.g2m_sender),
        flat(given.g2m_receiver),
        flat(given.mesh_sender),
        flat(given.mesh_receiver),
        given.mesh_latents,
        given.g2m_edges,
        given.enc_edge_w1,
        flat(given.enc_edge_b1),
        given.embed_w1,
        flat(given.embed_b1),
        given.embed_w2,
        flat(given.embed_gain),
        given.enc_edge_w2,
        flat(given.enc_edge_gain),
        given.enc_node_w1,
        flat(given.enc_node_b1),
        given.enc_node_w2,
        flat(given.enc_node_gain),
        given.mesh_edges,
        given.proc_edge_w1,
        given.proc_edge_b1,
        given.proc_edge_w2,
        given.proc_edge_gain,
        given.proc_node_w1,
        given.proc_node_b1,
        given.proc_node_w2,
        given.proc_node_gain,
    )
    operands = [given.grid_inputs, *wanted]
    dma = pltpu.SemaphoreType.DMA
    scratch = [pltpu.VMEM(part.shape, part.dtype) for part in wanted]
    scratch += [
        pltpu.VMEM((lat_rows + 2 * HALO, lon_cols + 2 * HALO, batch, width), BF),
        pltpu.VMEM((2, GRID_EDGES), I32),
        pltpu.SMEM((2, GRID_EDGES), I32),
        pltpu.VMEM((GRID_EDGES, batch, width), BF),
        pltpu.VMEM((2 * SLOTS, 2 * NODES), BF),
        pltpu.VMEM((2 * EDGES, 2 * PAIRS), BF),
        pltpu.VMEM((2 * EDGES, CLOSE), BF),
        pltpu.VMEM((CLOSE, D), BF),
        pltpu.VMEM((2 * EDGES, D), F32),
        pltpu.VMEM((PAIRS, 2, 128), BF),
        pltpu.VMEM((PAIRS, 2, 128), BF),
        pltpu.VMEM((STEPS, SLOTS, 2, D), BF),
        pltpu.VMEM((STEPS, SLOTS, 2, D), BF),
        dma((FETCHED,)),
        dma((PIECES,)),
        dma,
        dma((len(DIRECTIONS),)),
        dma((len(DIRECTIONS),)),
        dma,
        dma,
        dma((STEPS,)),
        dma((STEPS,)),
        dma((STEPS,)),
        dma((STEPS,)),
    ]
    return pl.pallas_call(
        kernel,
        out_shape=jax.ShapeDtypeStruct((NODES * batch, D), BF),
        in_specs=[pl.BlockSpec(memory_space=pl.ANY)] * len(operands),
        out_specs=pl.BlockSpec(memory_space=pltpu.VMEM),
        scratch_shapes=scratch,
        cost_estimate=pl.CostEstimate(
            flops=4 * 10**9, bytes_accessed=15 * 10**6, transcendentals=10**6
        ),
        compiler_params=pltpu.CompilerParams(
            collective_id=0, has_side_effects=True, vmem_limit_bytes=64 * 2**20
        ),
    )(*operands).reshape(NODES, batch, D)


def solution(mesh):
    nodes = P(("lat", "lon"), None)
    edges = P(("lat", "lon"))
    split = [P("lat", "lon", None, None), nodes, nodes, edges, edges, nodes, edges, edges]
    split += [P()] * (len(Given._fields) - len(split))
    return jax.shard_map(
        on_device,
        mesh=mesh,
        in_specs=tuple(split),
        out_specs=P(("lat", "lon"), None, None),
        check_vma=False,
    )
```

```python
from typing import Any, NamedTuple

import jax
import jax.numpy as jnp
from jax import lax
from jax.experimental import pallas as pl
from jax.experimental.pallas import tpu as pltpu
from jax.sharding import PartitionSpec as P

BF = jnp.bfloat16
F32 = jnp.float32
I32 = jnp.int32
MESH = pl.DeviceIdType.MESH

BATCH = 2
D = 512
HALO = 2
STEPS = 2
CHUNK = 64
LATS = 8
LONS = 16
CORES = 2
XS = LATS // CORES
CHIPS = XS * LONS
NODES = 32
CHIP_NODES = CORES * NODES
GRID_EDGES = 128
EDGES = 256
PLAIN = 2 * CHIPS
NEAR = (1, 15, 16, 17, 31, 48, 49, 63)
EXTRA = (6, 6, 3, 3, 3, 3, 3, 3)
START = (0, 6, 12, 15, 18, 21, 24, 27)
SLOTS = PLAIN + sum(EXTRA)
CLOSE = 2 * NODES + 2 * CHIP_NODES + 2 * sum(EXTRA)
DIRECTIONS = tuple((a, b) for a in (0, -1, 1) for b in (0, -1, 1) if (a, b) != (0, 0))


class Given(NamedTuple):
    grid_inputs: Any
    mesh_latents: Any
    g2m_edges: Any
    g2m_sender: Any
    g2m_receiver: Any
    mesh_edges: Any
    mesh_sender: Any
    mesh_receiver: Any
    embed_w1: Any
    embed_b1: Any
    embed_w2: Any
    embed_gain: Any
    enc_edge_w1: Any
    enc_edge_b1: Any
    enc_edge_w2: Any
    enc_edge_gain: Any
    enc_node_w1: Any
    enc_node_b1: Any
    enc_node_w2: Any
    enc_node_gain: Any
    proc_edge_w1: Any
    proc_edge_b1: Any
    proc_edge_w2: Any
    proc_edge_gain: Any
    proc_node_w1: Any
    proc_node_b1: Any
    proc_node_w2: Any
    proc_node_gain: Any


class Held(NamedTuple):
    g2m_sender: Any
    g2m_receiver: Any
    mesh_sender: Any
    mesh_receiver: Any
    mesh_latents: Any
    g2m_edges: Any
    enc_edge_w1: Any
    enc_edge_b1: Any
    embed_w1: Any
    embed_b1: Any
    embed_w2: Any
    embed_gain: Any
    enc_edge_w2: Any
    enc_edge_gain: Any
    enc_node_w1: Any
    enc_node_b1: Any
    enc_node_w2: Any
    enc_node_gain: Any
    mesh_edges: Any
    proc_edge_w1: Any
    proc_edge_b1: Any
    proc_edge_w2: Any
    proc_edge_gain: Any
    proc_node_w1: Any
    proc_node_b1: Any
    proc_node_w2: Any
    proc_node_gain: Any


FETCHED = len(Held._fields)
FIRST = FETCHED - 9
PIECES = 4


def mm(a, b):
    return jnp.dot(a, b, preferred_element_type=F32)


def mm_nt(a, b):
    return lax.dot_general(a, b, (((1,), (1,)), ((), ())), preferred_element_type=F32)


def iota(shape, dim):
    return lax.broadcasted_iota(I32, shape, dim)


def hot(mask):
    return jnp.where(mask, 1.0, 0.0).astype(BF)


def silu(v):
    half = 0.5 * v
    return half + half * jnp.tanh(half)


def norm(v, gain):
    centered = v - jnp.mean(v, axis=-1, keepdims=True)
    variance = jnp.mean(centered * centered, axis=-1, keepdims=True)
    return centered * lax.rsqrt(variance + 1e-05) * gain


def by_rows(act, *arrays):
    count = arrays[0].shape[0]
    pieces = [act(*(v[c : c + CHUNK] for v in arrays)) for c in range(0, count, CHUNK)]
    return jnp.concatenate(pieces, axis=0)


def silu_rows(*terms):
    return by_rows(lambda *parts: silu(sum(parts[1:], parts[0])).astype(BF), *terms)


def updated_rows(rows, v, gain):
    return by_rows(lambda r, part: (r.astype(F32) + norm(part, gain)).astype(BF), rows, v)


def doubled_column(row, count):
    shape = (2 * count, count)
    spread = jnp.where(iota(shape, 1) == (iota(shape, 0) >> 1), row.astype(F32), 0.0)
    return jnp.sum(spread, axis=1, keepdims=True).astype(I32)


def doubled_row(row, count):
    shape = (count, 2 * count)
    return mm(row.astype(F32).astype(BF), hot((iota(shape, 1) >> 1) == iota(shape, 0))).astype(I32)


def kernel(*refs):
    grid_hbm = refs[0]
    hbm = refs[1 : 1 + FETCHED]
    out_ref = refs[1 + FETCHED]
    refs = refs[2 + FETCHED :]
    held = Held(*refs[:FETCHED])
    (
        cells, found, sender, picked, pick_all, gather_far, gather_close, close_rows, edge_base,
        req_out, req_in, chip_rows, out_rows, in_rows,
        fetch_sem, cells_sem, sender_sem,
        halo_send, halo_recv, req_send, req_recv, row_send, row_recv,
        more_send, more_recv, share_send, share_recv,
    ) = refs[FETCHED:]

    lat = lax.axis_index("lat")
    lon = lax.axis_index("lon")
    lat_rows, lon_cols = grid_hbm.shape[:2]

    core = lat & 1
    beside = lat ^ 1

    def place(step_x, step_lon, sign):
        return (
            (lat + sign * CORES * step_x + LATS) & (LATS - 1),
            (lon + sign * step_lon + LONS) & (LONS - 1),
        )

    def for_all_chips(act):
        for step_lon in range(1, LONS):
            act(0, step_lon)

        def band(step_x, carry):
            for step_lon in range(LONS):
                act(step_x, step_lon)
            return carry

        lax.fori_loop(1, XS, band, 0)

    fetches = [
        pltpu.make_async_copy(hbm[n], held[n], fetch_sem.at[n]) for n in range(FETCHED)
    ]
    fetch = Held(*fetches)

    def ready(*copies):
        for copy in copies:
            copy.wait()

    for copy in fetches[:4]:
        copy.start()
    cells_copies = []
    for n in range(PIECES):
        rows = lat_rows // PIECES
        cells_copies.append(
            pltpu.make_async_copy(
                grid_hbm.at[pl.ds(n * rows, rows)],
                cells.at[pl.ds(HALO + n * rows, rows), pl.ds(HALO, lon_cols)],
                cells_sem.at[n],
            )
        )
    for copy in cells_copies:
        copy.start()

    barrier = pltpu.get_barrier_semaphore()
    others = [(a, b) for a in (-1, 1) for b in (0, -1, 1)]
    for a, b in others + [(0, -1), (0, 1)]:
        pl.semaphore_signal(
            barrier, inc=1, device_id_type=MESH,
            device_id=((lat + a + LATS) & (LATS - 1), (lon + b + LONS) & (LONS - 1)),
        )

    for copy in fetches[4:FIRST]:
        copy.start()

    def greet(step_x, step_lon):
        pl.semaphore_signal(
            barrier, inc=1, device_id=place(step_x, step_lon, 1), device_id_type=MESH
        )

    for step_lon in range(2, LONS - 1):
        greet(0, step_lon)

    def greet_band(step_x, carry):
        for step_lon in range(LONS):
            greet(step_x, step_lon)
        return carry

    lax.fori_loop(1, XS, greet_band, 0)

    ready(fetch.g2m_sender, fetch.g2m_receiver, fetch.mesh_sender, fetch.mesh_receiver)
    cell = held.g2m_sender[...]
    cell_row = (cell >> 10) - lat * lat_rows + HALO
    cell_col = ((cell & (LONS * lon_cols - 1)) - lon * lon_cols + HALO) & (LONS * lon_cols - 1)
    found[0:1] = jnp.clip(cell_row, 0, cells.shape[0] - 1)
    found[1:2] = jnp.clip(cell_col, 0, cells.shape[1] - 1)
    sender_copy = pltpu.make_async_copy(found, sender, sender_sem)
    sender_copy.start()
    senders = held.mesh_sender[...]
    owner = senders >> 5
    step_x = ((owner >> 5) - (lat >> 1)) & (XS - 1)
    rel = (step_x << 4) | (((owner & 15) - lon) & (LONS - 1))
    row = (((owner >> 4) & 1) << 5) | (senders & (NODES - 1))
    shape = (2 * CHIPS, EDGES)
    chip2 = hot((iota(shape, 0) >> 1) == rel)
    row2 = hot((iota(shape, 0) >> 1) == row)
    shape = (2 * CHIPS, 2 * CHIP_NODES)
    same = (iota(shape, 0) & 1) == (iota(shape, 1) & 1)
    asked = hot((mm_nt(chip2, row2) > 0.5) & same & (iota(shape, 0) >= 2))
    req_out[...] = asked.reshape(CHIPS, 2, 2 * CHIP_NODES)
    req_in[0] = jnp.zeros((2, 2 * CHIP_NODES), BF)
    for t in range(STEPS):
        in_rows[t, 0] = jnp.zeros((2, D), BF)
        in_rows[t, 1] = jnp.zeros((2, D), BF)

    pl.semaphore_wait(barrier, CHIPS - 1 + len(others))

    spans = {0: (0, lat_rows, HALO), -1: (0, HALO, HALO + lat_rows), 1: (lat_rows - HALO, HALO, 0)}
    spans_lon = {
        0: (0, lon_cols, HALO), -1: (0, HALO, HALO + lon_cols), 1: (lon_cols - HALO, HALO, 0)
    }
    halo = []
    for n, (a, b) in enumerate(DIRECTIONS):
        row0, rows, to_row = spans[a]
        col0, cols, to_col = spans_lon[b]
        halo.append(
            pltpu.make_async_remote_copy(
                src_ref=grid_hbm.at[pl.ds(row0, rows), pl.ds(col0, cols)],
                dst_ref=cells.at[pl.ds(to_row, rows), pl.ds(to_col, cols)],
                send_sem=halo_send.at[n],
                recv_sem=halo_recv.at[n],
                device_id=((lat + a + LATS) & (LATS - 1), (lon + b + LONS) & (LONS - 1)),
                device_id_type=MESH,
            )
        )
    groups = [
        [copy for copy, (a, _) in zip(halo, DIRECTIONS) if a == which] for which in (0, -1, 1)
    ]
    has_before = lat > 0
    has_after = lat < LATS - 1

    for copy in groups[0]:
        copy.start()

    @pl.when(has_before)
    def _():
        for copy in groups[1]:
            copy.start()

    @pl.when(has_after)
    def _():
        for copy in groups[2]:
            copy.start()

    def ask(step_x, step_lon):
        i = step_x * LONS + step_lon
        pltpu.make_async_remote_copy(
            src_ref=req_out.at[i], dst_ref=req_in.at[i], send_sem=req_send, recv_sem=req_recv,
            device_id=place(step_x, step_lon, 1), device_id_type=MESH,
        ).start()

    for_all_chips(ask)

    for copy in fetches[FIRST:]:
        copy.start()

    grid_receivers = held.g2m_receiver[...]
    shape = (2 * NODES, 2 * GRID_EDGES)
    total_grid = hot(
        iota(shape, 0) == 2 * doubled_row(grid_receivers, GRID_EDGES) + (iota(shape, 1) & 1)
    )
    shape = (2 * GRID_EDGES, NODES)
    gather_grid_recv = hot(iota(shape, 1) == doubled_column(grid_receivers, GRID_EDGES))

    ready(fetch.mesh_latents, fetch.g2m_edges, fetch.enc_edge_w1, fetch.enc_edge_b1)
    latents = held.mesh_latents[...]
    shape = (2 * GRID_EDGES, GRID_EDGES)
    grid_edges = mm(hot(iota(shape, 1) == (iota(shape, 0) >> 1)), held.g2m_edges[...]).astype(BF)
    mesh_recv = mm(latents, held.enc_edge_w1[2]).astype(BF)
    grid_base = (
        mm(grid_edges, held.enc_edge_w1[0])
        + mm(gather_grid_recv, mesh_recv)
        + held.enc_edge_b1[...]
    )
    shape = (2 * NODES, NODES)
    state = mm(hot(iota(shape, 1) == (iota(shape, 0) >> 1)), latents).astype(BF)

    sender_copy.wait()
    for copy in cells_copies:
        copy.wait()
    for copy in groups[0]:
        copy.wait_recv()

    @pl.when(has_after)
    def _():
        for copy in groups[1]:
            copy.wait_recv()

    @pl.when(has_before)
    def _():
        for copy in groups[2]:
            copy.wait_recv()

    def pick(k, carry):
        picked[k] = cells[sender[0, k], sender[1, k]]
        return carry

    lax.fori_loop(0, GRID_EDGES, pick, 0, unroll=32)

    ready(fetch.embed_w1, fetch.embed_b1, fetch.embed_w2, fetch.embed_gain)
    inputs = picked[...].reshape(2 * GRID_EDGES, picked.shape[2])
    bias = held.embed_b1[...]
    hidden = by_rows(lambda v: silu(v + bias).astype(BF), mm(inputs, held.embed_w1[...]))
    gain = held.embed_gain[...]
    latent = by_rows(lambda v: norm(v, gain).astype(BF), mm(hidden, held.embed_w2[...]))
    hidden = silu_rows(mm(latent, held.enc_edge_w1[1]), grid_base)
    asked_all = req_in.at[pl.ds(1, CHIPS - 1)]
    pltpu.make_async_copy(asked_all, asked_all, req_recv).wait()
    wanted = req_in[...].reshape(2 * CHIPS, 2 * CHIP_NODES)
    shape = (2 * CHIP_NODES, 2 * CHIP_NODES)
    before = hot(
        (iota(shape, 0) < iota(shape, 1)) & ((iota(shape, 0) & 1) == (iota(shape, 1) & 1))
    )
    place_of = mm(wanted, before).astype(BF)
    shape = (2 * SLOTS, 2 * CHIPS)
    line = iota(shape, 0)
    number = line >> 1
    chip = number >> 1
    kth = number & 1
    for i, start in zip(NEAR, START):
        later = number >= PLAIN + start
        chip = jnp.where(later, i, chip)
        kth = jnp.where(later, number - (PLAIN + start - 2), kth)
    choose = hot(iota(shape, 1) == 2 * chip + (line & 1))
    kth = kth.astype(F32)
    pick_all[...] = jnp.where(mm(choose, place_of) == kth, mm(choose, wanted), 0.0).astype(BF)

    ready(fetch.enc_edge_w2, fetch.enc_edge_gain)
    new_edges = updated_rows(grid_edges, mm(hidden, held.enc_edge_w2[...]), held.enc_edge_gain[...])
    summed = mm(total_grid, new_edges).astype(BF)
    ready(fetch.enc_node_w1, fetch.enc_node_b1, fetch.enc_node_w2, fetch.enc_node_gain)
    preact = (
        mm(state, held.enc_node_w1[0])
        + mm(summed, held.enc_node_w1[1])
        + held.enc_node_b1[...]
    )
    hidden = silu(preact).astype(BF)
    update = norm(mm(hidden, held.enc_node_w2[...]), held.enc_node_gain[...])
    state = (state.astype(F32) + update).astype(BF)

    ready(fetch.proc_edge_w1, fetch.proc_edge_b1, fetch.proc_edge_w2, fetch.proc_edge_gain)
    ready(fetch.proc_node_w1, fetch.proc_node_b1, fetch.proc_node_w2, fetch.proc_node_gain)
    for t in range(STEPS):
        chip_rows[t, core] = mm(state, held.proc_edge_w1[t, 1]).astype(BF)
        share = pltpu.make_async_remote_copy(
            src_ref=chip_rows.at[t, core], dst_ref=chip_rows.at[t, core],
            send_sem=share_send.at[t], recv_sem=share_recv.at[t],
            device_id=(beside, lon), device_id_type=MESH,
        )
        share.start()
        close_rows[: 2 * NODES] = mm(state, held.proc_edge_w1[t, 2]).astype(BF)
        node_base = mm(state, held.proc_node_w1[t, 0]) + held.proc_node_b1[t : t + 1]
        share.wait()
        outgoing = chip_rows[t].reshape(2 * CHIP_NODES, D)
        out_rows[t] = mm(pick_all[...], outgoing).astype(BF).reshape(SLOTS, 2, D)

        for n, i in enumerate(NEAR):
            span = pl.ds(PLAIN + START[n], EXTRA[n])
            pltpu.make_async_remote_copy(
                src_ref=out_rows.at[t, span], dst_ref=in_rows.at[t, span],
                send_sem=more_send.at[t], recv_sem=more_recv.at[t],
                device_id=place(i // LONS, i % LONS, -1), device_id_type=MESH,
            ).start()

        def give(step_x, step_lon, t=t):
            span = pl.ds(2 * (step_x * LONS + step_lon), 2)
            pltpu.make_async_remote_copy(
                src_ref=out_rows.at[t, span], dst_ref=in_rows.at[t, span],
                send_sem=row_send.at[t], recv_sem=row_recv.at[t],
                device_id=place(step_x, step_lon, -1), device_id_type=MESH,
            ).start()

        for_all_chips(give)

        if t == 0:
            chip1 = hot(iota((CHIPS, EDGES), 0) == rel)
            row1 = iota((CHIP_NODES, EDGES), 0) == row
            needed = hot(mm_nt(hot(row1), chip1) > 0.5)
            shape = (CHIP_NODES, CHIP_NODES)
            order = mm(hot(iota(shape, 1) < iota(shape, 0)), needed).astype(BF)
            rank = jnp.where(row1, mm(order, chip1), 0.0)
            rank = jnp.sum(rank, axis=0, keepdims=True).astype(I32)
            extra = jnp.zeros_like(rel)
            for i, start in zip(NEAR, START):
                extra = jnp.where(rel == i, start, extra)
            nowhere = -PLAIN
            far = jnp.where((rank < 2) & (rel > 0), 2 * rel + rank, nowhere)
            close = NODES + CHIP_NODES + extra + rank - 2
            close = jnp.where(rank < 2, nowhere, close)
            close = jnp.where(rel == 0, NODES + row, close)
            shape = (2 * EDGES, 2 * PLAIN)
            gather_far[...] = hot(
                iota(shape, 1) == 2 * doubled_column(far, EDGES) + (iota(shape, 0) & 1)
            )
            receivers = held.mesh_receiver[...]
            shape = (2 * EDGES, CLOSE)
            lane = iota(shape, 1) - (iota(shape, 0) & 1)
            gather_close[...] = hot(
                (lane == 2 * doubled_column(receivers, EDGES))
                | (lane == 2 * doubled_column(close, EDGES))
            )
            shape = (2 * NODES, 2 * EDGES)
            total_mesh = hot(iota(shape, 0) == 2 * doubled_row(receivers, EDGES) + (iota(shape, 1) & 1))

            ready(fetch.mesh_edges)
            shape = (2 * EDGES, EDGES)
            edge_state = mm(
                hot(iota(shape, 1) == (iota(shape, 0) >> 1)), held.mesh_edges[...]
            ).astype(BF)

        own_end = 2 * (NODES + CHIP_NODES)
        close_rows[2 * NODES : own_end] = outgoing
        arrived = in_rows.at[t, pl.ds(PLAIN, SLOTS - PLAIN)]
        pltpu.make_async_copy(arrived, arrived, more_recv.at[t]).wait()
        close_rows[own_end:] = in_rows[t, PLAIN:].reshape(2 * (SLOTS - PLAIN), D)
        edge_base[...] = (
            mm(edge_state, held.proc_edge_w1[t, 0])
            + mm(gather_close[...], close_rows[...])
            + held.proc_edge_b1[t : t + 1]
        )

        arrived = in_rows.at[t, pl.ds(2, PLAIN - 2)]
        pltpu.make_async_copy(arrived, arrived, row_recv.at[t]).wait()
        table = in_rows[t, :PLAIN].reshape(2 * PLAIN, D)
        gain = held.proc_edge_gain[t : t + 1]
        halves = []
        for span in (slice(0, EDGES), slice(EDGES, 2 * EDGES)):
            hidden = silu_rows(mm(gather_far[span], table), edge_base[span])
            halves.append(updated_rows(edge_state[span], mm(hidden, held.proc_edge_w2[t]), gain))
        edge_state = jnp.concatenate(halves, axis=0)
        summed = mm(total_mesh, edge_state).astype(BF)
        hidden = silu(node_base + mm(summed, held.proc_node_w1[t, 1])).astype(BF)
        update = norm(mm(hidden, held.proc_node_w2[t]), held.proc_node_gain[t : t + 1])
        state = (state.astype(F32) + update).astype(BF)

    out_ref[...] = state

    for copy in groups[0]:
        copy.wait_send()

    @pl.when(has_before)
    def _():
        for copy in groups[1]:
            copy.wait_send()

    @pl.when(has_after)
    def _():
        for copy in groups[2]:
            copy.wait_send()

    asked_all = req_out.at[pl.ds(1, CHIPS - 1)]
    pltpu.make_async_copy(asked_all, asked_all, req_send).wait()
    for t in range(STEPS):
        sent = out_rows.at[t, pl.ds(2, PLAIN - 2)]
        pltpu.make_async_copy(sent, sent, row_send.at[t]).wait()
        sent = out_rows.at[t, pl.ds(PLAIN, SLOTS - PLAIN)]
        pltpu.make_async_copy(sent, sent, more_send.at[t]).wait()


def on_device(*args):
    given = Given(*args)
    lat_rows, lon_cols, batch, width = given.grid_inputs.shape

    def flat(row):
        return row.reshape(1, row.shape[0])

    wanted = Held(
        flat(given.g2m_sender),
        flat(given.g2m_receiver),
        flat(given.mesh_sender),
        flat(given.mesh_receiver),
        given.mesh_latents,
        given.g2m_edges,
        given.enc_edge_w1,
        flat(given.enc_edge_b1),
        given.embed_w1,
        flat(given.embed_b1),
        given.embed_w2,
        flat(given.embed_gain),
        given.enc_edge_w2,
        flat(given.enc_edge_gain),
        given.enc_node_w1,
        flat(given.enc_node_b1),
        given.enc_node_w2,
        flat(given.enc_node_gain),
        given.mesh_edges,
        given.proc_edge_w1,
        given.proc_edge_b1,
        given.proc_edge_w2,
        given.proc_edge_gain,
        given.proc_node_w1,
        given.proc_node_b1,
        given.proc_node_w2,
        given.proc_node_gain,
    )
    operands = [given.grid_inputs, *wanted]
    dma = pltpu.SemaphoreType.DMA
    scratch = [pltpu.VMEM(part.shape, part.dtype) for part in wanted]
    scratch += [
        pltpu.VMEM((lat_rows + 2 * HALO, lon_cols + 2 * HALO, batch, width), BF),
        pltpu.VMEM((2, GRID_EDGES), I32),
        pltpu.SMEM((2, GRID_EDGES), I32),
        pltpu.VMEM((GRID_EDGES, batch, width), BF),
        pltpu.VMEM((2 * SLOTS, 2 * CHIP_NODES), BF),
        pltpu.VMEM((2 * EDGES, 2 * PLAIN), BF),
        pltpu.VMEM((2 * EDGES, CLOSE), BF),
        pltpu.VMEM((CLOSE, D), BF),
        pltpu.VMEM((2 * EDGES, D), F32),
        pltpu.VMEM((CHIPS, 2, 2 * CHIP_NODES), BF),
        pltpu.VMEM((CHIPS, 2, 2 * CHIP_NODES), BF),
        pltpu.VMEM((STEPS, CORES, 2 * NODES, D), BF),
        pltpu.VMEM((STEPS, SLOTS, 2, D), BF),
        pltpu.VMEM((STEPS, SLOTS, 2, D), BF),
        dma((FETCHED,)),
        dma((PIECES,)),
        dma,
        dma((len(DIRECTIONS),)),
        dma((len(DIRECTIONS),)),
        dma,
        dma,
        dma((STEPS,)),
        dma((STEPS,)),
        dma((STEPS,)),
        dma((STEPS,)),
        dma((STEPS,)),
        dma((STEPS,)),
    ]
    return pl.pallas_call(
        kernel,
        out_shape=jax.ShapeDtypeStruct((NODES * batch, D), BF),
        in_specs=[pl.BlockSpec(memory_space=pl.ANY)] * len(operands),
        out_specs=pl.BlockSpec(memory_space=pltpu.VMEM),
        scratch_shapes=scratch,
        cost_estimate=pl.CostEstimate(
            flops=4 * 10**9, bytes_accessed=15 * 10**6, transcendentals=10**6
        ),
        compiler_params=pltpu.CompilerParams(
            collective_id=0, has_side_effects=True, vmem_limit_bytes=64 * 2**20
        ),
    )(*operands).reshape(NODES, batch, D)


def solution(mesh):
    nodes = P(("lat", "lon"), None)
    edges = P(("lat", "lon"))
    split = [P("lat", "lon", None, None), nodes, nodes, edges, edges, nodes, edges, edges]
    split += [P()] * (len(Given._fields) - len(split))
    return jax.shard_map(
        on_device,
        mesh=mesh,
        in_specs=tuple(split),
        out_specs=P(("lat", "lon"), None, None),
        check_vma=False,
    )
```

```python
from typing import Any, NamedTuple

import jax
import jax.numpy as jnp
from jax import lax
from jax.experimental import pallas as pl
from jax.experimental.pallas import tpu as pltpu
from jax.sharding import PartitionSpec as P

BF = jnp.bfloat16
F32 = jnp.float32
I32 = jnp.int32
MESH = pl.DeviceIdType.MESH

BATCH = 2
D = 512
HALO = 2
STEPS = 2
CHUNK = 64
LATS = 8
LONS = 16
PAIRS = LATS * LONS
NODES = 32
GRID_EDGES = 128
EDGES = 256
NEAR = (1, 15, 16, 17, 31, 112, 113, 127)
EXTRA = 3
SLOTS = PAIRS + EXTRA * len(NEAR)
CLOSE = 4 * NODES + 2 * EXTRA * len(NEAR)
DIRECTIONS = tuple((a, b) for a in (0, -1, 1) for b in (0, -1, 1) if (a, b) != (0, 0))


class Given(NamedTuple):
    grid_inputs: Any
    mesh_latents: Any
    g2m_edges: Any
    g2m_sender: Any
    g2m_receiver: Any
    mesh_edges: Any
    mesh_sender: Any
    mesh_receiver: Any
    embed_w1: Any
    embed_b1: Any
    embed_w2: Any
    embed_gain: Any
    enc_edge_w1: Any
    enc_edge_b1: Any
    enc_edge_w2: Any
    enc_edge_gain: Any
    enc_node_w1: Any
    enc_node_b1: Any
    enc_node_w2: Any
    enc_node_gain: Any
    proc_edge_w1: Any
    proc_edge_b1: Any
    proc_edge_w2: Any
    proc_edge_gain: Any
    proc_node_w1: Any
    proc_node_b1: Any
    proc_node_w2: Any
    proc_node_gain: Any


class Held(NamedTuple):
    g2m_sender: Any
    g2m_receiver: Any
    mesh_sender: Any
    mesh_receiver: Any
    mesh_latents: Any
    g2m_edges: Any
    enc_edge_w1: Any
    enc_edge_b1: Any
    embed_w1: Any
    embed_b1: Any
    embed_w2: Any
    embed_gain: Any
    enc_edge_w2: Any
    enc_edge_gain: Any
    enc_node_w1: Any
    enc_node_b1: Any
    enc_node_w2: Any
    enc_node_gain: Any
    mesh_edges: Any
    proc_edge_w1: Any
    proc_edge_b1: Any
    proc_edge_w2: Any
    proc_edge_gain: Any
    proc_node_w1: Any
    proc_node_b1: Any
    proc_node_w2: Any
    proc_node_gain: Any


FETCHED = len(Held._fields)
FIRST = FETCHED - 9
PIECES = 4


def mm(a, b):
    return jnp.dot(a, b, preferred_element_type=F32)


def mm_nt(a, b):
    return lax.dot_general(a, b, (((1,), (1,)), ((), ())), preferred_element_type=F32)


def iota(shape, dim):
    return lax.broadcasted_iota(I32, shape, dim)


def hot(mask):
    return jnp.where(mask, 1.0, 0.0).astype(BF)


def silu(v):
    half = 0.5 * v
    return half + half * jnp.tanh(half)


def norm(v, gain):
    count = 1.0 / v.shape[-1]
    mean = jnp.sum(v, axis=-1, keepdims=True) * count
    square = jnp.sum(v * v, axis=-1, keepdims=True) * count
    scale = lax.rsqrt(jnp.maximum(square - mean * mean, 0.0) + 1e-05)
    return (v - mean) * scale * gain


def by_rows(act, *arrays):
    count = arrays[0].shape[0]
    pieces = [act(*(v[c : c + CHUNK] for v in arrays)) for c in range(0, count, CHUNK)]
    return jnp.concatenate(pieces, axis=0)


def silu_rows(*terms):
    return by_rows(lambda *parts: silu(sum(parts[1:], parts[0])).astype(BF), *terms)


def updated_rows(rows, v, gain):
    return by_rows(lambda r, part: (r.astype(F32) + norm(part, gain)).astype(BF), rows, v)


def doubled_column(row, count):
    shape = (2 * count, count)
    spread = jnp.where(iota(shape, 1) == (iota(shape, 0) >> 1), row.astype(F32), 0.0)
    return jnp.sum(spread, axis=1, keepdims=True).astype(I32)


def doubled_row(row, count):
    shape = (count, 2 * count)
    return mm(row.astype(F32).astype(BF), hot((iota(shape, 1) >> 1) == iota(shape, 0))).astype(I32)


def kernel(*refs):
    grid_hbm = refs[0]
    hbm = refs[1 : 1 + FETCHED]
    out_ref = refs[1 + FETCHED]
    refs = refs[2 + FETCHED :]
    held = Held(*refs[:FETCHED])
    (
        cells, found, sender, picked, pick_all, gather_far, gather_close, close_rows, edge_base,
        req_out, req_in, out_rows, in_rows,
        fetch_sem, cells_sem, sender_sem,
        halo_send, halo_recv, req_send, req_recv, row_send, row_recv,
        more_send, more_recv,
    ) = refs[FETCHED:]

    lat = lax.axis_index("lat")
    lon = lax.axis_index("lon")
    lat_rows, lon_cols = grid_hbm.shape[:2]

    def place(step_lat, step_lon, sign):
        return (
            (lat + sign * step_lat + LATS) & (LATS - 1),
            (lon + sign * step_lon + LONS) & (LONS - 1),
        )

    def for_all_others(act):
        for step_lon in range(1, LONS):
            act(0, step_lon)

        def band(step_lat, carry):
            for step_lon in range(LONS):
                act(step_lat, step_lon)
            return carry

        lax.fori_loop(1, LATS, band, 0)

    fetches = [
        pltpu.make_async_copy(hbm[n], held[n], fetch_sem.at[n]) for n in range(FETCHED)
    ]
    fetch = Held(*fetches)

    def ready(*copies):
        for copy in copies:
            copy.wait()

    for copy in fetches[:4]:
        copy.start()
    cells_copies = []
    for n in range(PIECES):
        rows = lat_rows // PIECES
        cells_copies.append(
            pltpu.make_async_copy(
                grid_hbm.at[pl.ds(n * rows, rows)],
                cells.at[pl.ds(HALO + n * rows, rows), pl.ds(HALO, lon_cols)],
                cells_sem.at[n],
            )
        )
    for copy in cells_copies:
        copy.start()

    barrier = pltpu.get_barrier_semaphore()
    for i in NEAR:
        pl.semaphore_signal(
            barrier, inc=1, device_id=place(i // LONS, i % LONS, 1), device_id_type=MESH
        )

    for copy in fetches[4:FIRST]:
        copy.start()

    def greet(step_lat, step_lon):
        pl.semaphore_signal(
            barrier, inc=1, device_id=place(step_lat, step_lon, 1), device_id_type=MESH
        )

    for step_lat in (0, 1, LATS - 1):
        for step_lon in range(2, LONS - 1):
            greet(step_lat, step_lon)

    def greet_band(step_lat, carry):
        for step_lon in range(LONS):
            greet(step_lat, step_lon)
        return carry

    lax.fori_loop(2, LATS - 1, greet_band, 0)

    ready(fetch.g2m_sender, fetch.g2m_receiver, fetch.mesh_sender, fetch.mesh_receiver)
    cell = held.g2m_sender[...]
    cell_row = (cell >> 10) - lat * lat_rows + HALO
    cell_col = ((cell & (LONS * lon_cols - 1)) - lon * lon_cols + HALO) & (LONS * lon_cols - 1)
    found[0:1] = jnp.clip(cell_row, 0, cells.shape[0] - 1)
    found[1:2] = jnp.clip(cell_col, 0, cells.shape[1] - 1)
    sender_copy = pltpu.make_async_copy(found, sender, sender_sem)
    sender_copy.start()
    senders = held.mesh_sender[...]
    owner = senders >> 5
    row = senders & (NODES - 1)
    rel = ((((owner >> 4) - lat) & (LATS - 1)) << 4) | (((owner & 15) - lon) & (LONS - 1))
    owner2 = hot((iota((2 * PAIRS, EDGES), 0) >> 1) == rel)
    row2 = hot((iota((128, EDGES), 0) >> 1) == row)
    asked = mm_nt(owner2, row2)
    shape = (2 * PAIRS, 128)
    same = (iota(shape, 0) & 1) == (iota(shape, 1) & 1)
    asked = hot((asked > 0.5) & same & (iota(shape, 0) >= 2))
    req_out[...] = asked.reshape(PAIRS, 2, 128)
    req_in[0] = jnp.zeros((2, 128), BF)
    for t in range(STEPS):
        in_rows[t, 0] = jnp.zeros((2, D), BF)

    pl.semaphore_wait(barrier, PAIRS - 1)

    spans = {0: (0, lat_rows, HALO), -1: (0, HALO, HALO + lat_rows), 1: (lat_rows - HALO, HALO, 0)}
    spans_lon = {
        0: (0, lon_cols, HALO), -1: (0, HALO, HALO + lon_cols), 1: (lon_cols - HALO, HALO, 0)
    }
    halo = []
    for n, (a, b) in enumerate(DIRECTIONS):
        row0, rows, to_row = spans[a]
        col0, cols, to_col = spans_lon[b]
        halo.append(
            pltpu.make_async_remote_copy(
                src_ref=grid_hbm.at[pl.ds(row0, rows), pl.ds(col0, cols)],
                dst_ref=cells.at[pl.ds(to_row, rows), pl.ds(to_col, cols)],
                send_sem=halo_send.at[n],
                recv_sem=halo_recv.at[n],
                device_id=((lat + a + LATS) & (LATS - 1), (lon + b + LONS) & (LONS - 1)),
                device_id_type=MESH,
            )
        )
    groups = [
        [copy for copy, (a, _) in zip(halo, DIRECTIONS) if a == which] for which in (0, -1, 1)
    ]
    has_before = lat > 0
    has_after = lat < LATS - 1

    for copy in groups[0]:
        copy.start()

    @pl.when(has_before)
    def _():
        for copy in groups[1]:
            copy.start()

    @pl.when(has_after)
    def _():
        for copy in groups[2]:
            copy.start()

    def ask(step_lat, step_lon):
        i = step_lat * LONS + step_lon
        pltpu.make_async_remote_copy(
            src_ref=req_out.at[i], dst_ref=req_in.at[i], send_sem=req_send, recv_sem=req_recv,
            device_id=place(step_lat, step_lon, 1), device_id_type=MESH,
        ).start()

    for_all_others(ask)

    for copy in fetches[FIRST:]:
        copy.start()

    grid_receivers = held.g2m_receiver[...]
    shape = (2 * NODES, 2 * GRID_EDGES)
    total_grid = hot(
        iota(shape, 0) == 2 * doubled_row(grid_receivers, GRID_EDGES) + (iota(shape, 1) & 1)
    )
    shape = (2 * GRID_EDGES, NODES)
    gather_grid_recv = hot(iota(shape, 1) == doubled_column(grid_receivers, GRID_EDGES))

    ready(fetch.mesh_latents, fetch.g2m_edges, fetch.enc_edge_w1, fetch.enc_edge_b1)
    latents = held.mesh_latents[...]
    shape = (2 * GRID_EDGES, GRID_EDGES)
    grid_edges = mm(hot(iota(shape, 1) == (iota(shape, 0) >> 1)), held.g2m_edges[...]).astype(BF)
    mesh_recv = mm(latents, held.enc_edge_w1[2]).astype(BF)
    grid_base = (
        mm(grid_edges, held.enc_edge_w1[0])
        + mm(gather_grid_recv, mesh_recv)
        + held.enc_edge_b1[...]
    )
    shape = (2 * NODES, NODES)
    state = mm(hot(iota(shape, 1) == (iota(shape, 0) >> 1)), latents).astype(BF)

    ready(fetch.embed_w1, fetch.embed_b1, fetch.embed_w2, fetch.embed_gain)
    ready(fetch.enc_edge_w2, fetch.enc_edge_gain)
    ready(fetch.enc_node_w1, fetch.enc_node_b1, fetch.enc_node_w2, fetch.enc_node_gain)
    enc_node_base = mm(state, held.enc_node_w1[0]) + held.enc_node_b1[...]

    sender_copy.wait()
    for copy in cells_copies:
        copy.wait()
    for copy in groups[0]:
        copy.wait_recv()

    @pl.when(has_after)
    def _():
        for copy in groups[1]:
            copy.wait_recv()

    @pl.when(has_before)
    def _():
        for copy in groups[2]:
            copy.wait_recv()

    def pick(k, carry):
        picked[k] = cells[sender[0, k], sender[1, k]]
        return carry

    lax.fori_loop(0, GRID_EDGES, pick, 0, unroll=32)

    inputs = picked[...].reshape(2 * GRID_EDGES, picked.shape[2])
    bias = held.embed_b1[...]
    hidden = by_rows(lambda v: silu(v + bias).astype(BF), mm(inputs, held.embed_w1[...]))
    gain = held.embed_gain[...]
    latent = by_rows(lambda v: norm(v, gain).astype(BF), mm(hidden, held.embed_w2[...]))
    hidden = silu_rows(mm(latent, held.enc_edge_w1[1]), grid_base)
    pltpu.make_async_copy(
        req_in.at[pl.ds(1, PAIRS - 1)], req_in.at[pl.ds(1, PAIRS - 1)], req_recv
    ).wait()
    wanted = req_in[...].reshape(2 * PAIRS, 128)[:, : 2 * NODES]
    shape = (2 * NODES, 2 * NODES)
    before = hot(
        (iota(shape, 0) < iota(shape, 1)) & ((iota(shape, 0) & 1) == (iota(shape, 1) & 1))
    )
    place_of = mm(wanted, before).astype(BF)
    first = jnp.where(place_of.astype(F32) < 0.5, wanted.astype(F32), 0.0).astype(BF)
    shape = (2 * EXTRA * len(NEAR), 2 * PAIRS)
    line = iota(shape, 0)
    which = jnp.zeros_like(line)
    target = jnp.full_like(line, NEAR[0])
    for n in range(1, len(NEAR)):
        later = line >= 2 * EXTRA * n
        which = jnp.where(later, n, which)
        target = jnp.where(later, NEAR[n], target)
    choose = hot(iota(shape, 1) == 2 * target + (line & 1))
    kth = ((line >> 1) - EXTRA * which + 1).astype(F32)[:, : 2 * NODES]
    more = jnp.where(mm(choose, place_of) == kth, mm(choose, wanted), 0.0).astype(BF)
    pick_all[: 2 * PAIRS] = first
    pick_all[2 * PAIRS :] = more

    new_edges = updated_rows(grid_edges, mm(hidden, held.enc_edge_w2[...]), held.enc_edge_gain[...])
    summed = mm(total_grid, new_edges).astype(BF)
    hidden = silu(enc_node_base + mm(summed, held.enc_node_w1[1])).astype(BF)
    update = norm(mm(hidden, held.enc_node_w2[...]), held.enc_node_gain[...])
    state = (state.astype(F32) + update).astype(BF)

    ready(fetch.proc_edge_w1)
    for t in range(STEPS):
        outgoing = mm(state, held.proc_edge_w1[t, 1]).astype(BF)
        out_rows[t] = mm(pick_all[...], outgoing).astype(BF).reshape(SLOTS, 2, D)

        for n, i in enumerate(NEAR):
            span = pl.ds(PAIRS + EXTRA * n, EXTRA)
            pltpu.make_async_remote_copy(
                src_ref=out_rows.at[t, span], dst_ref=in_rows.at[t, span],
                send_sem=more_send.at[t], recv_sem=more_recv.at[t],
                device_id=place(i // LONS, i % LONS, -1), device_id_type=MESH,
            ).start()

        def give(step_lat, step_lon, t=t):
            i = step_lat * LONS + step_lon
            pltpu.make_async_remote_copy(
                src_ref=out_rows.at[t, i], dst_ref=in_rows.at[t, i],
                send_sem=row_send.at[t], recv_sem=row_recv.at[t],
                device_id=place(step_lat, step_lon, -1), device_id_type=MESH,
            ).start()

        for_all_others(give)

        if t == 0:
            ready(fetch.proc_edge_b1, fetch.proc_edge_w2, fetch.proc_edge_gain)
            ready(fetch.proc_node_w1, fetch.proc_node_b1, fetch.proc_node_w2, fetch.proc_node_gain)
            owner1 = hot(iota((PAIRS, EDGES), 0) == rel)
            row1 = iota((NODES, EDGES), 0) == row
            needed = hot(mm_nt(hot(row1), owner1) > 0.5)
            below = hot(iota((NODES, NODES), 1) < iota((NODES, NODES), 0))
            order = mm(below, needed).astype(BF)
            rank = jnp.sum(jnp.where(row1, mm(order, owner1), 0.0), axis=0, keepdims=True).astype(I32)
            near = jnp.zeros_like(rel)
            for n, i in enumerate(NEAR):
                near = jnp.where(rel == i, n, near)
            nowhere = -PAIRS
            far = jnp.where((rank == 0) & (rel > 0), rel, nowhere)
            close = jnp.where(rank == 0, nowhere, 2 * NODES + EXTRA * near + rank - 1)
            close = jnp.where(rel == 0, NODES + row, close)
            shape = (2 * EDGES, 2 * PAIRS)
            gather_far[...] = hot(
                iota(shape, 1) == 2 * doubled_column(far, EDGES) + (iota(shape, 0) & 1)
            )
            receivers = held.mesh_receiver[...]
            shape = (2 * EDGES, CLOSE)
            lane = iota(shape, 1) - (iota(shape, 0) & 1)
            gather_close[...] = hot(
                (lane == 2 * doubled_column(receivers, EDGES))
                | (lane == 2 * doubled_column(close, EDGES))
            )
            shape = (2 * NODES, 2 * EDGES)
            total_mesh = hot(iota(shape, 0) == 2 * doubled_row(receivers, EDGES) + (iota(shape, 1) & 1))

            ready(fetch.mesh_edges)
            shape = (2 * EDGES, EDGES)
            edge_state = mm(
                hot(iota(shape, 1) == (iota(shape, 0) >> 1)), held.mesh_edges[...]
            ).astype(BF)

        close_rows[: 2 * NODES] = mm(state, held.proc_edge_w1[t, 2]).astype(BF)
        close_rows[2 * NODES : 4 * NODES] = outgoing
        node_base = mm(state, held.proc_node_w1[t, 0]) + held.proc_node_b1[t : t + 1]
        arrived = in_rows.at[t, pl.ds(PAIRS, SLOTS - PAIRS)]
        pltpu.make_async_copy(arrived, arrived, more_recv.at[t]).wait()
        close_rows[4 * NODES :] = in_rows[t, PAIRS:].reshape(2 * (SLOTS - PAIRS), D)
        edge_base[...] = (
            mm(edge_state, held.proc_edge_w1[t, 0])
            + mm(gather_close[...], close_rows[...])
            + held.proc_edge_b1[t : t + 1]
        )

        arrived = in_rows.at[t, pl.ds(1, PAIRS - 1)]
        pltpu.make_async_copy(arrived, arrived, row_recv.at[t]).wait()
        table = in_rows[t, :PAIRS].reshape(2 * PAIRS, D)
        gain = held.proc_edge_gain[t : t + 1]
        halves = []
        for span in (slice(0, EDGES), slice(EDGES, 2 * EDGES)):
            hidden = silu_rows(mm(gather_far[span], table), edge_base[span])
            halves.append(updated_rows(edge_state[span], mm(hidden, held.proc_edge_w2[t]), gain))
        edge_state = jnp.concatenate(halves, axis=0)
        summed = mm(total_mesh[:, :EDGES], halves[0]) + mm(total_mesh[:, EDGES:], halves[1])
        summed = summed.astype(BF)
        hidden = silu(node_base + mm(summed, held.proc_node_w1[t, 1])).astype(BF)
        update = norm(mm(hidden, held.proc_node_w2[t]), held.proc_node_gain[t : t + 1])
        state = (state.astype(F32) + update).astype(BF)

    out_ref[...] = state

    for copy in groups[0]:
        copy.wait_send()

    @pl.when(has_before)
    def _():
        for copy in groups[1]:
            copy.wait_send()

    @pl.when(has_after)
    def _():
        for copy in groups[2]:
            copy.wait_send()

    asked_all = req_out.at[pl.ds(1, PAIRS - 1)]
    pltpu.make_async_copy(asked_all, asked_all, req_send).wait()
    for t in range(STEPS):
        sent = out_rows.at[t, pl.ds(1, PAIRS - 1)]
        pltpu.make_async_copy(sent, sent, row_send.at[t]).wait()
        sent = out_rows.at[t, pl.ds(PAIRS, SLOTS - PAIRS)]
        pltpu.make_async_copy(sent, sent, more_send.at[t]).wait()


def on_device(*args):
    given = Given(*args)
    lat_rows, lon_cols, batch, width = given.grid_inputs.shape

    def flat(row):
        return row.reshape(1, row.shape[0])

    wanted = Held(
        flat(given.g2m_sender),
        flat(given.g2m_receiver),
        flat(given.mesh_sender),
        flat(given.mesh_receiver),
        given.mesh_latents,
        given.g2m_edges,
        given.enc_edge_w1,
        flat(given.enc_edge_b1),
        given.embed_w1,
        flat(given.embed_b1),
        given.embed_w2,
        flat(given.embed_gain),
        given.enc_edge_w2,
        flat(given.enc_edge_gain),
        given.enc_node_w1,
        flat(given.enc_node_b1),
        given.enc_node_w2,
        flat(given.enc_node_gain),
        given.mesh_edges,
        given.proc_edge_w1,
        given.proc_edge_b1,
        given.proc_edge_w2,
        given.proc_edge_gain,
        given.proc_node_w1,
        given.proc_node_b1,
        given.proc_node_w2,
        given.proc_node_gain,
    )
    operands = [given.grid_inputs, *wanted]
    dma = pltpu.SemaphoreType.DMA
    scratch = [pltpu.VMEM(part.shape, part.dtype) for part in wanted]
    scratch += [
        pltpu.VMEM((lat_rows + 2 * HALO, lon_cols + 2 * HALO, batch, width), BF),
        pltpu.VMEM((2, GRID_EDGES), I32),
        pltpu.SMEM((2, GRID_EDGES), I32),
        pltpu.VMEM((GRID_EDGES, batch, width), BF),
        pltpu.VMEM((2 * SLOTS, 2 * NODES), BF),
        pltpu.VMEM((2 * EDGES, 2 * PAIRS), BF),
        pltpu.VMEM((2 * EDGES, CLOSE), BF),
        pltpu.VMEM((CLOSE, D), BF),
        pltpu.VMEM((2 * EDGES, D), F32),
        pltpu.VMEM((PAIRS, 2, 128), BF),
        pltpu.VMEM((PAIRS, 2, 128), BF),
        pltpu.VMEM((STEPS, SLOTS, 2, D), BF),
        pltpu.VMEM((STEPS, SLOTS, 2, D), BF),
        dma((FETCHED,)),
        dma((PIECES,)),
        dma,
        dma((len(DIRECTIONS),)),
        dma((len(DIRECTIONS),)),
        dma,
        dma,
        dma((STEPS,)),
        dma((STEPS,)),
        dma((STEPS,)),
        dma((STEPS,)),
    ]
    return pl.pallas_call(
        kernel,
        out_shape=jax.ShapeDtypeStruct((NODES * batch, D), BF),
        in_specs=[pl.BlockSpec(memory_space=pl.ANY)] * len(operands),
        out_specs=pl.BlockSpec(memory_space=pltpu.VMEM),
        scratch_shapes=scratch,
        cost_estimate=pl.CostEstimate(
            flops=4 * 10**9, bytes_accessed=15 * 10**6, transcendentals=10**6
        ),
        compiler_params=pltpu.CompilerParams(
            collective_id=0, has_side_effects=True, vmem_limit_bytes=64 * 2**20
        ),
    )(*operands).reshape(NODES, batch, D)


def solution(mesh):
    nodes = P(("lat", "lon"), None)
    edges = P(("lat", "lon"))
    split = [P("lat", "lon", None, None), nodes, nodes, edges, edges, nodes, edges, edges]
    split += [P()] * (len(Given._fields) - len(split))
    return jax.shard_map(
        on_device,
        mesh=mesh,
        in_specs=tuple(split),
        out_specs=P(("lat", "lon"), None, None),
        check_vma=False,
    )
```

```python
from typing import Any, NamedTuple

import jax
import jax.numpy as jnp
from jax import lax
from jax.experimental import pallas as pl
from jax.experimental.pallas import tpu as pltpu
from jax.sharding import PartitionSpec as P

BF = jnp.bfloat16
F32 = jnp.float32
I32 = jnp.int32
MESH = pl.DeviceIdType.MESH

BATCH = 2
D = 512
HALO = 2
STEPS = 2
CHUNK = 64
LATS = 8
LONS = 16
PAIRS = LATS * LONS
NODES = 32
GRID_EDGES = 128
EDGES = 256
NEAR = (1, 15, 16, 17, 31, 112, 113, 127)
EXTRA = 3
SLOTS = PAIRS + EXTRA * len(NEAR)
CLOSE = 4 * NODES + 2 * EXTRA * len(NEAR)
DIRECTIONS = tuple((a, b) for a in (0, -1, 1) for b in (0, -1, 1) if (a, b) != (0, 0))


class Given(NamedTuple):
    grid_inputs: Any
    mesh_latents: Any
    g2m_edges: Any
    g2m_sender: Any
    g2m_receiver: Any
    mesh_edges: Any
    mesh_sender: Any
    mesh_receiver: Any
    embed_w1: Any
    embed_b1: Any
    embed_w2: Any
    embed_gain: Any
    enc_edge_w1: Any
    enc_edge_b1: Any
    enc_edge_w2: Any
    enc_edge_gain: Any
    enc_node_w1: Any
    enc_node_b1: Any
    enc_node_w2: Any
    enc_node_gain: Any
    proc_edge_w1: Any
    proc_edge_b1: Any
    proc_edge_w2: Any
    proc_edge_gain: Any
    proc_node_w1: Any
    proc_node_b1: Any
    proc_node_w2: Any
    proc_node_gain: Any


class Held(NamedTuple):
    g2m_sender: Any
    g2m_receiver: Any
    mesh_sender: Any
    mesh_receiver: Any
    mesh_latents: Any
    g2m_edges: Any
    enc_edge_w1: Any
    enc_edge_b1: Any
    embed_w1: Any
    embed_b1: Any
    embed_w2: Any
    embed_gain: Any
    enc_edge_w2: Any
    enc_edge_gain: Any
    enc_node_w1: Any
    enc_node_b1: Any
    enc_node_w2: Any
    enc_node_gain: Any
    mesh_edges: Any
    proc_edge_w1: Any
    proc_edge_b1: Any
    proc_edge_w2: Any
    proc_edge_gain: Any
    proc_node_w1: Any
    proc_node_b1: Any
    proc_node_w2: Any
    proc_node_gain: Any


FETCHED = len(Held._fields)
FIRST = FETCHED - 9
PIECES = 4


def mm(a, b):
    return jnp.dot(a, b, preferred_element_type=F32)


def mm_nt(a, b):
    return lax.dot_general(a, b, (((1,), (1,)), ((), ())), preferred_element_type=F32)


def iota(shape, dim):
    return lax.broadcasted_iota(I32, shape, dim)


def hot(mask):
    return jnp.where(mask, 1.0, 0.0).astype(BF)


def silu(v):
    half = 0.5 * v
    return half + half * jnp.tanh(half)


def norm(v, gain):
    count = 1.0 / v.shape[-1]
    mean = jnp.sum(v, axis=-1, keepdims=True) * count
    square = jnp.sum(v * v, axis=-1, keepdims=True) * count
    scale = lax.rsqrt(jnp.maximum(square - mean * mean, 0.0) + 1e-05)
    return (v - mean) * scale * gain


def by_rows(act, *arrays):
    count = arrays[0].shape[0]
    pieces = [act(*(v[c : c + CHUNK] for v in arrays)) for c in range(0, count, CHUNK)]
    return jnp.concatenate(pieces, axis=0)


def silu_rows(*terms):
    return by_rows(lambda *parts: silu(sum(parts[1:], parts[0])).astype(BF), *terms)


def updated_rows(rows, v, gain):
    return by_rows(lambda r, part: (r.astype(F32) + norm(part, gain)).astype(BF), rows, v)


def doubled_column(row, count):
    shape = (2 * count, count)
    spread = jnp.where(iota(shape, 1) == (iota(shape, 0) >> 1), row.astype(F32), 0.0)
    return jnp.sum(spread, axis=1, keepdims=True).astype(I32)


def doubled_row(row, count):
    shape = (count, 2 * count)
    return mm(row.astype(F32).astype(BF), hot((iota(shape, 1) >> 1) == iota(shape, 0))).astype(I32)


def kernel(*refs):
    grid_hbm = refs[0]
    hbm = refs[1 : 1 + FETCHED]
    out_ref = refs[1 + FETCHED]
    refs = refs[2 + FETCHED :]
    held = Held(*refs[:FETCHED])
    (
        cells, found, sender, picked, pick_all, gather_far, gather_close, close_rows, edge_base,
        req_out, req_in, out_rows, in_rows,
        fetch_sem, cells_sem, sender_sem,
        halo_send, halo_recv, req_send, req_recv, row_send, row_recv,
        more_send, more_recv,
    ) = refs[FETCHED:]

    lat = lax.axis_index("lat")
    lon = lax.axis_index("lon")
    lat_rows, lon_cols = grid_hbm.shape[:2]

    def place(step_lat, step_lon, sign):
        return (
            (lat + sign * step_lat + LATS) & (LATS - 1),
            (lon + sign * step_lon + LONS) & (LONS - 1),
        )

    def for_all_others(act):
        for step_lon in range(1, LONS):
            act(0, step_lon)

        def band(step_lat, carry):
            for step_lon in range(LONS):
                act(step_lat, step_lon)
            return carry

        lax.fori_loop(1, LATS, band, 0)

    fetches = [
        pltpu.make_async_copy(hbm[n], held[n], fetch_sem.at[n]) for n in range(FETCHED)
    ]
    fetch = Held(*fetches)

    def ready(*copies):
        for copy in copies:
            copy.wait()

    for copy in fetches[:4]:
        copy.start()
    cells_copies = []
    for n in range(PIECES):
        rows = lat_rows // PIECES
        cells_copies.append(
            pltpu.make_async_copy(
                grid_hbm.at[pl.ds(n * rows, rows)],
                cells.at[pl.ds(HALO + n * rows, rows), pl.ds(HALO, lon_cols)],
                cells_sem.at[n],
            )
        )
    for copy in cells_copies:
        copy.start()

    barrier = pltpu.get_barrier_semaphore()
    for i in NEAR:
        pl.semaphore_signal(
            barrier, inc=1, device_id=place(i // LONS, i % LONS, 1), device_id_type=MESH
        )

    def greet(step_lat, step_lon):
        pl.semaphore_signal(
            barrier, inc=1, device_id=place(step_lat, step_lon, 1), device_id_type=MESH
        )

    for step_lat in (0, 1, LATS - 1):
        for step_lon in range(2, LONS - 1):
            greet(step_lat, step_lon)

    def greet_band(step_lat, carry):
        for step_lon in range(LONS):
            greet(step_lat, step_lon)
        return carry

    lax.fori_loop(2, LATS - 1, greet_band, 0)

    pl.semaphore_wait(barrier, PAIRS - 1)

    spans = {0: (0, lat_rows, HALO), -1: (0, HALO, HALO + lat_rows), 1: (lat_rows - HALO, HALO, 0)}
    spans_lon = {
        0: (0, lon_cols, HALO), -1: (0, HALO, HALO + lon_cols), 1: (lon_cols - HALO, HALO, 0)
    }
    halo = []
    for n, (a, b) in enumerate(DIRECTIONS):
        row0, rows, to_row = spans[a]
        col0, cols, to_col = spans_lon[b]
        halo.append(
            pltpu.make_async_remote_copy(
                src_ref=grid_hbm.at[pl.ds(row0, rows), pl.ds(col0, cols)],
                dst_ref=cells.at[pl.ds(to_row, rows), pl.ds(to_col, cols)],
                send_sem=halo_send.at[n],
                recv_sem=halo_recv.at[n],
                device_id=((lat + a + LATS) & (LATS - 1), (lon + b + LONS) & (LONS - 1)),
                device_id_type=MESH,
            )
        )
    groups = [
        [copy for copy, (a, _) in zip(halo, DIRECTIONS) if a == which] for which in (0, -1, 1)
    ]
    has_before = lat > 0
    has_after = lat < LATS - 1

    for copy in groups[0]:
        copy.start()

    @pl.when(has_before)
    def _():
        for copy in groups[1]:
            copy.start()

    @pl.when(has_after)
    def _():
        for copy in groups[2]:
            copy.start()

    for copy in fetches[4:FIRST]:
        copy.start()

    ready(fetch.g2m_sender, fetch.g2m_receiver, fetch.mesh_sender, fetch.mesh_receiver)
    cell = held.g2m_sender[...]
    cell_row = (cell >> 10) - lat * lat_rows + HALO
    cell_col = ((cell & (LONS * lon_cols - 1)) - lon * lon_cols + HALO) & (LONS * lon_cols - 1)
    found[0:1] = jnp.clip(cell_row, 0, cells.shape[0] - 1)
    found[1:2] = jnp.clip(cell_col, 0, cells.shape[1] - 1)
    sender_copy = pltpu.make_async_copy(found, sender, sender_sem)
    sender_copy.start()
    senders = held.mesh_sender[...]
    owner = senders >> 5
    row = senders & (NODES - 1)
    rel = ((((owner >> 4) - lat) & (LATS - 1)) << 4) | (((owner & 15) - lon) & (LONS - 1))
    owner2 = hot((iota((2 * PAIRS, EDGES), 0) >> 1) == rel)
    row2 = hot((iota((128, EDGES), 0) >> 1) == row)
    asked = mm_nt(owner2, row2)
    shape = (2 * PAIRS, 128)
    same = (iota(shape, 0) & 1) == (iota(shape, 1) & 1)
    asked = hot((asked > 0.5) & same & (iota(shape, 0) >= 2))
    req_out[...] = asked.reshape(PAIRS, 2, 128)
    req_in[0] = jnp.zeros((2, 128), BF)
    for t in range(STEPS):
        in_rows[t, 0] = jnp.zeros((2, D), BF)

    def ask(step_lat, step_lon):
        i = step_lat * LONS + step_lon
        pltpu.make_async_remote_copy(
            src_ref=req_out.at[i], dst_ref=req_in.at[i], send_sem=req_send, recv_sem=req_recv,
            device_id=place(step_lat, step_lon, 1), device_id_type=MESH,
        ).start()

    for_all_others(ask)

    for copy in fetches[FIRST:]:
        copy.start()

    grid_receivers = held.g2m_receiver[...]
    shape = (2 * NODES, 2 * GRID_EDGES)
    total_grid = hot(
        iota(shape, 0) == 2 * doubled_row(grid_receivers, GRID_EDGES) + (iota(shape, 1) & 1)
    )
    shape = (2 * GRID_EDGES, NODES)
    gather_grid_recv = hot(iota(shape, 1) == doubled_column(grid_receivers, GRID_EDGES))

    ready(fetch.mesh_latents, fetch.g2m_edges, fetch.enc_edge_w1, fetch.enc_edge_b1)
    latents = held.mesh_latents[...]
    shape = (2 * GRID_EDGES, GRID_EDGES)
    grid_edges = mm(hot(iota(shape, 1) == (iota(shape, 0) >> 1)), held.g2m_edges[...]).astype(BF)
    mesh_recv = mm(latents, held.enc_edge_w1[2]).astype(BF)
    grid_base = (
        mm(grid_edges, held.enc_edge_w1[0])
        + mm(gather_grid_recv, mesh_recv)
        + held.enc_edge_b1[...]
    )
    shape = (2 * NODES, NODES)
    state = mm(hot(iota(shape, 1) == (iota(shape, 0) >> 1)), latents).astype(BF)

    ready(fetch.embed_w1, fetch.embed_b1, fetch.embed_w2, fetch.embed_gain)
    ready(fetch.enc_edge_w2, fetch.enc_edge_gain)
    ready(fetch.enc_node_w1, fetch.enc_node_b1, fetch.enc_node_w2, fetch.enc_node_gain)
    enc_node_base = mm(state, held.enc_node_w1[0]) + held.enc_node_b1[...]

    sender_copy.wait()
    for copy in cells_copies:
        copy.wait()
    for copy in groups[0]:
        copy.wait_recv()

    @pl.when(has_after)
    def _():
        for copy in groups[1]:
            copy.wait_recv()

    @pl.when(has_before)
    def _():
        for copy in groups[2]:
            copy.wait_recv()

    def pick(k, carry):
        picked[k] = cells[sender[0, k], sender[1, k]]
        return carry

    lax.fori_loop(0, GRID_EDGES, pick, 0, unroll=32)

    inputs = picked[...].reshape(2 * GRID_EDGES, picked.shape[2])
    bias = held.embed_b1[...]
    hidden = by_rows(lambda v: silu(v + bias).astype(BF), mm(inputs, held.embed_w1[...]))
    gain = held.embed_gain[...]
    latent = by_rows(lambda v: norm(v, gain).astype(BF), mm(hidden, held.embed_w2[...]))
    hidden = silu_rows(mm(latent, held.enc_edge_w1[1]), grid_base)
    pltpu.make_async_copy(
        req_in.at[pl.ds(1, PAIRS - 1)], req_in.at[pl.ds(1, PAIRS - 1)], req_recv
    ).wait()
    wanted = req_in[...].reshape(2 * PAIRS, 128)[:, : 2 * NODES]
    shape = (2 * NODES, 2 * NODES)
    before = hot(
        (iota(shape, 0) < iota(shape, 1)) & ((iota(shape, 0) & 1) == (iota(shape, 1) & 1))
    )
    place_of = mm(wanted, before).astype(BF)
    first = jnp.where(place_of.astype(F32) < 0.5, wanted.astype(F32), 0.0).astype(BF)
    shape = (2 * EXTRA * len(NEAR), 2 * PAIRS)
    line = iota(shape, 0)
    which = jnp.zeros_like(line)
    target = jnp.full_like(line, NEAR[0])
    for n in range(1, len(NEAR)):
        later = line >= 2 * EXTRA * n
        which = jnp.where(later, n, which)
        target = jnp.where(later, NEAR[n], target)
    choose = hot(iota(shape, 1) == 2 * target + (line & 1))
    kth = ((line >> 1) - EXTRA * which + 1).astype(F32)[:, : 2 * NODES]
    more = jnp.where(mm(choose, place_of) == kth, mm(choose, wanted), 0.0).astype(BF)
    pick_all[: 2 * PAIRS] = first
    pick_all[2 * PAIRS :] = more

    new_edges = updated_rows(grid_edges, mm(hidden, held.enc_edge_w2[...]), held.enc_edge_gain[...])
    summed = mm(total_grid, new_edges).astype(BF)
    hidden = silu(enc_node_base + mm(summed, held.enc_node_w1[1])).astype(BF)
    update = norm(mm(hidden, held.enc_node_w2[...]), held.enc_node_gain[...])
    state = (state.astype(F32) + update).astype(BF)

    ready(fetch.proc_edge_w1)
    for t in range(STEPS):
        outgoing = mm(state, held.proc_edge_w1[t, 1]).astype(BF)
        out_rows[t] = mm(pick_all[...], outgoing).astype(BF).reshape(SLOTS, 2, D)

        for n, i in enumerate(NEAR):
            span = pl.ds(PAIRS + EXTRA * n, EXTRA)
            pltpu.make_async_remote_copy(
                src_ref=out_rows.at[t, span], dst_ref=in_rows.at[t, span],
                send_sem=more_send.at[t], recv_sem=more_recv.at[t],
                device_id=place(i // LONS, i % LONS, -1), device_id_type=MESH,
            ).start()

        def give(step_lat, step_lon, t=t):
            i = step_lat * LONS + step_lon
            pltpu.make_async_remote_copy(
                src_ref=out_rows.at[t, i], dst_ref=in_rows.at[t, i],
                send_sem=row_send.at[t], recv_sem=row_recv.at[t],
                device_id=place(step_lat, step_lon, -1), device_id_type=MESH,
            ).start()

        for_all_others(give)

        if t == 0:
            ready(fetch.proc_edge_b1, fetch.proc_edge_w2, fetch.proc_edge_gain)
            ready(fetch.proc_node_w1, fetch.proc_node_b1, fetch.proc_node_w2, fetch.proc_node_gain)
            owner1 = hot(iota((PAIRS, EDGES), 0) == rel)
            row1 = iota((NODES, EDGES), 0) == row
            needed = hot(mm_nt(hot(row1), owner1) > 0.5)
            below = hot(iota((NODES, NODES), 1) < iota((NODES, NODES), 0))
            order = mm(below, needed).astype(BF)
            rank = jnp.sum(jnp.where(row1, mm(order, owner1), 0.0), axis=0, keepdims=True).astype(I32)
            near = jnp.zeros_like(rel)
            for n, i in enumerate(NEAR):
                near = jnp.where(rel == i, n, near)
            nowhere = -PAIRS
            far = jnp.where((rank == 0) & (rel > 0), rel, nowhere)
            close = jnp.where(rank == 0, nowhere, 2 * NODES + EXTRA * near + rank - 1)
            close = jnp.where(rel == 0, NODES + row, close)
            shape = (2 * EDGES, 2 * PAIRS)
            gather_far[...] = hot(
                iota(shape, 1) == 2 * doubled_column(far, EDGES) + (iota(shape, 0) & 1)
            )
            receivers = held.mesh_receiver[...]
            shape = (2 * EDGES, CLOSE)
            lane = iota(shape, 1) - (iota(shape, 0) & 1)
            gather_close[...] = hot(
                (lane == 2 * doubled_column(receivers, EDGES))
                | (lane == 2 * doubled_column(close, EDGES))
            )
            shape = (2 * NODES, 2 * EDGES)
            total_mesh = hot(iota(shape, 0) == 2 * doubled_row(receivers, EDGES) + (iota(shape, 1) & 1))

            ready(fetch.mesh_edges)
            shape = (2 * EDGES, EDGES)
            edge_state = mm(
                hot(iota(shape, 1) == (iota(shape, 0) >> 1)), held.mesh_edges[...]
            ).astype(BF)

        close_rows[: 2 * NODES] = mm(state, held.proc_edge_w1[t, 2]).astype(BF)
        close_rows[2 * NODES : 4 * NODES] = outgoing
        node_base = mm(state, held.proc_node_w1[t, 0]) + held.proc_node_b1[t : t + 1]
        arrived = in_rows.at[t, pl.ds(PAIRS, SLOTS - PAIRS)]
        pltpu.make_async_copy(arrived, arrived, more_recv.at[t]).wait()
        close_rows[4 * NODES :] = in_rows[t, PAIRS:].reshape(2 * (SLOTS - PAIRS), D)
        edge_base[...] = (
            mm(edge_state, held.proc_edge_w1[t, 0])
            + mm(gather_close[...], close_rows[...])
            + held.proc_edge_b1[t : t + 1]
        )

        arrived = in_rows.at[t, pl.ds(1, PAIRS - 1)]
        pltpu.make_async_copy(arrived, arrived, row_recv.at[t]).wait()
        table = in_rows[t, :PAIRS].reshape(2 * PAIRS, D)
        gain = held.proc_edge_gain[t : t + 1]
        halves = []
        for span in (slice(0, EDGES), slice(EDGES, 2 * EDGES)):
            hidden = silu_rows(mm(gather_far[span], table), edge_base[span])
            halves.append(updated_rows(edge_state[span], mm(hidden, held.proc_edge_w2[t]), gain))
        edge_state = jnp.concatenate(halves, axis=0)
        summed = mm(total_mesh[:, :EDGES], halves[0]) + mm(total_mesh[:, EDGES:], halves[1])
        summed = summed.astype(BF)
        hidden = silu(node_base + mm(summed, held.proc_node_w1[t, 1])).astype(BF)
        update = norm(mm(hidden, held.proc_node_w2[t]), held.proc_node_gain[t : t + 1])
        state = (state.astype(F32) + update).astype(BF)

    out_ref[...] = state

    for copy in groups[0]:
        copy.wait_send()

    @pl.when(has_before)
    def _():
        for copy in groups[1]:
            copy.wait_send()

    @pl.when(has_after)
    def _():
        for copy in groups[2]:
            copy.wait_send()

    asked_all = req_out.at[pl.ds(1, PAIRS - 1)]
    pltpu.make_async_copy(asked_all, asked_all, req_send).wait()
    for t in range(STEPS):
        sent = out_rows.at[t, pl.ds(1, PAIRS - 1)]
        pltpu.make_async_copy(sent, sent, row_send.at[t]).wait()
        sent = out_rows.at[t, pl.ds(PAIRS, SLOTS - PAIRS)]
        pltpu.make_async_copy(sent, sent, more_send.at[t]).wait()


def on_device(*args):
    given = Given(*args)
    lat_rows, lon_cols, batch, width = given.grid_inputs.shape

    def flat(row):
        return row.reshape(1, row.shape[0])

    wanted = Held(
        flat(given.g2m_sender),
        flat(given.g2m_receiver),
        flat(given.mesh_sender),
        flat(given.mesh_receiver),
        given.mesh_latents,
        given.g2m_edges,
        given.enc_edge_w1,
        flat(given.enc_edge_b1),
        given.embed_w1,
        flat(given.embed_b1),
        given.embed_w2,
        flat(given.embed_gain),
        given.enc_edge_w2,
        flat(given.enc_edge_gain),
        given.enc_node_w1,
        flat(given.enc_node_b1),
        given.enc_node_w2,
        flat(given.enc_node_gain),
        given.mesh_edges,
        given.proc_edge_w1,
        given.proc_edge_b1,
        given.proc_edge_w2,
        given.proc_edge_gain,
        given.proc_node_w1,
        given.proc_node_b1,
        given.proc_node_w2,
        given.proc_node_gain,
    )
    operands = [given.grid_inputs, *wanted]
    dma = pltpu.SemaphoreType.DMA
    scratch = [pltpu.VMEM(part.shape, part.dtype) for part in wanted]
    scratch += [
        pltpu.VMEM((lat_rows + 2 * HALO, lon_cols + 2 * HALO, batch, width), BF),
        pltpu.VMEM((2, GRID_EDGES), I32),
        pltpu.SMEM((2, GRID_EDGES), I32),
        pltpu.VMEM((GRID_EDGES, batch, width), BF),
        pltpu.VMEM((2 * SLOTS, 2 * NODES), BF),
        pltpu.VMEM((2 * EDGES, 2 * PAIRS), BF),
        pltpu.VMEM((2 * EDGES, CLOSE), BF),
        pltpu.VMEM((CLOSE, D), BF),
        pltpu.VMEM((2 * EDGES, D), F32),
        pltpu.VMEM((PAIRS, 2, 128), BF),
        pltpu.VMEM((PAIRS, 2, 128), BF),
        pltpu.VMEM((STEPS, SLOTS, 2, D), BF),
        pltpu.VMEM((STEPS, SLOTS, 2, D), BF),
        dma((FETCHED,)),
        dma((PIECES,)),
        dma,
        dma((len(DIRECTIONS),)),
        dma((len(DIRECTIONS),)),
        dma,
        dma,
        dma((STEPS,)),
        dma((STEPS,)),
        dma((STEPS,)),
        dma((STEPS,)),
    ]
    return pl.pallas_call(
        kernel,
        out_shape=jax.ShapeDtypeStruct((NODES * batch, D), BF),
        in_specs=[pl.BlockSpec(memory_space=pl.ANY)] * len(operands),
        out_specs=pl.BlockSpec(memory_space=pltpu.VMEM),
        scratch_shapes=scratch,
        cost_estimate=pl.CostEstimate(
            flops=4 * 10**9, bytes_accessed=15 * 10**6, transcendentals=10**6
        ),
        compiler_params=pltpu.CompilerParams(
            collective_id=0, has_side_effects=True, vmem_limit_bytes=64 * 2**20
        ),
    )(*operands).reshape(NODES, batch, D)


def solution(mesh):
    nodes = P(("lat", "lon"), None)
    edges = P(("lat", "lon"))
    split = [P("lat", "lon", None, None), nodes, nodes, edges, edges, nodes, edges, edges]
    split += [P()] * (len(Given._fields) - len(split))
    return jax.shard_map(
        on_device,
        mesh=mesh,
        in_specs=tuple(split),
        out_specs=P(("lat", "lon"), None, None),
        check_vma=False,
    )
```

```python
from typing import Any, NamedTuple

import jax
import jax.numpy as jnp
from jax import lax
from jax.experimental import pallas as pl
from jax.experimental.pallas import tpu as pltpu
from jax.sharding import PartitionSpec as P

BF = jnp.bfloat16
F32 = jnp.float32
I32 = jnp.int32
MESH = pl.DeviceIdType.MESH

BATCH = 2
D = 512
HALO = 2
STEPS = 2
CHUNK = 64
LATS = 8
LONS = 16
PAIRS = LATS * LONS
NODES = 32
GRID_EDGES = 128
EDGES = 256
NEAR = (1, 15, 16, 17, 31, 112, 113, 127)
EXTRA = 3
SLOTS = PAIRS + EXTRA * len(NEAR)
CLOSE = 4 * NODES + 2 * EXTRA * len(NEAR)
DIRECTIONS = tuple((a, b) for a in (0, -1, 1) for b in (0, -1, 1) if (a, b) != (0, 0))


class Given(NamedTuple):
    grid_inputs: Any
    mesh_latents: Any
    g2m_edges: Any
    g2m_sender: Any
    g2m_receiver: Any
    mesh_edges: Any
    mesh_sender: Any
    mesh_receiver: Any
    embed_w1: Any
    embed_b1: Any
    embed_w2: Any
    embed_gain: Any
    enc_edge_w1: Any
    enc_edge_b1: Any
    enc_edge_w2: Any
    enc_edge_gain: Any
    enc_node_w1: Any
    enc_node_b1: Any
    enc_node_w2: Any
    enc_node_gain: Any
    proc_edge_w1: Any
    proc_edge_b1: Any
    proc_edge_w2: Any
    proc_edge_gain: Any
    proc_node_w1: Any
    proc_node_b1: Any
    proc_node_w2: Any
    proc_node_gain: Any


class Held(NamedTuple):
    g2m_sender: Any
    g2m_receiver: Any
    mesh_sender: Any
    mesh_receiver: Any
    mesh_latents: Any
    g2m_edges: Any
    enc_edge_w1: Any
    enc_edge_b1: Any
    embed_w1: Any
    embed_b1: Any
    embed_w2: Any
    embed_gain: Any
    enc_edge_w2: Any
    enc_edge_gain: Any
    enc_node_w1: Any
    enc_node_b1: Any
    enc_node_w2: Any
    enc_node_gain: Any
    mesh_edges: Any
    proc_edge_w1: Any
    proc_edge_b1: Any
    proc_edge_w2: Any
    proc_edge_gain: Any
    proc_node_w1: Any
    proc_node_b1: Any
    proc_node_w2: Any
    proc_node_gain: Any


FETCHED = len(Held._fields)
FIRST = FETCHED - 9
PIECES = 4


def mm(a, b):
    return jnp.dot(a, b, preferred_element_type=F32)


def mm_nt(a, b):
    return lax.dot_general(a, b, (((1,), (1,)), ((), ())), preferred_element_type=F32)


def iota(shape, dim):
    return lax.broadcasted_iota(I32, shape, dim)


def hot(mask):
    return jnp.where(mask, 1.0, 0.0).astype(BF)


def silu(v):
    half = 0.5 * v
    return half + half * jnp.tanh(half)


def norm(v, gain):
    count = 1.0 / v.shape[-1]
    mean = jnp.sum(v, axis=-1, keepdims=True) * count
    square = jnp.sum(v * v, axis=-1, keepdims=True) * count
    scale = lax.rsqrt(jnp.maximum(square - mean * mean, 0.0) + 1e-05)
    return (v - mean) * scale * gain


def by_rows(act, *arrays):
    count = arrays[0].shape[0]
    pieces = [act(*(v[c : c + CHUNK] for v in arrays)) for c in range(0, count, CHUNK)]
    return jnp.concatenate(pieces, axis=0)


def silu_rows(*terms):
    return by_rows(lambda *parts: silu(sum(parts[1:], parts[0])).astype(BF), *terms)


def updated_rows(rows, v, gain):
    return by_rows(lambda r, part: (r.astype(F32) + norm(part, gain)).astype(BF), rows, v)


def doubled_column(row, count):
    shape = (2 * count, count)
    spread = jnp.where(iota(shape, 1) == (iota(shape, 0) >> 1), row.astype(F32), 0.0)
    return jnp.sum(spread, axis=1, keepdims=True).astype(I32)


def doubled_row(row, count):
    shape = (count, 2 * count)
    return mm(row.astype(F32).astype(BF), hot((iota(shape, 1) >> 1) == iota(shape, 0))).astype(I32)


def kernel(*refs):
    grid_hbm = refs[0]
    hbm = refs[1 : 1 + FETCHED]
    out_ref = refs[1 + FETCHED]
    refs = refs[2 + FETCHED :]
    held = Held(*refs[:FETCHED])
    (
        cells, found, sender, picked, pick_all, gather_far, gather_close, close_rows, edge_base,
        req_out, req_in, out_rows, in_rows,
        fetch_sem, cells_sem, sender_sem,
        halo_send, halo_recv, req_send, req_recv, row_send, row_recv,
        more_send, more_recv,
    ) = refs[FETCHED:]

    lat = lax.axis_index("lat")
    lon = lax.axis_index("lon")
    lat_rows, lon_cols = grid_hbm.shape[:2]

    def place(step_lat, step_lon, sign):
        return (
            (lat + sign * step_lat + LATS) & (LATS - 1),
            (lon + sign * step_lon + LONS) & (LONS - 1),
        )

    def for_all_others(act):
        for step_lon in range(1, LONS):
            act(0, step_lon)

        def band(step_lat, carry):
            for step_lon in range(LONS):
                act(step_lat, step_lon)
            return carry

        lax.fori_loop(1, LATS, band, 0)

    fetches = [
        pltpu.make_async_copy(hbm[n], held[n], fetch_sem.at[n]) for n in range(FETCHED)
    ]
    fetch = Held(*fetches)

    def ready(*copies):
        for copy in copies:
            copy.wait()

    for copy in fetches[:4]:
        copy.start()
    cells_copies = []
    for n in range(PIECES):
        rows = lat_rows // PIECES
        cells_copies.append(
            pltpu.make_async_copy(
                grid_hbm.at[pl.ds(n * rows, rows)],
                cells.at[pl.ds(HALO + n * rows, rows), pl.ds(HALO, lon_cols)],
                cells_sem.at[n],
            )
        )
    for copy in cells_copies:
        copy.start()

    barrier = pltpu.get_barrier_semaphore()
    for i in NEAR:
        pl.semaphore_signal(
            barrier, inc=1, device_id=place(i // LONS, i % LONS, 1), device_id_type=MESH
        )

    def greet(step_lat, step_lon):
        pl.semaphore_signal(
            barrier, inc=1, device_id=place(step_lat, step_lon, 1), device_id_type=MESH
        )

    for step_lat in (0, 1, LATS - 1):
        for step_lon in range(2, LONS - 1):
            greet(step_lat, step_lon)

    def greet_band(step_lat, carry):
        for step_lon in range(LONS):
            greet(step_lat, step_lon)
        return carry

    lax.fori_loop(2, LATS - 1, greet_band, 0)

    pl.semaphore_wait(barrier, PAIRS - 1)

    spans = {0: (0, lat_rows, HALO), -1: (0, HALO, HALO + lat_rows), 1: (lat_rows - HALO, HALO, 0)}
    spans_lon = {
        0: (0, lon_cols, HALO), -1: (0, HALO, HALO + lon_cols), 1: (lon_cols - HALO, HALO, 0)
    }
    halo = []
    for n, (a, b) in enumerate(DIRECTIONS):
        row0, rows, to_row = spans[a]
        col0, cols, to_col = spans_lon[b]
        halo.append(
            pltpu.make_async_remote_copy(
                src_ref=grid_hbm.at[pl.ds(row0, rows), pl.ds(col0, cols)],
                dst_ref=cells.at[pl.ds(to_row, rows), pl.ds(to_col, cols)],
                send_sem=halo_send.at[n],
                recv_sem=halo_recv.at[n],
                device_id=((lat + a + LATS) & (LATS - 1), (lon + b + LONS) & (LONS - 1)),
                device_id_type=MESH,
            )
        )
    groups = [
        [copy for copy, (a, _) in zip(halo, DIRECTIONS) if a == which] for which in (0, -1, 1)
    ]
    has_before = lat > 0
    has_after = lat < LATS - 1

    for copy in groups[0]:
        copy.start()

    @pl.when(has_before)
    def _():
        for copy in groups[1]:
            copy.start()

    @pl.when(has_after)
    def _():
        for copy in groups[2]:
            copy.start()

    for copy in fetches[4:FIRST]:
        copy.start()

    ready(fetch.g2m_sender, fetch.g2m_receiver, fetch.mesh_sender, fetch.mesh_receiver)
    cell = held.g2m_sender[...]
    cell_row = (cell >> 10) - lat * lat_rows + HALO
    cell_col = ((cell & (LONS * lon_cols - 1)) - lon * lon_cols + HALO) & (LONS * lon_cols - 1)
    found[0:1] = jnp.clip(cell_row, 0, cells.shape[0] - 1)
    found[1:2] = jnp.clip(cell_col, 0, cells.shape[1] - 1)
    sender_copy = pltpu.make_async_copy(found, sender, sender_sem)
    sender_copy.start()
    senders = held.mesh_sender[...]
    owner = senders >> 5
    row = senders & (NODES - 1)
    rel = ((((owner >> 4) - lat) & (LATS - 1)) << 4) | (((owner & 15) - lon) & (LONS - 1))
    owner2 = hot((iota((2 * PAIRS, EDGES), 0) >> 1) == rel)
    row2 = hot((iota((128, EDGES), 0) >> 1) == row)
    asked = mm_nt(owner2, row2)
    shape = (2 * PAIRS, 128)
    same = (iota(shape, 0) & 1) == (iota(shape, 1) & 1)
    asked = hot((asked > 0.5) & same & (iota(shape, 0) >= 2))
    req_out[...] = asked.reshape(PAIRS, 2, 128)
    req_in[0] = jnp.zeros((2, 128), BF)
    for t in range(STEPS):
        in_rows[t, 0] = jnp.zeros((2, D), BF)

    def ask(step_lat, step_lon):
        i = step_lat * LONS + step_lon
        pltpu.make_async_remote_copy(
            src_ref=req_out.at[i], dst_ref=req_in.at[i], send_sem=req_send, recv_sem=req_recv,
            device_id=place(step_lat, step_lon, 1), device_id_type=MESH,
        ).start()

    for_all_others(ask)

    for copy in fetches[FIRST:]:
        copy.start()

    grid_receivers = held.g2m_receiver[...]
    shape = (2 * NODES, 2 * GRID_EDGES)
    total_grid = hot(
        iota(shape, 0) == 2 * doubled_row(grid_receivers, GRID_EDGES) + (iota(shape, 1) & 1)
    )
    shape = (2 * GRID_EDGES, NODES)
    gather_grid_recv = hot(iota(shape, 1) == doubled_column(grid_receivers, GRID_EDGES))

    ready(fetch.mesh_latents, fetch.g2m_edges, fetch.enc_edge_w1, fetch.enc_edge_b1)
    latents = held.mesh_latents[...]
    shape = (2 * GRID_EDGES, GRID_EDGES)
    grid_edges = mm(hot(iota(shape, 1) == (iota(shape, 0) >> 1)), held.g2m_edges[...]).astype(BF)
    mesh_recv = mm(latents, held.enc_edge_w1[2]).astype(BF)
    grid_base = (
        mm(grid_edges, held.enc_edge_w1[0])
        + mm(gather_grid_recv, mesh_recv)
        + held.enc_edge_b1[...]
    )
    shape = (2 * NODES, NODES)
    state = mm(hot(iota(shape, 1) == (iota(shape, 0) >> 1)), latents).astype(BF)

    ready(fetch.embed_w1, fetch.embed_b1, fetch.embed_w2, fetch.embed_gain)
    ready(fetch.enc_edge_w2, fetch.enc_edge_gain)
    ready(fetch.enc_node_w1, fetch.enc_node_b1, fetch.enc_node_w2, fetch.enc_node_gain)
    enc_node_base = mm(state, held.enc_node_w1[0]) + held.enc_node_b1[...]

    sender_copy.wait()
    for copy in cells_copies:
        copy.wait()
    for copy in groups[0]:
        copy.wait_recv()

    @pl.when(has_after)
    def _():
        for copy in groups[1]:
            copy.wait_recv()

    @pl.when(has_before)
    def _():
        for copy in groups[2]:
            copy.wait_recv()

    def pick(k, carry):
        picked[k] = cells[sender[0, k], sender[1, k]]
        return carry

    lax.fori_loop(0, GRID_EDGES, pick, 0, unroll=32)

    pltpu.make_async_copy(
        req_in.at[pl.ds(1, PAIRS - 1)], req_in.at[pl.ds(1, PAIRS - 1)], req_recv
    ).wait()
    wanted = req_in[...].reshape(2 * PAIRS, 128)[:, : 2 * NODES]
    shape = (2 * NODES, 2 * NODES)
    before = hot(
        (iota(shape, 0) < iota(shape, 1)) & ((iota(shape, 0) & 1) == (iota(shape, 1) & 1))
    )
    place_of = mm(wanted, before).astype(BF)
    first = jnp.where(place_of.astype(F32) < 0.5, wanted.astype(F32), 0.0).astype(BF)
    shape = (2 * EXTRA * len(NEAR), 2 * PAIRS)
    line = iota(shape, 0)
    which = jnp.zeros_like(line)
    target = jnp.full_like(line, NEAR[0])
    for n in range(1, len(NEAR)):
        later = line >= 2 * EXTRA * n
        which = jnp.where(later, n, which)
        target = jnp.where(later, NEAR[n], target)
    choose = hot(iota(shape, 1) == 2 * target + (line & 1))
    kth = ((line >> 1) - EXTRA * which + 1).astype(F32)[:, : 2 * NODES]
    more = jnp.where(mm(choose, place_of) == kth, mm(choose, wanted), 0.0).astype(BF)
    pick_all[: 2 * PAIRS] = first
    pick_all[2 * PAIRS :] = more

    inputs = picked[...].reshape(2 * GRID_EDGES, picked.shape[2])
    bias = held.embed_b1[...]
    hidden = by_rows(lambda v: silu(v + bias).astype(BF), mm(inputs, held.embed_w1[...]))
    gain = held.embed_gain[...]
    latent = by_rows(lambda v: norm(v, gain).astype(BF), mm(hidden, held.embed_w2[...]))
    hidden = silu_rows(mm(latent, held.enc_edge_w1[1]), grid_base)
    new_edges = updated_rows(grid_edges, mm(hidden, held.enc_edge_w2[...]), held.enc_edge_gain[...])
    summed = mm(total_grid, new_edges).astype(BF)
    hidden = silu(enc_node_base + mm(summed, held.enc_node_w1[1])).astype(BF)
    update = norm(mm(hidden, held.enc_node_w2[...]), held.enc_node_gain[...])
    state = (state.astype(F32) + update).astype(BF)

    ready(fetch.proc_edge_w1)
    for t in range(STEPS):
        outgoing = mm(state, held.proc_edge_w1[t, 1]).astype(BF)
        out_rows[t] = mm(pick_all[...], outgoing).astype(BF).reshape(SLOTS, 2, D)

        for n, i in enumerate(NEAR):
            span = pl.ds(PAIRS + EXTRA * n, EXTRA)
            pltpu.make_async_remote_copy(
                src_ref=out_rows.at[t, span], dst_ref=in_rows.at[t, span],
                send_sem=more_send.at[t], recv_sem=more_recv.at[t],
                device_id=place(i // LONS, i % LONS, -1), device_id_type=MESH,
            ).start()

        def give(step_lat, step_lon, t=t):
            i = step_lat * LONS + step_lon
            pltpu.make_async_remote_copy(
                src_ref=out_rows.at[t, i], dst_ref=in_rows.at[t, i],
                send_sem=row_send.at[t], recv_sem=row_recv.at[t],
                device_id=place(step_lat, step_lon, -1), device_id_type=MESH,
            ).start()

        for_all_others(give)

        if t == 0:
            ready(fetch.proc_edge_b1, fetch.proc_edge_w2, fetch.proc_edge_gain)
            ready(fetch.proc_node_w1, fetch.proc_node_b1, fetch.proc_node_w2, fetch.proc_node_gain)
            owner1 = hot(iota((PAIRS, EDGES), 0) == rel)
            row1 = iota((NODES, EDGES), 0) == row
            needed = hot(mm_nt(hot(row1), owner1) > 0.5)
            below = hot(iota((NODES, NODES), 1) < iota((NODES, NODES), 0))
            order = mm(below, needed).astype(BF)
            rank = jnp.sum(jnp.where(row1, mm(order, owner1), 0.0), axis=0, keepdims=True).astype(I32)
            near = jnp.zeros_like(rel)
            for n, i in enumerate(NEAR):
                near = jnp.where(rel == i, n, near)
            nowhere = -PAIRS
            far = jnp.where((rank == 0) & (rel > 0), rel, nowhere)
            close = jnp.where(rank == 0, nowhere, 2 * NODES + EXTRA * near + rank - 1)
            close = jnp.where(rel == 0, NODES + row, close)
            receivers = held.mesh_receiver[...]
            shape = (2 * EDGES, EDGES)
            twice = hot(iota(shape, 1) == (iota(shape, 0) >> 1))
            columns = jnp.concatenate([far, close, receivers, jnp.zeros((5, EDGES), I32)], axis=0)
            columns = mm_nt(twice, columns.astype(F32).astype(BF)).astype(I32)
            shape = (2 * EDGES, 2 * PAIRS)
            gather_far[...] = hot(iota(shape, 1) == 2 * columns[:, 0:1] + (iota(shape, 0) & 1))
            shape = (2 * EDGES, CLOSE)
            lane = iota(shape, 1) - (iota(shape, 0) & 1)
            gather_close[...] = hot((lane == 2 * columns[:, 2:3]) | (lane == 2 * columns[:, 1:2]))
            shape = (2 * NODES, 2 * EDGES)
            total_mesh = hot(iota(shape, 0) == 2 * doubled_row(receivers, EDGES) + (iota(shape, 1) & 1))

            ready(fetch.mesh_edges)
            edge_state = mm(twice, held.mesh_edges[...]).astype(BF)

        close_rows[: 2 * NODES] = mm(state, held.proc_edge_w1[t, 2]).astype(BF)
        close_rows[2 * NODES : 4 * NODES] = outgoing
        node_base = mm(state, held.proc_node_w1[t, 0]) + held.proc_node_b1[t : t + 1]
        arrived = in_rows.at[t, pl.ds(PAIRS, SLOTS - PAIRS)]
        pltpu.make_async_copy(arrived, arrived, more_recv.at[t]).wait()
        close_rows[4 * NODES :] = in_rows[t, PAIRS:].reshape(2 * (SLOTS - PAIRS), D)
        edge_base[...] = (
            mm(edge_state, held.proc_edge_w1[t, 0])
            + mm(gather_close[...], close_rows[...])
            + held.proc_edge_b1[t : t + 1]
        )

        arrived = in_rows.at[t, pl.ds(1, PAIRS - 1)]
        pltpu.make_async_copy(arrived, arrived, row_recv.at[t]).wait()
        table = in_rows[t, :PAIRS].reshape(2 * PAIRS, D)
        gain = held.proc_edge_gain[t : t + 1]
        halves = []
        for span in (slice(0, EDGES), slice(EDGES, 2 * EDGES)):
            hidden = silu_rows(mm(gather_far[span], table), edge_base[span])
            halves.append(updated_rows(edge_state[span], mm(hidden, held.proc_edge_w2[t]), gain))
        edge_state = jnp.concatenate(halves, axis=0)
        summed = mm(total_mesh[:, :EDGES], halves[0]) + mm(total_mesh[:, EDGES:], halves[1])
        summed = summed.astype(BF)
        hidden = silu(node_base + mm(summed, held.proc_node_w1[t, 1])).astype(BF)
        update = norm(mm(hidden, held.proc_node_w2[t]), held.proc_node_gain[t : t + 1])
        state = (state.astype(F32) + update).astype(BF)

    out_ref[...] = state

    for copy in groups[0]:
        copy.wait_send()

    @pl.when(has_before)
    def _():
        for copy in groups[1]:
            copy.wait_send()

    @pl.when(has_after)
    def _():
        for copy in groups[2]:
            copy.wait_send()

    asked_all = req_out.at[pl.ds(1, PAIRS - 1)]
    pltpu.make_async_copy(asked_all, asked_all, req_send).wait()
    for t in range(STEPS):
        sent = out_rows.at[t, pl.ds(1, PAIRS - 1)]
        pltpu.make_async_copy(sent, sent, row_send.at[t]).wait()
        sent = out_rows.at[t, pl.ds(PAIRS, SLOTS - PAIRS)]
        pltpu.make_async_copy(sent, sent, more_send.at[t]).wait()


def on_device(*args):
    given = Given(*args)
    lat_rows, lon_cols, batch, width = given.grid_inputs.shape

    def flat(row):
        return row.reshape(1, row.shape[0])

    wanted = Held(
        flat(given.g2m_sender),
        flat(given.g2m_receiver),
        flat(given.mesh_sender),
        flat(given.mesh_receiver),
        given.mesh_latents,
        given.g2m_edges,
        given.enc_edge_w1,
        flat(given.enc_edge_b1),
        given.embed_w1,
        flat(given.embed_b1),
        given.embed_w2,
        flat(given.embed_gain),
        given.enc_edge_w2,
        flat(given.enc_edge_gain),
        given.enc_node_w1,
        flat(given.enc_node_b1),
        given.enc_node_w2,
        flat(given.enc_node_gain),
        given.mesh_edges,
        given.proc_edge_w1,
        given.proc_edge_b1,
        given.proc_edge_w2,
        given.proc_edge_gain,
        given.proc_node_w1,
        given.proc_node_b1,
        given.proc_node_w2,
        given.proc_node_gain,
    )
    operands = [given.grid_inputs, *wanted]
    dma = pltpu.SemaphoreType.DMA
    scratch = [pltpu.VMEM(part.shape, part.dtype) for part in wanted]
    scratch += [
        pltpu.VMEM((lat_rows + 2 * HALO, lon_cols + 2 * HALO, batch, width), BF),
        pltpu.VMEM((2, GRID_EDGES), I32),
        pltpu.SMEM((2, GRID_EDGES), I32),
        pltpu.VMEM((GRID_EDGES, batch, width), BF),
        pltpu.VMEM((2 * SLOTS, 2 * NODES), BF),
        pltpu.VMEM((2 * EDGES, 2 * PAIRS), BF),
        pltpu.VMEM((2 * EDGES, CLOSE), BF),
        pltpu.VMEM((CLOSE, D), BF),
        pltpu.VMEM((2 * EDGES, D), F32),
        pltpu.VMEM((PAIRS, 2, 128), BF),
        pltpu.VMEM((PAIRS, 2, 128), BF),
        pltpu.VMEM((STEPS, SLOTS, 2, D), BF),
        pltpu.VMEM((STEPS, SLOTS, 2, D), BF),
        dma((FETCHED,)),
        dma((PIECES,)),
        dma,
        dma((len(DIRECTIONS),)),
        dma((len(DIRECTIONS),)),
        dma,
        dma,
        dma((STEPS,)),
        dma((STEPS,)),
        dma((STEPS,)),
        dma((STEPS,)),
    ]
    return pl.pallas_call(
        kernel,
        out_shape=jax.ShapeDtypeStruct((NODES * batch, D), BF),
        in_specs=[pl.BlockSpec(memory_space=pl.ANY)] * len(operands),
        out_specs=pl.BlockSpec(memory_space=pltpu.VMEM),
        scratch_shapes=scratch,
        cost_estimate=pl.CostEstimate(
            flops=4 * 10**9, bytes_accessed=15 * 10**6, transcendentals=10**6
        ),
        compiler_params=pltpu.CompilerParams(
            collective_id=0, has_side_effects=True, vmem_limit_bytes=64 * 2**20
        ),
    )(*operands).reshape(NODES, batch, D)


def solution(mesh):
    nodes = P(("lat", "lon"), None)
    edges = P(("lat", "lon"))
    split = [P("lat", "lon", None, None), nodes, nodes, edges, edges, nodes, edges, edges]
    split += [P()] * (len(Given._fields) - len(split))
    return jax.shard_map(
        on_device,
        mesh=mesh,
        in_specs=tuple(split),
        out_specs=P(("lat", "lon"), None, None),
        check_vma=False,
    )
```

```python
from typing import Any, NamedTuple

import jax
import jax.numpy as jnp
from jax import lax
from jax.experimental import pallas as pl
from jax.experimental.pallas import tpu as pltpu
from jax.sharding import PartitionSpec as P

BF = jnp.bfloat16
F32 = jnp.float32
I32 = jnp.int32
MESH = pl.DeviceIdType.MESH

BATCH = 2
D = 512
HALO = 2
STEPS = 2
CHUNK = 64
LATS = 8
LONS = 16
PAIRS = LATS * LONS
NODES = 32
GRID_EDGES = 128
EDGES = 256
NEAR = (1, 15, 16, 17, 31, 112, 113, 127)
EXTRA = 3
SLOTS = PAIRS + EXTRA * len(NEAR)
CLOSE = 4 * NODES + 2 * EXTRA * len(NEAR)
DIRECTIONS = tuple((a, b) for a in (0, -1, 1) for b in (0, -1, 1) if (a, b) != (0, 0))


class Given(NamedTuple):
    grid_inputs: Any
    mesh_latents: Any
    g2m_edges: Any
    g2m_sender: Any
    g2m_receiver: Any
    mesh_edges: Any
    mesh_sender: Any
    mesh_receiver: Any
    embed_w1: Any
    embed_b1: Any
    embed_w2: Any
    embed_gain: Any
    enc_edge_w1: Any
    enc_edge_b1: Any
    enc_edge_w2: Any
    enc_edge_gain: Any
    enc_node_w1: Any
    enc_node_b1: Any
    enc_node_w2: Any
    enc_node_gain: Any
    proc_edge_w1: Any
    proc_edge_b1: Any
    proc_edge_w2: Any
    proc_edge_gain: Any
    proc_node_w1: Any
    proc_node_b1: Any
    proc_node_w2: Any
    proc_node_gain: Any


class Held(NamedTuple):
    g2m_sender: Any
    g2m_receiver: Any
    mesh_sender: Any
    mesh_receiver: Any
    mesh_latents: Any
    g2m_edges: Any
    enc_edge_w1: Any
    enc_edge_b1: Any
    embed_w1: Any
    embed_b1: Any
    embed_w2: Any
    embed_gain: Any
    enc_edge_w2: Any
    enc_edge_gain: Any
    enc_node_w1: Any
    enc_node_b1: Any
    enc_node_w2: Any
    enc_node_gain: Any
    mesh_edges: Any
    proc_edge_w1: Any
    proc_edge_b1: Any
    proc_edge_w2: Any
    proc_edge_gain: Any
    proc_node_w1: Any
    proc_node_b1: Any
    proc_node_w2: Any
    proc_node_gain: Any


FETCHED = len(Held._fields)
BASE = 8
PIECES = 4


def mm(a, b):
    return jnp.dot(a, b, preferred_element_type=F32)


def mm_nt(a, b):
    return lax.dot_general(a, b, (((1,), (1,)), ((), ())), preferred_element_type=F32)


def iota(shape, dim):
    return lax.broadcasted_iota(I32, shape, dim)


def hot(mask):
    return jnp.where(mask, 1.0, 0.0).astype(BF)


def silu(v):
    half = 0.5 * v
    return half + half * jnp.tanh(half)


def norm(v, gain):
    count = 1.0 / v.shape[-1]
    mean = jnp.sum(v, axis=-1, keepdims=True) * count
    square = jnp.sum(v * v, axis=-1, keepdims=True) * count
    scale = lax.rsqrt(jnp.maximum(square - mean * mean, 0.0) + 1e-05)
    return (v - mean) * scale * gain


def by_rows(act, *arrays):
    count = arrays[0].shape[0]
    pieces = [act(*(v[c : c + CHUNK] for v in arrays)) for c in range(0, count, CHUNK)]
    return jnp.concatenate(pieces, axis=0)


def silu_rows(*terms):
    return by_rows(lambda *parts: silu(sum(parts[1:], parts[0])).astype(BF), *terms)


def updated_rows(rows, v, gain):
    return by_rows(lambda r, part: (r.astype(F32) + norm(part, gain)).astype(BF), rows, v)


def doubled_column(row, count):
    shape = (2 * count, count)
    spread = jnp.where(iota(shape, 1) == (iota(shape, 0) >> 1), row.astype(F32), 0.0)
    return jnp.sum(spread, axis=1, keepdims=True).astype(I32)


def doubled_row(row, count):
    shape = (count, 2 * count)
    return mm(row.astype(F32).astype(BF), hot((iota(shape, 1) >> 1) == iota(shape, 0))).astype(I32)


def kernel(*refs):
    grid_hbm = refs[0]
    hbm = refs[1 : 1 + FETCHED]
    out_ref = refs[1 + FETCHED]
    refs = refs[2 + FETCHED :]
    held = Held(*refs[:FETCHED])
    (
        cells, found, sender, picked, pick_all, gather_far, gather_close, close_rows, edge_base,
        req_out, req_in, out_rows, in_rows,
        fetch_sem, cells_sem, sender_sem,
        halo_send, halo_recv, req_send, req_recv, row_send, row_recv,
        more_send, more_recv,
    ) = refs[FETCHED:]

    lat = lax.axis_index("lat")
    lon = lax.axis_index("lon")
    lat_rows, lon_cols = grid_hbm.shape[:2]

    def place(step_lat, step_lon, sign):
        return (
            (lat + sign * step_lat + LATS) & (LATS - 1),
            (lon + sign * step_lon + LONS) & (LONS - 1),
        )

    def for_all_others(act):
        for step_lon in range(1, LONS):
            act(0, step_lon)

        def band(step_lat, carry):
            for step_lon in range(LONS):
                act(step_lat, step_lon)
            return carry

        lax.fori_loop(1, LATS, band, 0)

    fetches = [
        pltpu.make_async_copy(hbm[n], held[n], fetch_sem.at[n]) for n in range(FETCHED)
    ]
    fetch = Held(*fetches)

    def ready(*copies):
        for copy in copies:
            copy.wait()

    for copy in fetches[:4]:
        copy.start()
    cells_copies = []
    for n in range(PIECES):
        rows = lat_rows // PIECES
        cells_copies.append(
            pltpu.make_async_copy(
                grid_hbm.at[pl.ds(n * rows, rows)],
                cells.at[pl.ds(HALO + n * rows, rows), pl.ds(HALO, lon_cols)],
                cells_sem.at[n],
            )
        )
    for copy in cells_copies:
        copy.start()

    barrier = pltpu.get_barrier_semaphore()
    for i in NEAR:
        pl.semaphore_signal(
            barrier, inc=1, device_id=place(i // LONS, i % LONS, 1), device_id_type=MESH
        )

    def greet(step_lat, step_lon):
        pl.semaphore_signal(
            barrier, inc=1, device_id=place(step_lat, step_lon, 1), device_id_type=MESH
        )

    for step_lat in (0, 1, LATS - 1):
        for step_lon in range(2, LONS - 1):
            greet(step_lat, step_lon)

    def greet_band(step_lat, carry):
        for step_lon in range(LONS):
            greet(step_lat, step_lon)
        return carry

    lax.fori_loop(2, LATS - 1, greet_band, 0)

    pl.semaphore_wait(barrier, PAIRS - 1)

    spans = {0: (0, lat_rows, HALO), -1: (0, HALO, HALO + lat_rows), 1: (lat_rows - HALO, HALO, 0)}
    spans_lon = {
        0: (0, lon_cols, HALO), -1: (0, HALO, HALO + lon_cols), 1: (lon_cols - HALO, HALO, 0)
    }
    halo = []
    for n, (a, b) in enumerate(DIRECTIONS):
        row0, rows, to_row = spans[a]
        col0, cols, to_col = spans_lon[b]
        halo.append(
            pltpu.make_async_remote_copy(
                src_ref=grid_hbm.at[pl.ds(row0, rows), pl.ds(col0, cols)],
                dst_ref=cells.at[pl.ds(to_row, rows), pl.ds(to_col, cols)],
                send_sem=halo_send.at[n],
                recv_sem=halo_recv.at[n],
                device_id=((lat + a + LATS) & (LATS - 1), (lon + b + LONS) & (LONS - 1)),
                device_id_type=MESH,
            )
        )
    groups = [
        [copy for copy, (a, _) in zip(halo, DIRECTIONS) if a == which] for which in (0, -1, 1)
    ]
    has_before = lat > 0
    has_after = lat < LATS - 1

    for copy in groups[0]:
        copy.start()

    @pl.when(has_before)
    def _():
        for copy in groups[1]:
            copy.start()

    @pl.when(has_after)
    def _():
        for copy in groups[2]:
            copy.start()

    for copy in fetches[4:BASE]:
        copy.start()

    ready(fetch.g2m_sender, fetch.g2m_receiver, fetch.mesh_sender, fetch.mesh_receiver)
    cell = held.g2m_sender[...]
    cell_row = (cell >> 10) - lat * lat_rows + HALO
    cell_col = ((cell & (LONS * lon_cols - 1)) - lon * lon_cols + HALO) & (LONS * lon_cols - 1)
    found[0:1] = jnp.clip(cell_row, 0, cells.shape[0] - 1)
    found[1:2] = jnp.clip(cell_col, 0, cells.shape[1] - 1)
    sender_copy = pltpu.make_async_copy(found, sender, sender_sem)
    sender_copy.start()
    senders = held.mesh_sender[...]
    owner = senders >> 5
    row = senders & (NODES - 1)
    rel = ((((owner >> 4) - lat) & (LATS - 1)) << 4) | (((owner & 15) - lon) & (LONS - 1))
    owner2 = hot((iota((2 * PAIRS, EDGES), 0) >> 1) == rel)
    row2 = hot((iota((128, EDGES), 0) >> 1) == row)
    asked = mm_nt(owner2, row2)
    shape = (2 * PAIRS, 128)
    same = (iota(shape, 0) & 1) == (iota(shape, 1) & 1)
    asked = hot((asked > 0.5) & same & (iota(shape, 0) >= 2))
    req_out[...] = asked.reshape(PAIRS, 2, 128)
    req_in[0] = jnp.zeros((2, 128), BF)
    for t in range(STEPS):
        in_rows[t, 0] = jnp.zeros((2, D), BF)

    def ask(step_lat, step_lon):
        i = step_lat * LONS + step_lon
        pltpu.make_async_remote_copy(
            src_ref=req_out.at[i], dst_ref=req_in.at[i], send_sem=req_send, recv_sem=req_recv,
            device_id=place(step_lat, step_lon, 1), device_id_type=MESH,
        ).start()

    for_all_others(ask)

    for copy in fetches[BASE:]:
        copy.start()

    grid_receivers = held.g2m_receiver[...]
    shape = (2 * NODES, 2 * GRID_EDGES)
    total_grid = hot(
        iota(shape, 0) == 2 * doubled_row(grid_receivers, GRID_EDGES) + (iota(shape, 1) & 1)
    )
    shape = (2 * GRID_EDGES, NODES)
    gather_grid_recv = hot(iota(shape, 1) == doubled_column(grid_receivers, GRID_EDGES))

    ready(fetch.mesh_latents, fetch.g2m_edges, fetch.enc_edge_w1, fetch.enc_edge_b1)
    latents = held.mesh_latents[...]
    shape = (2 * GRID_EDGES, GRID_EDGES)
    grid_edges = mm(hot(iota(shape, 1) == (iota(shape, 0) >> 1)), held.g2m_edges[...]).astype(BF)
    mesh_recv = mm(latents, held.enc_edge_w1[2]).astype(BF)
    grid_base = (
        mm(grid_edges, held.enc_edge_w1[0])
        + mm(gather_grid_recv, mesh_recv)
        + held.enc_edge_b1[...]
    )
    shape = (2 * NODES, NODES)
    state = mm(hot(iota(shape, 1) == (iota(shape, 0) >> 1)), latents).astype(BF)

    ready(fetch.embed_w1, fetch.embed_b1, fetch.embed_w2, fetch.embed_gain)
    ready(fetch.enc_edge_w2, fetch.enc_edge_gain)
    ready(fetch.enc_node_w1, fetch.enc_node_b1, fetch.enc_node_w2, fetch.enc_node_gain)
    enc_node_base = mm(state, held.enc_node_w1[0]) + held.enc_node_b1[...]

    sender_copy.wait()
    for copy in cells_copies:
        copy.wait()
    for copy in groups[0]:
        copy.wait_recv()

    @pl.when(has_after)
    def _():
        for copy in groups[1]:
            copy.wait_recv()

    @pl.when(has_before)
    def _():
        for copy in groups[2]:
            copy.wait_recv()

    def pick(k, carry):
        picked[k] = cells[sender[0, k], sender[1, k]]
        return carry

    lax.fori_loop(0, GRID_EDGES, pick, 0, unroll=32)

    inputs = picked[...].reshape(2 * GRID_EDGES, picked.shape[2])
    bias = held.embed_b1[...]
    hidden = by_rows(lambda v: silu(v + bias).astype(BF), mm(inputs, held.embed_w1[...]))
    gain = held.embed_gain[...]
    latent = by_rows(lambda v: norm(v, gain).astype(BF), mm(hidden, held.embed_w2[...]))
    hidden = silu_rows(mm(latent, held.enc_edge_w1[1]), grid_base)
    new_edges = updated_rows(grid_edges, mm(hidden, held.enc_edge_w2[...]), held.enc_edge_gain[...])
    summed = mm(total_grid, new_edges).astype(BF)
    pltpu.make_async_copy(
        req_in.at[pl.ds(1, PAIRS - 1)], req_in.at[pl.ds(1, PAIRS - 1)], req_recv
    ).wait()
    wanted = req_in[...].reshape(2 * PAIRS, 128)[:, : 2 * NODES]
    shape = (2 * NODES, 2 * NODES)
    before = hot(
        (iota(shape, 0) < iota(shape, 1)) & ((iota(shape, 0) & 1) == (iota(shape, 1) & 1))
    )
    place_of = mm(wanted, before).astype(BF)
    first = jnp.where(place_of.astype(F32) < 0.5, wanted.astype(F32), 0.0).astype(BF)
    shape = (2 * EXTRA * len(NEAR), 2 * PAIRS)
    line = iota(shape, 0)
    which = jnp.zeros_like(line)
    target = jnp.full_like(line, NEAR[0])
    for n in range(1, len(NEAR)):
        later = line >= 2 * EXTRA * n
        which = jnp.where(later, n, which)
        target = jnp.where(later, NEAR[n], target)
    choose = hot(iota(shape, 1) == 2 * target + (line & 1))
    kth = ((line >> 1) - EXTRA * which + 1).astype(F32)[:, : 2 * NODES]
    more = jnp.where(mm(choose, place_of) == kth, mm(choose, wanted), 0.0).astype(BF)
    pick_all[: 2 * PAIRS] = first
    pick_all[2 * PAIRS :] = more

    hidden = silu(enc_node_base + mm(summed, held.enc_node_w1[1])).astype(BF)
    update = norm(mm(hidden, held.enc_node_w2[...]), held.enc_node_gain[...])
    state = (state.astype(F32) + update).astype(BF)

    ready(fetch.proc_edge_w1)
    for t in range(STEPS):
        outgoing = mm(state, held.proc_edge_w1[t, 1]).astype(BF)
        out_rows[t] = mm(pick_all[...], outgoing).astype(BF).reshape(SLOTS, 2, D)

        for n, i in enumerate(NEAR):
            span = pl.ds(PAIRS + EXTRA * n, EXTRA)
            pltpu.make_async_remote_copy(
                src_ref=out_rows.at[t, span], dst_ref=in_rows.at[t, span],
                send_sem=more_send.at[t], recv_sem=more_recv.at[t],
                device_id=place(i // LONS, i % LONS, -1), device_id_type=MESH,
            ).start()

        def give(step_lat, step_lon, t=t):
            i = step_lat * LONS + step_lon
            pltpu.make_async_remote_copy(
                src_ref=out_rows.at[t, i], dst_ref=in_rows.at[t, i],
                send_sem=row_send.at[t], recv_sem=row_recv.at[t],
                device_id=place(step_lat, step_lon, -1), device_id_type=MESH,
            ).start()

        for_all_others(give)

        if t == 0:
            ready(fetch.proc_edge_b1, fetch.proc_edge_w2, fetch.proc_edge_gain)
            ready(fetch.proc_node_w1, fetch.proc_node_b1, fetch.proc_node_w2, fetch.proc_node_gain)
            owner1 = hot(iota((PAIRS, EDGES), 0) == rel)
            row1 = iota((NODES, EDGES), 0) == row
            needed = hot(mm_nt(hot(row1), owner1) > 0.5)
            below = hot(iota((NODES, NODES), 1) < iota((NODES, NODES), 0))
            order = mm(below, needed).astype(BF)
            rank = jnp.sum(jnp.where(row1, mm(order, owner1), 0.0), axis=0, keepdims=True).astype(I32)
            near = jnp.zeros_like(rel)
            for n, i in enumerate(NEAR):
                near = jnp.where(rel == i, n, near)
            nowhere = -PAIRS
            far = jnp.where((rank == 0) & (rel > 0), rel, nowhere)
            close = jnp.where(rank == 0, nowhere, 2 * NODES + EXTRA * near + rank - 1)
            close = jnp.where(rel == 0, NODES + row, close)
            shape = (2 * EDGES, 2 * PAIRS)
            gather_far[...] = hot(
                iota(shape, 1) == 2 * doubled_column(far, EDGES) + (iota(shape, 0) & 1)
            )
            receivers = held.mesh_receiver[...]
            shape = (2 * EDGES, CLOSE)
            lane = iota(shape, 1) - (iota(shape, 0) & 1)
            gather_close[...] = hot(
                (lane == 2 * doubled_column(receivers, EDGES))
                | (lane == 2 * doubled_column(close, EDGES))
            )
            shape = (2 * NODES, 2 * EDGES)
            total_mesh = hot(iota(shape, 0) == 2 * doubled_row(receivers, EDGES) + (iota(shape, 1) & 1))

            ready(fetch.mesh_edges)
            shape = (2 * EDGES, EDGES)
            edge_state = mm(
                hot(iota(shape, 1) == (iota(shape, 0) >> 1)), held.mesh_edges[...]
            ).astype(BF)

        close_rows[: 2 * NODES] = mm(state, held.proc_edge_w1[t, 2]).astype(BF)
        close_rows[2 * NODES : 4 * NODES] = outgoing
        node_base = mm(state, held.proc_node_w1[t, 0]) + held.proc_node_b1[t : t + 1]
        arrived = in_rows.at[t, pl.ds(PAIRS, SLOTS - PAIRS)]
        pltpu.make_async_copy(arrived, arrived, more_recv.at[t]).wait()
        close_rows[4 * NODES :] = in_rows[t, PAIRS:].reshape(2 * (SLOTS - PAIRS), D)
        edge_base[...] = (
            mm(edge_state, held.proc_edge_w1[t, 0])
            + mm(gather_close[...], close_rows[...])
            + held.proc_edge_b1[t : t + 1]
        )

        arrived = in_rows.at[t, pl.ds(1, PAIRS - 1)]
        pltpu.make_async_copy(arrived, arrived, row_recv.at[t]).wait()
        table = in_rows[t, :PAIRS].reshape(2 * PAIRS, D)
        gain = held.proc_edge_gain[t : t + 1]
        halves = []
        for span in (slice(0, EDGES), slice(EDGES, 2 * EDGES)):
            hidden = silu_rows(mm(gather_far[span], table), edge_base[span])
            halves.append(updated_rows(edge_state[span], mm(hidden, held.proc_edge_w2[t]), gain))
        edge_state = jnp.concatenate(halves, axis=0)
        summed = mm(total_mesh[:, :EDGES], halves[0]) + mm(total_mesh[:, EDGES:], halves[1])
        summed = summed.astype(BF)
        hidden = silu(node_base + mm(summed, held.proc_node_w1[t, 1])).astype(BF)
        update = norm(mm(hidden, held.proc_node_w2[t]), held.proc_node_gain[t : t + 1])
        state = (state.astype(F32) + update).astype(BF)

    out_ref[...] = state

    for copy in groups[0]:
        copy.wait_send()

    @pl.when(has_before)
    def _():
        for copy in groups[1]:
            copy.wait_send()

    @pl.when(has_after)
    def _():
        for copy in groups[2]:
            copy.wait_send()

    asked_all = req_out.at[pl.ds(1, PAIRS - 1)]
    pltpu.make_async_copy(asked_all, asked_all, req_send).wait()
    for t in range(STEPS):
        sent = out_rows.at[t, pl.ds(1, PAIRS - 1)]
        pltpu.make_async_copy(sent, sent, row_send.at[t]).wait()
        sent = out_rows.at[t, pl.ds(PAIRS, SLOTS - PAIRS)]
        pltpu.make_async_copy(sent, sent, more_send.at[t]).wait()


def on_device(*args):
    given = Given(*args)
    lat_rows, lon_cols, batch, width = given.grid_inputs.shape

    def flat(row):
        return row.reshape(1, row.shape[0])

    wanted = Held(
        flat(given.g2m_sender),
        flat(given.g2m_receiver),
        flat(given.mesh_sender),
        flat(given.mesh_receiver),
        given.mesh_latents,
        given.g2m_edges,
        given.enc_edge_w1,
        flat(given.enc_edge_b1),
        given.embed_w1,
        flat(given.embed_b1),
        given.embed_w2,
        flat(given.embed_gain),
        given.enc_edge_w2,
        flat(given.enc_edge_gain),
        given.enc_node_w1,
        flat(given.enc_node_b1),
        given.enc_node_w2,
        flat(given.enc_node_gain),
        given.mesh_edges,
        given.proc_edge_w1,
        given.proc_edge_b1,
        given.proc_edge_w2,
        given.proc_edge_gain,
        given.proc_node_w1,
        given.proc_node_b1,
        given.proc_node_w2,
        given.proc_node_gain,
    )
    operands = [given.grid_inputs, *wanted]
    dma = pltpu.SemaphoreType.DMA
    scratch = [pltpu.VMEM(part.shape, part.dtype) for part in wanted]
    scratch += [
        pltpu.VMEM((lat_rows + 2 * HALO, lon_cols + 2 * HALO, batch, width), BF),
        pltpu.VMEM((2, GRID_EDGES), I32),
        pltpu.SMEM((2, GRID_EDGES), I32),
        pltpu.VMEM((GRID_EDGES, batch, width), BF),
        pltpu.VMEM((2 * SLOTS, 2 * NODES), BF),
        pltpu.VMEM((2 * EDGES, 2 * PAIRS), BF),
        pltpu.VMEM((2 * EDGES, CLOSE), BF),
        pltpu.VMEM((CLOSE, D), BF),
        pltpu.VMEM((2 * EDGES, D), F32),
        pltpu.VMEM((PAIRS, 2, 128), BF),
        pltpu.VMEM((PAIRS, 2, 128), BF),
        pltpu.VMEM((STEPS, SLOTS, 2, D), BF),
        pltpu.VMEM((STEPS, SLOTS, 2, D), BF),
        dma((FETCHED,)),
        dma((PIECES,)),
        dma,
        dma((len(DIRECTIONS),)),
        dma((len(DIRECTIONS),)),
        dma,
        dma,
        dma((STEPS,)),
        dma((STEPS,)),
        dma((STEPS,)),
        dma((STEPS,)),
    ]
    return pl.pallas_call(
        kernel,
        out_shape=jax.ShapeDtypeStruct((NODES * batch, D), BF),
        in_specs=[pl.BlockSpec(memory_space=pl.ANY)] * len(operands),
        out_specs=pl.BlockSpec(memory_space=pltpu.VMEM),
        scratch_shapes=scratch,
        cost_estimate=pl.CostEstimate(
            flops=4 * 10**9, bytes_accessed=15 * 10**6, transcendentals=10**6
        ),
        compiler_params=pltpu.CompilerParams(
            collective_id=0, has_side_effects=True, vmem_limit_bytes=64 * 2**20
        ),
    )(*operands).reshape(NODES, batch, D)


def solution(mesh):
    nodes = P(("lat", "lon"), None)
    edges = P(("lat", "lon"))
    split = [P("lat", "lon", None, None), nodes, nodes, edges, edges, nodes, edges, edges]
    split += [P()] * (len(Given._fields) - len(split))
    return jax.shard_map(
        on_device,
        mesh=mesh,
        in_specs=tuple(split),
        out_specs=P(("lat", "lon"), None, None),
        check_vma=False,
    )
```

```python
from typing import Any, NamedTuple

import jax
import jax.numpy as jnp
from jax import lax
from jax.experimental import pallas as pl
from jax.experimental.pallas import tpu as pltpu
from jax.sharding import PartitionSpec as P

BF = jnp.bfloat16
F32 = jnp.float32
I32 = jnp.int32
MESH = pl.DeviceIdType.MESH

BATCH = 2
D = 512
HALO = 2
STEPS = 2
CHUNK = 64
LATS = 8
LONS = 16
PAIRS = LATS * LONS
NODES = 32
GRID_EDGES = 128
EDGES = 256
NEAR = (1, 15, 16, 17, 31, 112, 113, 127)
EXTRA = 3
SLOTS = PAIRS + EXTRA * len(NEAR)
CLOSE = 4 * NODES + 2 * EXTRA * len(NEAR)
DIRECTIONS = tuple((a, b) for a in (0, -1, 1) for b in (0, -1, 1) if (a, b) != (0, 0))


class Given(NamedTuple):
    grid_inputs: Any
    mesh_latents: Any
    g2m_edges: Any
    g2m_sender: Any
    g2m_receiver: Any
    mesh_edges: Any
    mesh_sender: Any
    mesh_receiver: Any
    embed_w1: Any
    embed_b1: Any
    embed_w2: Any
    embed_gain: Any
    enc_edge_w1: Any
    enc_edge_b1: Any
    enc_edge_w2: Any
    enc_edge_gain: Any
    enc_node_w1: Any
    enc_node_b1: Any
    enc_node_w2: Any
    enc_node_gain: Any
    proc_edge_w1: Any
    proc_edge_b1: Any
    proc_edge_w2: Any
    proc_edge_gain: Any
    proc_node_w1: Any
    proc_node_b1: Any
    proc_node_w2: Any
    proc_node_gain: Any


class Held(NamedTuple):
    g2m_sender: Any
    g2m_receiver: Any
    mesh_sender: Any
    mesh_receiver: Any
    mesh_latents: Any
    g2m_edges: Any
    enc_edge_w1: Any
    enc_edge_b1: Any
    embed_w1: Any
    embed_b1: Any
    embed_w2: Any
    embed_gain: Any
    enc_edge_w2: Any
    enc_edge_gain: Any
    enc_node_w1: Any
    enc_node_b1: Any
    enc_node_w2: Any
    enc_node_gain: Any
    mesh_edges: Any
    proc_edge_w1: Any
    proc_edge_b1: Any
    proc_edge_w2: Any
    proc_edge_gain: Any
    proc_node_w1: Any
    proc_node_b1: Any
    proc_node_w2: Any
    proc_node_gain: Any


FETCHED = len(Held._fields)
BASE = 8
PIECES = 4


def mm(a, b):
    return jnp.dot(a, b, preferred_element_type=F32)


def mm_nt(a, b):
    return lax.dot_general(a, b, (((1,), (1,)), ((), ())), preferred_element_type=F32)


def iota(shape, dim):
    return lax.broadcasted_iota(I32, shape, dim)


def hot(mask):
    return jnp.where(mask, 1.0, 0.0).astype(BF)


def silu(v):
    half = 0.5 * v
    return half + half * jnp.tanh(half)


def norm(v, gain):
    count = 1.0 / v.shape[-1]
    mean = jnp.sum(v, axis=-1, keepdims=True) * count
    square = jnp.sum(v * v, axis=-1, keepdims=True) * count
    scale = lax.rsqrt(jnp.maximum(square - mean * mean, 0.0) + 1e-05)
    return (v - mean) * scale * gain


def by_rows(act, *arrays):
    count = arrays[0].shape[0]
    pieces = [act(*(v[c : c + CHUNK] for v in arrays)) for c in range(0, count, CHUNK)]
    return jnp.concatenate(pieces, axis=0)


def silu_rows(*terms):
    return by_rows(lambda *parts: silu(sum(parts[1:], parts[0])).astype(BF), *terms)


def updated_rows(rows, v, gain):
    return by_rows(lambda r, part: (r.astype(F32) + norm(part, gain)).astype(BF), rows, v)


def doubled_column(row, count):
    shape = (2 * count, count)
    spread = jnp.where(iota(shape, 1) == (iota(shape, 0) >> 1), row.astype(F32), 0.0)
    return jnp.sum(spread, axis=1, keepdims=True).astype(I32)


def doubled_row(row, count):
    shape = (count, 2 * count)
    return mm(row.astype(F32).astype(BF), hot((iota(shape, 1) >> 1) == iota(shape, 0))).astype(I32)


def kernel(*refs):
    grid_hbm = refs[0]
    hbm = refs[1 : 1 + FETCHED]
    out_ref = refs[1 + FETCHED]
    refs = refs[2 + FETCHED :]
    held = Held(*refs[:FETCHED])
    (
        cells, found, sender, picked, asked_row, asked_place, own_rows, gather_far, gather_close, close_rows, edge_base,
        req_out, req_in, out_rows, in_rows,
        fetch_sem, cells_sem, sender_sem,
        halo_send, halo_recv, req_send, req_recv, row_send, row_recv,
        more_send, more_recv, asked_sem,
    ) = refs[FETCHED:]

    lat = lax.axis_index("lat")
    lon = lax.axis_index("lon")
    lat_rows, lon_cols = grid_hbm.shape[:2]

    def place(step_lat, step_lon, sign):
        return (
            (lat + sign * step_lat + LATS) & (LATS - 1),
            (lon + sign * step_lon + LONS) & (LONS - 1),
        )

    def for_all_others(act):
        for step_lon in range(1, LONS):
            act(0, step_lon)

        def band(step_lat, carry):
            for step_lon in range(LONS):
                act(step_lat, step_lon)
            return carry

        lax.fori_loop(1, LATS, band, 0)

    fetches = [
        pltpu.make_async_copy(hbm[n], held[n], fetch_sem.at[n]) for n in range(FETCHED)
    ]
    fetch = Held(*fetches)

    def ready(*copies):
        for copy in copies:
            copy.wait()

    for copy in fetches[:4]:
        copy.start()
    cells_copies = []
    for n in range(PIECES):
        rows = lat_rows // PIECES
        cells_copies.append(
            pltpu.make_async_copy(
                grid_hbm.at[pl.ds(n * rows, rows)],
                cells.at[pl.ds(HALO + n * rows, rows), pl.ds(HALO, lon_cols)],
                cells_sem.at[n],
            )
        )
    for copy in cells_copies:
        copy.start()

    barrier = pltpu.get_barrier_semaphore()
    for i in NEAR:
        pl.semaphore_signal(
            barrier, inc=1, device_id=place(i // LONS, i % LONS, 1), device_id_type=MESH
        )

    def greet(step_lat, step_lon):
        pl.semaphore_signal(
            barrier, inc=1, device_id=place(step_lat, step_lon, 1), device_id_type=MESH
        )

    for step_lat in (0, 1, LATS - 1):
        for step_lon in range(2, LONS - 1):
            greet(step_lat, step_lon)

    def greet_band(step_lat, carry):
        for step_lon in range(LONS):
            greet(step_lat, step_lon)
        return carry

    lax.fori_loop(2, LATS - 1, greet_band, 0)

    pl.semaphore_wait(barrier, PAIRS - 1)

    spans = {0: (0, lat_rows, HALO), -1: (0, HALO, HALO + lat_rows), 1: (lat_rows - HALO, HALO, 0)}
    spans_lon = {
        0: (0, lon_cols, HALO), -1: (0, HALO, HALO + lon_cols), 1: (lon_cols - HALO, HALO, 0)
    }
    halo = []
    for n, (a, b) in enumerate(DIRECTIONS):
        row0, rows, to_row = spans[a]
        col0, cols, to_col = spans_lon[b]
        halo.append(
            pltpu.make_async_remote_copy(
                src_ref=grid_hbm.at[pl.ds(row0, rows), pl.ds(col0, cols)],
                dst_ref=cells.at[pl.ds(to_row, rows), pl.ds(to_col, cols)],
                send_sem=halo_send.at[n],
                recv_sem=halo_recv.at[n],
                device_id=((lat + a + LATS) & (LATS - 1), (lon + b + LONS) & (LONS - 1)),
                device_id_type=MESH,
            )
        )
    groups = [
        [copy for copy, (a, _) in zip(halo, DIRECTIONS) if a == which] for which in (0, -1, 1)
    ]
    has_before = lat > 0
    has_after = lat < LATS - 1

    for copy in groups[0]:
        copy.start()

    @pl.when(has_before)
    def _():
        for copy in groups[1]:
            copy.start()

    @pl.when(has_after)
    def _():
        for copy in groups[2]:
            copy.start()

    for copy in fetches[4:BASE]:
        copy.start()

    ready(fetch.g2m_sender, fetch.g2m_receiver, fetch.mesh_sender, fetch.mesh_receiver)
    cell = held.g2m_sender[...]
    cell_row = (cell >> 10) - lat * lat_rows + HALO
    cell_col = ((cell & (LONS * lon_cols - 1)) - lon * lon_cols + HALO) & (LONS * lon_cols - 1)
    found[0:1] = jnp.clip(cell_row, 0, cells.shape[0] - 1)
    found[1:2] = jnp.clip(cell_col, 0, cells.shape[1] - 1)
    sender_copy = pltpu.make_async_copy(found, sender, sender_sem)
    sender_copy.start()
    senders = held.mesh_sender[...]
    owner = senders >> 5
    row = senders & (NODES - 1)
    rel = ((((owner >> 4) - lat) & (LATS - 1)) << 4) | (((owner & 15) - lon) & (LONS - 1))
    owner2 = hot((iota((2 * PAIRS, EDGES), 0) >> 1) == rel)
    row2 = hot((iota((128, EDGES), 0) >> 1) == row)
    asked = mm_nt(owner2, row2)
    shape = (2 * PAIRS, 128)
    same = (iota(shape, 0) & 1) == (iota(shape, 1) & 1)
    asked = hot((asked > 0.5) & same & (iota(shape, 0) >= 2))
    req_out[...] = asked.reshape(PAIRS, 2, 128)
    req_in[0] = jnp.zeros((2, 128), BF)
    for t in range(STEPS):
        in_rows[t, 0] = jnp.zeros((2, D), BF)

    def ask(step_lat, step_lon):
        i = step_lat * LONS + step_lon
        pltpu.make_async_remote_copy(
            src_ref=req_out.at[i], dst_ref=req_in.at[i], send_sem=req_send, recv_sem=req_recv,
            device_id=place(step_lat, step_lon, 1), device_id_type=MESH,
        ).start()

    for_all_others(ask)

    for copy in fetches[BASE:]:
        copy.start()

    grid_receivers = held.g2m_receiver[...]
    shape = (2 * NODES, 2 * GRID_EDGES)
    total_grid = hot(
        iota(shape, 0) == 2 * doubled_row(grid_receivers, GRID_EDGES) + (iota(shape, 1) & 1)
    )
    shape = (2 * GRID_EDGES, NODES)
    gather_grid_recv = hot(iota(shape, 1) == doubled_column(grid_receivers, GRID_EDGES))

    ready(fetch.mesh_latents, fetch.g2m_edges, fetch.enc_edge_w1, fetch.enc_edge_b1)
    latents = held.mesh_latents[...]
    shape = (2 * GRID_EDGES, GRID_EDGES)
    grid_edges = mm(hot(iota(shape, 1) == (iota(shape, 0) >> 1)), held.g2m_edges[...]).astype(BF)
    mesh_recv = mm(latents, held.enc_edge_w1[2]).astype(BF)
    grid_base = (
        mm(grid_edges, held.enc_edge_w1[0])
        + mm(gather_grid_recv, mesh_recv)
        + held.enc_edge_b1[...]
    )
    shape = (2 * NODES, NODES)
    state = mm(hot(iota(shape, 1) == (iota(shape, 0) >> 1)), latents).astype(BF)

    ready(fetch.embed_w1, fetch.embed_b1, fetch.embed_w2, fetch.embed_gain)
    ready(fetch.enc_edge_w2, fetch.enc_edge_gain)
    ready(fetch.enc_node_w1, fetch.enc_node_b1, fetch.enc_node_w2, fetch.enc_node_gain)
    enc_node_base = mm(state, held.enc_node_w1[0]) + held.enc_node_b1[...]

    sender_copy.wait()
    for copy in cells_copies:
        copy.wait()
    for copy in groups[0]:
        copy.wait_recv()

    @pl.when(has_after)
    def _():
        for copy in groups[1]:
            copy.wait_recv()

    @pl.when(has_before)
    def _():
        for copy in groups[2]:
            copy.wait_recv()

    def pick(k, carry):
        picked[k] = cells[sender[0, k], sender[1, k]]
        return carry

    lax.fori_loop(0, GRID_EDGES, pick, 0, unroll=32)

    inputs = picked[...].reshape(2 * GRID_EDGES, picked.shape[2])
    bias = held.embed_b1[...]
    hidden = by_rows(lambda v: silu(v + bias).astype(BF), mm(inputs, held.embed_w1[...]))
    gain = held.embed_gain[...]
    latent = by_rows(lambda v: norm(v, gain).astype(BF), mm(hidden, held.embed_w2[...]))
    hidden = silu_rows(mm(latent, held.enc_edge_w1[1]), grid_base)
    pltpu.make_async_copy(
        req_in.at[pl.ds(1, PAIRS - 1)], req_in.at[pl.ds(1, PAIRS - 1)], req_recv
    ).wait()
    wanted = req_in[...].reshape(2 * PAIRS, 128)[:, : 2 * NODES]
    shape = (2 * NODES, 2 * NODES)
    before = hot(
        (iota(shape, 0) < iota(shape, 1)) & ((iota(shape, 0) & 1) == (iota(shape, 1) & 1))
    )
    place_of = mm(wanted, before).astype(BF)
    first = jnp.where(place_of.astype(F32) < 0.5, wanted.astype(F32), 0.0).astype(BF)
    shape = (2 * EXTRA * len(NEAR), 2 * PAIRS)
    line = iota(shape, 0)
    which = jnp.zeros_like(line)
    target = jnp.full_like(line, NEAR[0])
    for n in range(1, len(NEAR)):
        later = line >= 2 * EXTRA * n
        which = jnp.where(later, n, which)
        target = jnp.where(later, NEAR[n], target)
    choose = hot(iota(shape, 1) == 2 * target + (line & 1))
    kth = ((line >> 1) - EXTRA * which + 1).astype(F32)[:, : 2 * NODES]
    more = jnp.where(mm(choose, place_of) == kth, mm(choose, wanted), 0.0).astype(BF)
    lanes = iota((8, 2 * NODES), 1).astype(F32).astype(BF)
    chosen = mm_nt(lanes, jnp.concatenate([first, more], axis=0)).astype(I32)
    asked_row[...] = (chosen[0:1] >> 1) & (NODES - 1)
    asked_copy = pltpu.make_async_copy(asked_row, asked_place, asked_sem)
    asked_copy.start()

    new_edges = updated_rows(grid_edges, mm(hidden, held.enc_edge_w2[...]), held.enc_edge_gain[...])
    summed = mm(total_grid, new_edges).astype(BF)
    hidden = silu(enc_node_base + mm(summed, held.enc_node_w1[1])).astype(BF)
    update = norm(mm(hidden, held.enc_node_w2[...]), held.enc_node_gain[...])
    state = (state.astype(F32) + update).astype(BF)

    ready(fetch.proc_edge_w1)
    asked_copy.wait()
    for t in range(STEPS):
        outgoing = mm(state, held.proc_edge_w1[t, 1]).astype(BF)
        own_rows[...] = outgoing.reshape(NODES, 2, D)

        def fill(i, t=t):
            out_rows[t, i] = own_rows[asked_place[0, 2 * i]]

        for i in range(PAIRS, SLOTS):
            fill(i)
        for n, i in enumerate(NEAR):
            span = pl.ds(PAIRS + EXTRA * n, EXTRA)
            pltpu.make_async_remote_copy(
                src_ref=out_rows.at[t, span], dst_ref=in_rows.at[t, span],
                send_sem=more_send.at[t], recv_sem=more_recv.at[t],
                device_id=place(i // LONS, i % LONS, -1), device_id_type=MESH,
            ).start()

        def give(step_lat, step_lon, t=t):
            i = step_lat * LONS + step_lon
            pltpu.make_async_remote_copy(
                src_ref=out_rows.at[t, i], dst_ref=in_rows.at[t, i],
                send_sem=row_send.at[t], recv_sem=row_recv.at[t],
                device_id=place(step_lat, step_lon, -1), device_id_type=MESH,
            ).start()

        for step_lon in range(1, LONS):
            fill(step_lon)
        for step_lon in range(1, LONS):
            give(0, step_lon)

        def give_band(step_lat, carry, fill=fill, give=give):
            for step_lon in range(LONS):
                fill(step_lat * LONS + step_lon)
            for step_lon in range(LONS):
                give(step_lat, step_lon)
            return carry

        lax.fori_loop(1, LATS, give_band, 0)

        if t == 0:
            ready(fetch.proc_edge_b1, fetch.proc_edge_w2, fetch.proc_edge_gain)
            ready(fetch.proc_node_w1, fetch.proc_node_b1, fetch.proc_node_w2, fetch.proc_node_gain)
            owner1 = hot(iota((PAIRS, EDGES), 0) == rel)
            row1 = iota((NODES, EDGES), 0) == row
            needed = hot(mm_nt(hot(row1), owner1) > 0.5)
            below = hot(iota((NODES, NODES), 1) < iota((NODES, NODES), 0))
            order = mm(below, needed).astype(BF)
            rank = jnp.sum(jnp.where(row1, mm(order, owner1), 0.0), axis=0, keepdims=True).astype(I32)
            near = jnp.zeros_like(rel)
            for n, i in enumerate(NEAR):
                near = jnp.where(rel == i, n, near)
            nowhere = -PAIRS
            far = jnp.where((rank == 0) & (rel > 0), rel, nowhere)
            close = jnp.where(rank == 0, nowhere, 2 * NODES + EXTRA * near + rank - 1)
            close = jnp.where(rel == 0, NODES + row, close)
            shape = (2 * EDGES, 2 * PAIRS)
            gather_far[...] = hot(
                iota(shape, 1) == 2 * doubled_column(far, EDGES) + (iota(shape, 0) & 1)
            )
            receivers = held.mesh_receiver[...]
            shape = (2 * EDGES, CLOSE)
            lane = iota(shape, 1) - (iota(shape, 0) & 1)
            gather_close[...] = hot(
                (lane == 2 * doubled_column(receivers, EDGES))
                | (lane == 2 * doubled_column(close, EDGES))
            )
            shape = (2 * NODES, 2 * EDGES)
            total_mesh = hot(iota(shape, 0) == 2 * doubled_row(receivers, EDGES) + (iota(shape, 1) & 1))

            ready(fetch.mesh_edges)
            shape = (2 * EDGES, EDGES)
            edge_state = mm(
                hot(iota(shape, 1) == (iota(shape, 0) >> 1)), held.mesh_edges[...]
            ).astype(BF)

        close_rows[: 2 * NODES] = mm(state, held.proc_edge_w1[t, 2]).astype(BF)
        close_rows[2 * NODES : 4 * NODES] = outgoing
        node_base = mm(state, held.proc_node_w1[t, 0]) + held.proc_node_b1[t : t + 1]
        arrived = in_rows.at[t, pl.ds(PAIRS, SLOTS - PAIRS)]
        pltpu.make_async_copy(arrived, arrived, more_recv.at[t]).wait()
        close_rows[4 * NODES :] = in_rows[t, PAIRS:].reshape(2 * (SLOTS - PAIRS), D)
        edge_base[...] = (
            mm(edge_state, held.proc_edge_w1[t, 0])
            + mm(gather_close[...], close_rows[...])
            + held.proc_edge_b1[t : t + 1]
        )

        arrived = in_rows.at[t, pl.ds(1, PAIRS - 1)]
        pltpu.make_async_copy(arrived, arrived, row_recv.at[t]).wait()
        table = in_rows[t, :PAIRS].reshape(2 * PAIRS, D)
        gain = held.proc_edge_gain[t : t + 1]
        halves = []
        for span in (slice(0, EDGES), slice(EDGES, 2 * EDGES)):
            hidden = silu_rows(mm(gather_far[span], table), edge_base[span])
            halves.append(updated_rows(edge_state[span], mm(hidden, held.proc_edge_w2[t]), gain))
        edge_state = jnp.concatenate(halves, axis=0)
        summed = mm(total_mesh[:, :EDGES], halves[0]) + mm(total_mesh[:, EDGES:], halves[1])
        summed = summed.astype(BF)
        hidden = silu(node_base + mm(summed, held.proc_node_w1[t, 1])).astype(BF)
        update = norm(mm(hidden, held.proc_node_w2[t]), held.proc_node_gain[t : t + 1])
        state = (state.astype(F32) + update).astype(BF)

    out_ref[...] = state

    for copy in groups[0]:
        copy.wait_send()

    @pl.when(has_before)
    def _():
        for copy in groups[1]:
            copy.wait_send()

    @pl.when(has_after)
    def _():
        for copy in groups[2]:
            copy.wait_send()

    asked_all = req_out.at[pl.ds(1, PAIRS - 1)]
    pltpu.make_async_copy(asked_all, asked_all, req_send).wait()
    for t in range(STEPS):
        sent = out_rows.at[t, pl.ds(1, PAIRS - 1)]
        pltpu.make_async_copy(sent, sent, row_send.at[t]).wait()
        sent = out_rows.at[t, pl.ds(PAIRS, SLOTS - PAIRS)]
        pltpu.make_async_copy(sent, sent, more_send.at[t]).wait()


def on_device(*args):
    given = Given(*args)
    lat_rows, lon_cols, batch, width = given.grid_inputs.shape

    def flat(row):
        return row.reshape(1, row.shape[0])

    wanted = Held(
        flat(given.g2m_sender),
        flat(given.g2m_receiver),
        flat(given.mesh_sender),
        flat(given.mesh_receiver),
        given.mesh_latents,
        given.g2m_edges,
        given.enc_edge_w1,
        flat(given.enc_edge_b1),
        given.embed_w1,
        flat(given.embed_b1),
        given.embed_w2,
        flat(given.embed_gain),
        given.enc_edge_w2,
        flat(given.enc_edge_gain),
        given.enc_node_w1,
        flat(given.enc_node_b1),
        given.enc_node_w2,
        flat(given.enc_node_gain),
        given.mesh_edges,
        given.proc_edge_w1,
        given.proc_edge_b1,
        given.proc_edge_w2,
        given.proc_edge_gain,
        given.proc_node_w1,
        given.proc_node_b1,
        given.proc_node_w2,
        given.proc_node_gain,
    )
    operands = [given.grid_inputs, *wanted]
    dma = pltpu.SemaphoreType.DMA
    scratch = [pltpu.VMEM(part.shape, part.dtype) for part in wanted]
    scratch += [
        pltpu.VMEM((lat_rows + 2 * HALO, lon_cols + 2 * HALO, batch, width), BF),
        pltpu.VMEM((2, GRID_EDGES), I32),
        pltpu.SMEM((2, GRID_EDGES), I32),
        pltpu.VMEM((GRID_EDGES, batch, width), BF),
        pltpu.VMEM((1, 2 * SLOTS), I32),
        pltpu.SMEM((1, 2 * SLOTS), I32),
        pltpu.VMEM((NODES, 2, D), BF),
        pltpu.VMEM((2 * EDGES, 2 * PAIRS), BF),
        pltpu.VMEM((2 * EDGES, CLOSE), BF),
        pltpu.VMEM((CLOSE, D), BF),
        pltpu.VMEM((2 * EDGES, D), F32),
        pltpu.VMEM((PAIRS, 2, 128), BF),
        pltpu.VMEM((PAIRS, 2, 128), BF),
        pltpu.VMEM((STEPS, SLOTS, 2, D), BF),
        pltpu.VMEM((STEPS, SLOTS, 2, D), BF),
        dma((FETCHED,)),
        dma((PIECES,)),
        dma,
        dma((len(DIRECTIONS),)),
        dma((len(DIRECTIONS),)),
        dma,
        dma,
        dma((STEPS,)),
        dma((STEPS,)),
        dma((STEPS,)),
        dma((STEPS,)),
        dma,
    ]
    return pl.pallas_call(
        kernel,
        out_shape=jax.ShapeDtypeStruct((NODES * batch, D), BF),
        in_specs=[pl.BlockSpec(memory_space=pl.ANY)] * len(operands),
        out_specs=pl.BlockSpec(memory_space=pltpu.VMEM),
        scratch_shapes=scratch,
        cost_estimate=pl.CostEstimate(
            flops=4 * 10**9, bytes_accessed=15 * 10**6, transcendentals=10**6
        ),
        compiler_params=pltpu.CompilerParams(
            collective_id=0, has_side_effects=True, vmem_limit_bytes=64 * 2**20
        ),
    )(*operands).reshape(NODES, batch, D)


def solution(mesh):
    nodes = P(("lat", "lon"), None)
    edges = P(("lat", "lon"))
    split = [P("lat", "lon", None, None), nodes, nodes, edges, edges, nodes, edges, edges]
    split += [P()] * (len(Given._fields) - len(split))
    return jax.shard_map(
        on_device,
        mesh=mesh,
        in_specs=tuple(split),
        out_specs=P(("lat", "lon"), None, None),
        check_vma=False,
    )
```

```python
from typing import Any, NamedTuple

import jax
import jax.numpy as jnp
from jax import lax
from jax.experimental import pallas as pl
from jax.experimental.pallas import tpu as pltpu
from jax.sharding import PartitionSpec as P

BF = jnp.bfloat16
F32 = jnp.float32
I32 = jnp.int32
MESH = pl.DeviceIdType.MESH

BATCH = 2
D = 512
HALO = 2
STEPS = 2
CHUNK = 64
LATS = 8
LONS = 16
PAIRS = LATS * LONS
NODES = 32
GRID_EDGES = 128
EDGES = 256
NEAR = (1, 15, 16, 17, 31, 112, 113, 127)
EXTRA = 3
SLOTS = PAIRS + EXTRA * len(NEAR)
CLOSE = 4 * NODES + 2 * EXTRA * len(NEAR)
DIRECTIONS = tuple((a, b) for a in (0, -1, 1) for b in (0, -1, 1) if (a, b) != (0, 0))


class Given(NamedTuple):
    grid_inputs: Any
    mesh_latents: Any
    g2m_edges: Any
    g2m_sender: Any
    g2m_receiver: Any
    mesh_edges: Any
    mesh_sender: Any
    mesh_receiver: Any
    embed_w1: Any
    embed_b1: Any
    embed_w2: Any
    embed_gain: Any
    enc_edge_w1: Any
    enc_edge_b1: Any
    enc_edge_w2: Any
    enc_edge_gain: Any
    enc_node_w1: Any
    enc_node_b1: Any
    enc_node_w2: Any
    enc_node_gain: Any
    proc_edge_w1: Any
    proc_edge_b1: Any
    proc_edge_w2: Any
    proc_edge_gain: Any
    proc_node_w1: Any
    proc_node_b1: Any
    proc_node_w2: Any
    proc_node_gain: Any


class Held(NamedTuple):
    g2m_sender: Any
    g2m_receiver: Any
    mesh_sender: Any
    mesh_receiver: Any
    mesh_latents: Any
    g2m_edges: Any
    enc_edge_w1: Any
    enc_edge_b1: Any
    embed_w1: Any
    embed_b1: Any
    embed_w2: Any
    embed_gain: Any
    enc_edge_w2: Any
    enc_edge_gain: Any
    enc_node_w1: Any
    enc_node_b1: Any
    enc_node_w2: Any
    enc_node_gain: Any
    mesh_edges: Any
    proc_edge_w1: Any
    proc_edge_b1: Any
    proc_edge_w2: Any
    proc_edge_gain: Any
    proc_node_w1: Any
    proc_node_b1: Any
    proc_node_w2: Any
    proc_node_gain: Any


FETCHED = len(Held._fields)
BASE = 8
PIECES = 4


def mm(a, b):
    return jnp.dot(a, b, preferred_element_type=F32)


def mm_nt(a, b):
    return lax.dot_general(a, b, (((1,), (1,)), ((), ())), preferred_element_type=F32)


def iota(shape, dim):
    return lax.broadcasted_iota(I32, shape, dim)


def hot(mask):
    return jnp.where(mask, 1.0, 0.0).astype(BF)


def silu(v):
    half = 0.5 * v
    return half + half * jnp.tanh(half)


def norm(v, gain):
    count = 1.0 / v.shape[-1]
    mean = jnp.sum(v, axis=-1, keepdims=True) * count
    square = jnp.sum(v * v, axis=-1, keepdims=True) * count
    scale = lax.rsqrt(jnp.maximum(square - mean * mean, 0.0) + 1e-05)
    return (v - mean) * scale * gain


def by_rows(act, *arrays):
    count = arrays[0].shape[0]
    pieces = [act(*(v[c : c + CHUNK] for v in arrays)) for c in range(0, count, CHUNK)]
    return jnp.concatenate(pieces, axis=0)


def silu_rows(*terms):
    return by_rows(lambda *parts: silu(sum(parts[1:], parts[0])).astype(BF), *terms)


def updated_rows(rows, v, gain):
    return by_rows(lambda r, part: (r.astype(F32) + norm(part, gain)).astype(BF), rows, v)


def doubled_column(row, count):
    shape = (2 * count, count)
    spread = jnp.where(iota(shape, 1) == (iota(shape, 0) >> 1), row.astype(F32), 0.0)
    return jnp.sum(spread, axis=1, keepdims=True).astype(I32)


def doubled_row(row, count):
    shape = (count, 2 * count)
    return mm(row.astype(F32).astype(BF), hot((iota(shape, 1) >> 1) == iota(shape, 0))).astype(I32)


def kernel(*refs):
    grid_hbm = refs[0]
    hbm = refs[1 : 1 + FETCHED]
    out_ref = refs[1 + FETCHED]
    refs = refs[2 + FETCHED :]
    held = Held(*refs[:FETCHED])
    (
        cells, found, sender, picked, asked_row, asked_place, own_rows, gather_far, gather_close, close_rows, edge_base,
        req_out, req_in, out_rows, in_rows,
        fetch_sem, cells_sem, sender_sem,
        halo_send, halo_recv, req_send, req_recv, row_send, row_recv,
        more_send, more_recv, asked_sem,
    ) = refs[FETCHED:]

    lat = lax.axis_index("lat")
    lon = lax.axis_index("lon")
    lat_rows, lon_cols = grid_hbm.shape[:2]

    def place(step_lat, step_lon, sign):
        return (
            (lat + sign * step_lat + LATS) & (LATS - 1),
            (lon + sign * step_lon + LONS) & (LONS - 1),
        )

    def for_all_others(act):
        for step_lon in range(1, LONS):
            act(0, step_lon)

        def band(step_lat, carry):
            for step_lon in range(LONS):
                act(step_lat, step_lon)
            return carry

        lax.fori_loop(1, LATS, band, 0)

    fetches = [
        pltpu.make_async_copy(hbm[n], held[n], fetch_sem.at[n]) for n in range(FETCHED)
    ]
    fetch = Held(*fetches)

    def ready(*copies):
        for copy in copies:
            copy.wait()

    for copy in fetches[:4]:
        copy.start()
    cells_copies = []
    for n in range(PIECES):
        rows = lat_rows // PIECES
        cells_copies.append(
            pltpu.make_async_copy(
                grid_hbm.at[pl.ds(n * rows, rows)],
                cells.at[pl.ds(HALO + n * rows, rows), pl.ds(HALO, lon_cols)],
                cells_sem.at[n],
            )
        )
    for copy in cells_copies:
        copy.start()

    barrier = pltpu.get_barrier_semaphore()
    for i in NEAR:
        pl.semaphore_signal(
            barrier, inc=1, device_id=place(i // LONS, i % LONS, 1), device_id_type=MESH
        )

    def greet(step_lat, step_lon):
        pl.semaphore_signal(
            barrier, inc=1, device_id=place(step_lat, step_lon, 1), device_id_type=MESH
        )

    for step_lat in (0, 1, LATS - 1):
        for step_lon in range(2, LONS - 1):
            greet(step_lat, step_lon)

    def greet_band(step_lat, carry):
        for step_lon in range(LONS):
            greet(step_lat, step_lon)
        return carry

    lax.fori_loop(2, LATS - 1, greet_band, 0)

    pl.semaphore_wait(barrier, PAIRS - 1)

    spans = {0: (0, lat_rows, HALO), -1: (0, HALO, HALO + lat_rows), 1: (lat_rows - HALO, HALO, 0)}
    spans_lon = {
        0: (0, lon_cols, HALO), -1: (0, HALO, HALO + lon_cols), 1: (lon_cols - HALO, HALO, 0)
    }
    halo = []
    for n, (a, b) in enumerate(DIRECTIONS):
        row0, rows, to_row = spans[a]
        col0, cols, to_col = spans_lon[b]
        halo.append(
            pltpu.make_async_remote_copy(
                src_ref=grid_hbm.at[pl.ds(row0, rows), pl.ds(col0, cols)],
                dst_ref=cells.at[pl.ds(to_row, rows), pl.ds(to_col, cols)],
                send_sem=halo_send.at[n],
                recv_sem=halo_recv.at[n],
                device_id=((lat + a + LATS) & (LATS - 1), (lon + b + LONS) & (LONS - 1)),
                device_id_type=MESH,
            )
        )
    groups = [
        [copy for copy, (a, _) in zip(halo, DIRECTIONS) if a == which] for which in (0, -1, 1)
    ]
    has_before = lat > 0
    has_after = lat < LATS - 1

    for copy in groups[0]:
        copy.start()

    @pl.when(has_before)
    def _():
        for copy in groups[1]:
            copy.start()

    @pl.when(has_after)
    def _():
        for copy in groups[2]:
            copy.start()

    for copy in fetches[4:BASE]:
        copy.start()

    ready(fetch.g2m_sender, fetch.g2m_receiver, fetch.mesh_sender, fetch.mesh_receiver)
    cell = held.g2m_sender[...]
    cell_row = (cell >> 10) - lat * lat_rows + HALO
    cell_col = ((cell & (LONS * lon_cols - 1)) - lon * lon_cols + HALO) & (LONS * lon_cols - 1)
    found[0:1] = jnp.clip(cell_row, 0, cells.shape[0] - 1)
    found[1:2] = jnp.clip(cell_col, 0, cells.shape[1] - 1)
    sender_copy = pltpu.make_async_copy(found, sender, sender_sem)
    sender_copy.start()
    senders = held.mesh_sender[...]
    owner = senders >> 5
    row = senders & (NODES - 1)
    rel = ((((owner >> 4) - lat) & (LATS - 1)) << 4) | (((owner & 15) - lon) & (LONS - 1))
    owner2 = hot((iota((2 * PAIRS, EDGES), 0) >> 1) == rel)
    row2 = hot((iota((128, EDGES), 0) >> 1) == row)
    asked = mm_nt(owner2, row2)
    shape = (2 * PAIRS, 128)
    same = (iota(shape, 0) & 1) == (iota(shape, 1) & 1)
    asked = hot((asked > 0.5) & same & (iota(shape, 0) >= 2))
    req_out[...] = asked.reshape(PAIRS, 2, 128)
    req_in[0] = jnp.zeros((2, 128), BF)
    for t in range(STEPS):
        in_rows[t, 0] = jnp.zeros((2, D), BF)

    def ask(step_lat, step_lon):
        i = step_lat * LONS + step_lon
        pltpu.make_async_remote_copy(
            src_ref=req_out.at[i], dst_ref=req_in.at[i], send_sem=req_send, recv_sem=req_recv,
            device_id=place(step_lat, step_lon, 1), device_id_type=MESH,
        ).start()

    for_all_others(ask)

    for copy in fetches[BASE:]:
        copy.start()

    grid_receivers = held.g2m_receiver[...]
    shape = (2 * NODES, 2 * GRID_EDGES)
    total_grid = hot(
        iota(shape, 0) == 2 * doubled_row(grid_receivers, GRID_EDGES) + (iota(shape, 1) & 1)
    )
    shape = (2 * GRID_EDGES, NODES)
    gather_grid_recv = hot(iota(shape, 1) == doubled_column(grid_receivers, GRID_EDGES))

    ready(fetch.mesh_latents, fetch.g2m_edges, fetch.enc_edge_w1, fetch.enc_edge_b1)
    latents = held.mesh_latents[...]
    shape = (2 * GRID_EDGES, GRID_EDGES)
    grid_edges = mm(hot(iota(shape, 1) == (iota(shape, 0) >> 1)), held.g2m_edges[...]).astype(BF)
    mesh_recv = mm(latents, held.enc_edge_w1[2]).astype(BF)
    grid_base = (
        mm(grid_edges, held.enc_edge_w1[0])
        + mm(gather_grid_recv, mesh_recv)
        + held.enc_edge_b1[...]
    )
    shape = (2 * NODES, NODES)
    state = mm(hot(iota(shape, 1) == (iota(shape, 0) >> 1)), latents).astype(BF)

    ready(fetch.embed_w1, fetch.embed_b1, fetch.embed_w2, fetch.embed_gain)
    ready(fetch.enc_edge_w2, fetch.enc_edge_gain)
    ready(fetch.enc_node_w1, fetch.enc_node_b1, fetch.enc_node_w2, fetch.enc_node_gain)
    enc_node_base = mm(state, held.enc_node_w1[0]) + held.enc_node_b1[...]

    sender_copy.wait()
    for copy in cells_copies:
        copy.wait()
    for copy in groups[0]:
        copy.wait_recv()

    @pl.when(has_after)
    def _():
        for copy in groups[1]:
            copy.wait_recv()

    @pl.when(has_before)
    def _():
        for copy in groups[2]:
            copy.wait_recv()

    def pick(k, carry):
        picked[k] = cells[sender[0, k], sender[1, k]]
        return carry

    lax.fori_loop(0, GRID_EDGES, pick, 0, unroll=32)

    inputs = picked[...].reshape(2 * GRID_EDGES, picked.shape[2])
    bias = held.embed_b1[...]
    hidden = by_rows(lambda v: silu(v + bias).astype(BF), mm(inputs, held.embed_w1[...]))
    gain = held.embed_gain[...]
    latent = by_rows(lambda v: norm(v, gain).astype(BF), mm(hidden, held.embed_w2[...]))
    hidden = silu_rows(mm(latent, held.enc_edge_w1[1]), grid_base)
    pltpu.make_async_copy(
        req_in.at[pl.ds(1, PAIRS - 1)], req_in.at[pl.ds(1, PAIRS - 1)], req_recv
    ).wait()
    wanted = req_in[...].reshape(2 * PAIRS, 128)[:, : 2 * NODES]
    shape = (2 * NODES, 2 * NODES)
    before = hot(
        (iota(shape, 0) < iota(shape, 1)) & ((iota(shape, 0) & 1) == (iota(shape, 1) & 1))
    )
    place_of = mm(wanted, before).astype(BF)
    first = jnp.where(place_of.astype(F32) < 0.5, wanted.astype(F32), 0.0).astype(BF)
    shape = (2 * EXTRA * len(NEAR), 2 * PAIRS)
    line = iota(shape, 0)
    which = jnp.zeros_like(line)
    target = jnp.full_like(line, NEAR[0])
    for n in range(1, len(NEAR)):
        later = line >= 2 * EXTRA * n
        which = jnp.where(later, n, which)
        target = jnp.where(later, NEAR[n], target)
    choose = hot(iota(shape, 1) == 2 * target + (line & 1))
    kth = ((line >> 1) - EXTRA * which + 1).astype(F32)[:, : 2 * NODES]
    more = jnp.where(mm(choose, place_of) == kth, mm(choose, wanted), 0.0).astype(BF)
    lanes = iota((8, 2 * NODES), 1).astype(F32).astype(BF)
    chosen = mm_nt(lanes, jnp.concatenate([first, more], axis=0)).astype(I32)
    asked_row[...] = (chosen[0:1] >> 1) & (NODES - 1)
    asked_copy = pltpu.make_async_copy(asked_row, asked_place, asked_sem)
    asked_copy.start()

    new_edges = updated_rows(grid_edges, mm(hidden, held.enc_edge_w2[...]), held.enc_edge_gain[...])
    summed = mm(total_grid, new_edges).astype(BF)
    hidden = silu(enc_node_base + mm(summed, held.enc_node_w1[1])).astype(BF)
    update = norm(mm(hidden, held.enc_node_w2[...]), held.enc_node_gain[...])
    state = (state.astype(F32) + update).astype(BF)

    ready(fetch.proc_edge_w1)
    asked_copy.wait()
    for t in range(STEPS):
        outgoing = mm(state, held.proc_edge_w1[t, 1]).astype(BF)
        own_rows[...] = outgoing.reshape(NODES, 2, D)

        def fill(i, t=t):
            out_rows[t, i] = own_rows[asked_place[0, 2 * i]]

        for i in range(PAIRS, SLOTS):
            fill(i)
        for n, i in enumerate(NEAR):
            span = pl.ds(PAIRS + EXTRA * n, EXTRA)
            pltpu.make_async_remote_copy(
                src_ref=out_rows.at[t, span], dst_ref=in_rows.at[t, span],
                send_sem=more_send.at[t], recv_sem=more_recv.at[t],
                device_id=place(i // LONS, i % LONS, -1), device_id_type=MESH,
            ).start()

        def give(step_lat, step_lon, t=t):
            i = step_lat * LONS + step_lon
            pltpu.make_async_remote_copy(
                src_ref=out_rows.at[t, i], dst_ref=in_rows.at[t, i],
                send_sem=row_send.at[t], recv_sem=row_recv.at[t],
                device_id=place(step_lat, step_lon, -1), device_id_type=MESH,
            ).start()

        for step_lon in range(1, LONS):
            fill(step_lon)
        for step_lon in range(1, LONS):
            give(0, step_lon)

        def give_band(step_lat, carry, fill=fill, give=give):
            for step_lon in range(LONS):
                fill(step_lat * LONS + step_lon)
            for step_lon in range(LONS):
                give(step_lat, step_lon)
            return carry

        lax.fori_loop(1, LATS, give_band, 0)

        if t == 0:
            ready(fetch.proc_edge_b1, fetch.proc_edge_w2, fetch.proc_edge_gain)
            ready(fetch.proc_node_w1, fetch.proc_node_b1, fetch.proc_node_w2, fetch.proc_node_gain)
            owner1 = hot(iota((PAIRS, EDGES), 0) == rel)
            row1 = iota((NODES, EDGES), 0) == row
            needed = hot(mm_nt(hot(row1), owner1) > 0.5)
            below = hot(iota((NODES, NODES), 1) < iota((NODES, NODES), 0))
            order = mm(below, needed).astype(BF)
            rank = jnp.sum(jnp.where(row1, mm(order, owner1), 0.0), axis=0, keepdims=True).astype(I32)
            near = jnp.zeros_like(rel)
            for n, i in enumerate(NEAR):
                near = jnp.where(rel == i, n, near)
            nowhere = -PAIRS
            far = jnp.where((rank == 0) & (rel > 0), rel, nowhere)
            close = jnp.where(rank == 0, nowhere, 2 * NODES + EXTRA * near + rank - 1)
            close = jnp.where(rel == 0, NODES + row, close)
            receivers = held.mesh_receiver[...]
            shape = (2 * EDGES, EDGES)
            twice = hot(iota(shape, 1) == (iota(shape, 0) >> 1))
            columns = jnp.concatenate([far, close, receivers, jnp.zeros((5, EDGES), I32)], axis=0)
            columns = mm_nt(twice, columns.astype(F32).astype(BF)).astype(I32)
            shape = (2 * EDGES, 2 * PAIRS)
            gather_far[...] = hot(iota(shape, 1) == 2 * columns[:, 0:1] + (iota(shape, 0) & 1))
            shape = (2 * EDGES, CLOSE)
            lane = iota(shape, 1) - (iota(shape, 0) & 1)
            gather_close[...] = hot((lane == 2 * columns[:, 2:3]) | (lane == 2 * columns[:, 1:2]))
            shape = (2 * NODES, 2 * EDGES)
            total_mesh = hot(iota(shape, 0) == 2 * doubled_row(receivers, EDGES) + (iota(shape, 1) & 1))

            ready(fetch.mesh_edges)
            edge_state = mm(twice, held.mesh_edges[...]).astype(BF)

        close_rows[: 2 * NODES] = mm(state, held.proc_edge_w1[t, 2]).astype(BF)
        close_rows[2 * NODES : 4 * NODES] = outgoing
        node_base = mm(state, held.proc_node_w1[t, 0]) + held.proc_node_b1[t : t + 1]
        arrived = in_rows.at[t, pl.ds(PAIRS, SLOTS - PAIRS)]
        pltpu.make_async_copy(arrived, arrived, more_recv.at[t]).wait()
        close_rows[4 * NODES :] = in_rows[t, PAIRS:].reshape(2 * (SLOTS - PAIRS), D)
        edge_base[...] = (
            mm(edge_state, held.proc_edge_w1[t, 0])
            + mm(gather_close[...], close_rows[...])
            + held.proc_edge_b1[t : t + 1]
        )

        if t == 0:
            for copy in groups[0]:
                copy.wait_send()

            @pl.when(has_before)
            def _():
                for copy in groups[1]:
                    copy.wait_send()

            @pl.when(has_after)
            def _():
                for copy in groups[2]:
                    copy.wait_send()

            asked_all = req_out.at[pl.ds(1, PAIRS - 1)]
            pltpu.make_async_copy(asked_all, asked_all, req_send).wait()
        sent = out_rows.at[t, pl.ds(PAIRS, SLOTS - PAIRS)]
        pltpu.make_async_copy(sent, sent, more_send.at[t]).wait()
        sent = out_rows.at[t, pl.ds(1, PAIRS - 1)]
        pltpu.make_async_copy(sent, sent, row_send.at[t]).wait()
        arrived = in_rows.at[t, pl.ds(1, PAIRS - 1)]
        pltpu.make_async_copy(arrived, arrived, row_recv.at[t]).wait()
        table = in_rows[t, :PAIRS].reshape(2 * PAIRS, D)
        gain = held.proc_edge_gain[t : t + 1]
        halves = []
        for span in (slice(0, EDGES), slice(EDGES, 2 * EDGES)):
            hidden = silu_rows(mm(gather_far[span], table), edge_base[span])
            halves.append(updated_rows(edge_state[span], mm(hidden, held.proc_edge_w2[t]), gain))
        edge_state = jnp.concatenate(halves, axis=0)
        summed = mm(total_mesh[:, :EDGES], halves[0]) + mm(total_mesh[:, EDGES:], halves[1])
        summed = summed.astype(BF)
        hidden = silu(node_base + mm(summed, held.proc_node_w1[t, 1])).astype(BF)
        update = norm(mm(hidden, held.proc_node_w2[t]), held.proc_node_gain[t : t + 1])
        state = (state.astype(F32) + update).astype(BF)

    out_ref[...] = state


def on_device(*args):
    given = Given(*args)
    lat_rows, lon_cols, batch, width = given.grid_inputs.shape

    def flat(row):
        return row.reshape(1, row.shape[0])

    wanted = Held(
        flat(given.g2m_sender),
        flat(given.g2m_receiver),
        flat(given.mesh_sender),
        flat(given.mesh_receiver),
        given.mesh_latents,
        given.g2m_edges,
        given.enc_edge_w1,
        flat(given.enc_edge_b1),
        given.embed_w1,
        flat(given.embed_b1),
        given.embed_w2,
        flat(given.embed_gain),
        given.enc_edge_w2,
        flat(given.enc_edge_gain),
        given.enc_node_w1,
        flat(given.enc_node_b1),
        given.enc_node_w2,
        flat(given.enc_node_gain),
        given.mesh_edges,
        given.proc_edge_w1,
        given.proc_edge_b1,
        given.proc_edge_w2,
        given.proc_edge_gain,
        given.proc_node_w1,
        given.proc_node_b1,
        given.proc_node_w2,
        given.proc_node_gain,
    )
    operands = [given.grid_inputs, *wanted]
    dma = pltpu.SemaphoreType.DMA
    scratch = [pltpu.VMEM(part.shape, part.dtype) for part in wanted]
    scratch += [
        pltpu.VMEM((lat_rows + 2 * HALO, lon_cols + 2 * HALO, batch, width), BF),
        pltpu.VMEM((2, GRID_EDGES), I32),
        pltpu.SMEM((2, GRID_EDGES), I32),
        pltpu.VMEM((GRID_EDGES, batch, width), BF),
        pltpu.VMEM((1, 2 * SLOTS), I32),
        pltpu.SMEM((1, 2 * SLOTS), I32),
        pltpu.VMEM((NODES, 2, D), BF),
        pltpu.VMEM((2 * EDGES, 2 * PAIRS), BF),
        pltpu.VMEM((2 * EDGES, CLOSE), BF),
        pltpu.VMEM((CLOSE, D), BF),
        pltpu.VMEM((2 * EDGES, D), F32),
        pltpu.VMEM((PAIRS, 2, 128), BF),
        pltpu.VMEM((PAIRS, 2, 128), BF),
        pltpu.VMEM((STEPS, SLOTS, 2, D), BF),
        pltpu.VMEM((STEPS, SLOTS, 2, D), BF),
        dma((FETCHED,)),
        dma((PIECES,)),
        dma,
        dma((len(DIRECTIONS),)),
        dma((len(DIRECTIONS),)),
        dma,
        dma,
        dma((STEPS,)),
        dma((STEPS,)),
        dma((STEPS,)),
        dma((STEPS,)),
        dma,
    ]
    return pl.pallas_call(
        kernel,
        out_shape=jax.ShapeDtypeStruct((NODES * batch, D), BF),
        in_specs=[pl.BlockSpec(memory_space=pl.ANY)] * len(operands),
        out_specs=pl.BlockSpec(memory_space=pltpu.VMEM),
        scratch_shapes=scratch,
        cost_estimate=pl.CostEstimate(
            flops=4 * 10**9, bytes_accessed=15 * 10**6, transcendentals=10**6
        ),
        compiler_params=pltpu.CompilerParams(
            collective_id=0, has_side_effects=True, vmem_limit_bytes=64 * 2**20
        ),
    )(*operands).reshape(NODES, batch, D)


def solution(mesh):
    nodes = P(("lat", "lon"), None)
    edges = P(("lat", "lon"))
    split = [P("lat", "lon", None, None), nodes, nodes, edges, edges, nodes, edges, edges]
    split += [P()] * (len(Given._fields) - len(split))
    return jax.shard_map(
        on_device,
        mesh=mesh,
        in_specs=tuple(split),
        out_specs=P(("lat", "lon"), None, None),
        check_vma=False,
    )
```

```python
from typing import Any, NamedTuple

import jax
import jax.numpy as jnp
from jax import lax
from jax.experimental import pallas as pl
from jax.experimental.pallas import tpu as pltpu
from jax.sharding import PartitionSpec as P

BF = jnp.bfloat16
F32 = jnp.float32
I32 = jnp.int32
MESH = pl.DeviceIdType.MESH

BATCH = 2
D = 512
HALO = 2
STEPS = 2
CHUNK = 64
LATS = 8
LONS = 16
PAIRS = LATS * LONS
NODES = 32
GRID_EDGES = 128
EDGES = 256
NEAR = (1, 15, 16, 17, 31, 112, 113, 127)
EXTRA = 3
SLOTS = PAIRS + EXTRA * len(NEAR)
CLOSE = 4 * NODES + 2 * EXTRA * len(NEAR)
DIRECTIONS = tuple((a, b) for a in (0, -1, 1) for b in (0, -1, 1) if (a, b) != (0, 0))


class Given(NamedTuple):
    grid_inputs: Any
    mesh_latents: Any
    g2m_edges: Any
    g2m_sender: Any
    g2m_receiver: Any
    mesh_edges: Any
    mesh_sender: Any
    mesh_receiver: Any
    embed_w1: Any
    embed_b1: Any
    embed_w2: Any
    embed_gain: Any
    enc_edge_w1: Any
    enc_edge_b1: Any
    enc_edge_w2: Any
    enc_edge_gain: Any
    enc_node_w1: Any
    enc_node_b1: Any
    enc_node_w2: Any
    enc_node_gain: Any
    proc_edge_w1: Any
    proc_edge_b1: Any
    proc_edge_w2: Any
    proc_edge_gain: Any
    proc_node_w1: Any
    proc_node_b1: Any
    proc_node_w2: Any
    proc_node_gain: Any


class Held(NamedTuple):
    g2m_sender: Any
    g2m_receiver: Any
    mesh_sender: Any
    mesh_receiver: Any
    mesh_latents: Any
    g2m_edges: Any
    enc_edge_w1: Any
    enc_edge_b1: Any
    embed_w1: Any
    embed_b1: Any
    embed_w2: Any
    embed_gain: Any
    enc_edge_w2: Any
    enc_edge_gain: Any
    enc_node_w1: Any
    enc_node_b1: Any
    enc_node_w2: Any
    enc_node_gain: Any
    mesh_edges: Any
    proc_edge_w1: Any
    proc_edge_b1: Any
    proc_edge_w2: Any
    proc_edge_gain: Any
    proc_node_w1: Any
    proc_node_b1: Any
    proc_node_w2: Any
    proc_node_gain: Any


FETCHED = len(Held._fields)
BASE = 8
PIECES = 4


def mm(a, b):
    return jnp.dot(a, b, preferred_element_type=F32)


def mm_nt(a, b):
    return lax.dot_general(a, b, (((1,), (1,)), ((), ())), preferred_element_type=F32)


def iota(shape, dim):
    return lax.broadcasted_iota(I32, shape, dim)


def hot(mask):
    return jnp.where(mask, 1.0, 0.0).astype(BF)


def silu(v):
    half = 0.5 * v
    return half + half * jnp.tanh(half)


def norm(v, gain):
    count = 1.0 / v.shape[-1]
    mean = jnp.sum(v, axis=-1, keepdims=True) * count
    square = jnp.sum(v * v, axis=-1, keepdims=True) * count
    scale = lax.rsqrt(jnp.maximum(square - mean * mean, 0.0) + 1e-05)
    return (v - mean) * scale * gain


def by_rows(act, *arrays):
    count = arrays[0].shape[0]
    pieces = [act(*(v[c : c + CHUNK] for v in arrays)) for c in range(0, count, CHUNK)]
    return jnp.concatenate(pieces, axis=0)


def silu_rows(*terms):
    return by_rows(lambda *parts: silu(sum(parts[1:], parts[0])).astype(BF), *terms)


def updated_rows(rows, v, gain):
    return by_rows(lambda r, part: (r.astype(F32) + norm(part, gain)).astype(BF), rows, v)


def doubled_column(row, count):
    shape = (2 * count, count)
    spread = jnp.where(iota(shape, 1) == (iota(shape, 0) >> 1), row.astype(F32), 0.0)
    return jnp.sum(spread, axis=1, keepdims=True).astype(I32)


def doubled_row(row, count):
    shape = (count, 2 * count)
    return mm(row.astype(F32).astype(BF), hot((iota(shape, 1) >> 1) == iota(shape, 0))).astype(I32)


def kernel(*refs):
    grid_hbm = refs[0]
    hbm = refs[1 : 1 + FETCHED]
    out_ref = refs[1 + FETCHED]
    refs = refs[2 + FETCHED :]
    held = Held(*refs[:FETCHED])
    (
        cells, found, sender, picked, asked_row, asked_place, own_rows, gather_far, gather_close, close_rows, edge_base,
        req_out, req_in, out_rows, in_rows,
        fetch_sem, cells_sem, sender_sem,
        halo_send, halo_recv, req_send, req_recv, row_send, row_recv,
        more_send, more_recv, asked_sem,
    ) = refs[FETCHED:]

    lat = lax.axis_index("lat")
    lon = lax.axis_index("lon")
    lat_rows, lon_cols = grid_hbm.shape[:2]

    def place(step_lat, step_lon, sign):
        return (
            (lat + sign * step_lat + LATS) & (LATS - 1),
            (lon + sign * step_lon + LONS) & (LONS - 1),
        )

    def for_all_others(act):
        for step_lon in range(1, LONS):
            act(0, step_lon)

        def band(step_lat, carry):
            for step_lon in range(LONS):
                act(step_lat, step_lon)
            return carry

        lax.fori_loop(1, LATS, band, 0)

    fetches = [
        pltpu.make_async_copy(hbm[n], held[n], fetch_sem.at[n]) for n in range(FETCHED)
    ]
    fetch = Held(*fetches)

    def ready(*copies):
        for copy in copies:
            copy.wait()

    for copy in fetches[:4]:
        copy.start()
    cells_copies = []
    for n in range(PIECES):
        rows = lat_rows // PIECES
        cells_copies.append(
            pltpu.make_async_copy(
                grid_hbm.at[pl.ds(n * rows, rows)],
                cells.at[pl.ds(HALO + n * rows, rows), pl.ds(HALO, lon_cols)],
                cells_sem.at[n],
            )
        )
    for copy in cells_copies:
        copy.start()

    barrier = pltpu.get_barrier_semaphore()
    for i in NEAR:
        pl.semaphore_signal(
            barrier, inc=1, device_id=place(i // LONS, i % LONS, 1), device_id_type=MESH
        )

    def greet(step_lat, step_lon):
        pl.semaphore_signal(
            barrier, inc=1, device_id=place(step_lat, step_lon, 1), device_id_type=MESH
        )

    for step_lat in (0, 1, LATS - 1):
        for step_lon in range(2, LONS - 1):
            greet(step_lat, step_lon)

    def greet_band(step_lat, carry):
        for step_lon in range(LONS):
            greet(step_lat, step_lon)
        return carry

    lax.fori_loop(2, LATS - 1, greet_band, 0)

    pl.semaphore_wait(barrier, PAIRS - 1)

    spans = {0: (0, lat_rows, HALO), -1: (0, HALO, HALO + lat_rows), 1: (lat_rows - HALO, HALO, 0)}
    spans_lon = {
        0: (0, lon_cols, HALO), -1: (0, HALO, HALO + lon_cols), 1: (lon_cols - HALO, HALO, 0)
    }
    halo = []
    for n, (a, b) in enumerate(DIRECTIONS):
        row0, rows, to_row = spans[a]
        col0, cols, to_col = spans_lon[b]
        halo.append(
            pltpu.make_async_remote_copy(
                src_ref=grid_hbm.at[pl.ds(row0, rows), pl.ds(col0, cols)],
                dst_ref=cells.at[pl.ds(to_row, rows), pl.ds(to_col, cols)],
                send_sem=halo_send.at[n],
                recv_sem=halo_recv.at[n],
                device_id=((lat + a + LATS) & (LATS - 1), (lon + b + LONS) & (LONS - 1)),
                device_id_type=MESH,
            )
        )
    groups = [
        [copy for copy, (a, _) in zip(halo, DIRECTIONS) if a == which] for which in (0, -1, 1)
    ]
    has_before = lat > 0
    has_after = lat < LATS - 1

    for copy in groups[0]:
        copy.start()

    @pl.when(has_before)
    def _():
        for copy in groups[1]:
            copy.start()

    @pl.when(has_after)
    def _():
        for copy in groups[2]:
            copy.start()

    for copy in fetches[4:BASE]:
        copy.start()

    ready(fetch.g2m_sender, fetch.g2m_receiver, fetch.mesh_sender, fetch.mesh_receiver)
    cell = held.g2m_sender[...]
    cell_row = (cell >> 10) - lat * lat_rows + HALO
    cell_col = ((cell & (LONS * lon_cols - 1)) - lon * lon_cols + HALO) & (LONS * lon_cols - 1)
    found[0:1] = jnp.clip(cell_row, 0, cells.shape[0] - 1)
    found[1:2] = jnp.clip(cell_col, 0, cells.shape[1] - 1)
    sender_copy = pltpu.make_async_copy(found, sender, sender_sem)
    sender_copy.start()
    senders = held.mesh_sender[...]
    owner = senders >> 5
    row = senders & (NODES - 1)
    rel = ((((owner >> 4) - lat) & (LATS - 1)) << 4) | (((owner & 15) - lon) & (LONS - 1))
    owner2 = hot((iota((2 * PAIRS, EDGES), 0) >> 1) == rel)
    row2 = hot((iota((128, EDGES), 0) >> 1) == row)
    asked = mm_nt(owner2, row2)
    shape = (2 * PAIRS, 128)
    same = (iota(shape, 0) & 1) == (iota(shape, 1) & 1)
    asked = hot((asked > 0.5) & same & (iota(shape, 0) >= 2))
    req_out[...] = asked.reshape(PAIRS, 2, 128)
    req_in[0] = jnp.zeros((2, 128), BF)
    for t in range(STEPS):
        in_rows[t, 0] = jnp.zeros((2, D), BF)

    def ask(step_lat, step_lon):
        i = step_lat * LONS + step_lon
        pltpu.make_async_remote_copy(
            src_ref=req_out.at[i], dst_ref=req_in.at[i], send_sem=req_send, recv_sem=req_recv,
            device_id=place(step_lat, step_lon, 1), device_id_type=MESH,
        ).start()

    for_all_others(ask)

    for copy in fetches[BASE:]:
        copy.start()

    grid_receivers = held.g2m_receiver[...]
    shape = (2 * NODES, 2 * GRID_EDGES)
    total_grid = hot(
        iota(shape, 0) == 2 * doubled_row(grid_receivers, GRID_EDGES) + (iota(shape, 1) & 1)
    )
    shape = (2 * GRID_EDGES, NODES)
    gather_grid_recv = hot(iota(shape, 1) == doubled_column(grid_receivers, GRID_EDGES))

    ready(fetch.mesh_latents, fetch.g2m_edges, fetch.enc_edge_w1, fetch.enc_edge_b1)
    latents = held.mesh_latents[...]
    shape = (2 * GRID_EDGES, GRID_EDGES)
    grid_edges = mm(hot(iota(shape, 1) == (iota(shape, 0) >> 1)), held.g2m_edges[...]).astype(BF)
    mesh_recv = mm(latents, held.enc_edge_w1[2]).astype(BF)
    grid_base = (
        mm(grid_edges, held.enc_edge_w1[0])
        + mm(gather_grid_recv, mesh_recv)
        + held.enc_edge_b1[...]
    )
    shape = (2 * NODES, NODES)
    state = mm(hot(iota(shape, 1) == (iota(shape, 0) >> 1)), latents).astype(BF)

    ready(fetch.embed_w1, fetch.embed_b1, fetch.embed_w2, fetch.embed_gain)
    ready(fetch.enc_edge_w2, fetch.enc_edge_gain)
    ready(fetch.enc_node_w1, fetch.enc_node_b1, fetch.enc_node_w2, fetch.enc_node_gain)
    enc_node_base = mm(state, held.enc_node_w1[0]) + held.enc_node_b1[...]

    sender_copy.wait()
    for copy in cells_copies:
        copy.wait()
    for copy in groups[0]:
        copy.wait_recv()

    @pl.when(has_after)
    def _():
        for copy in groups[1]:
            copy.wait_recv()

    @pl.when(has_before)
    def _():
        for copy in groups[2]:
            copy.wait_recv()

    def pick(k, carry):
        picked[k] = cells[sender[0, k], sender[1, k]]
        return carry

    lax.fori_loop(0, GRID_EDGES, pick, 0, unroll=32)

    inputs = picked[...].reshape(2 * GRID_EDGES, picked.shape[2])
    bias = held.embed_b1[...]
    hidden = by_rows(lambda v: silu(v + bias).astype(BF), mm(inputs, held.embed_w1[...]))
    gain = held.embed_gain[...]
    latent = by_rows(lambda v: norm(v, gain).astype(BF), mm(hidden, held.embed_w2[...]))
    hidden = silu_rows(mm(latent, held.enc_edge_w1[1]), grid_base)
    pltpu.make_async_copy(
        req_in.at[pl.ds(1, PAIRS - 1)], req_in.at[pl.ds(1, PAIRS - 1)], req_recv
    ).wait()
    wanted = req_in[...].reshape(2 * PAIRS, 128)[:, : 2 * NODES]
    shape = (2 * NODES, 2 * NODES)
    before = hot(
        (iota(shape, 0) < iota(shape, 1)) & ((iota(shape, 0) & 1) == (iota(shape, 1) & 1))
    )
    place_of = mm(wanted, before).astype(BF)
    first = jnp.where(place_of.astype(F32) < 0.5, wanted.astype(F32), 0.0).astype(BF)
    shape = (2 * EXTRA * len(NEAR), 2 * PAIRS)
    line = iota(shape, 0)
    which = jnp.zeros_like(line)
    target = jnp.full_like(line, NEAR[0])
    for n in range(1, len(NEAR)):
        later = line >= 2 * EXTRA * n
        which = jnp.where(later, n, which)
        target = jnp.where(later, NEAR[n], target)
    choose = hot(iota(shape, 1) == 2 * target + (line & 1))
    kth = ((line >> 1) - EXTRA * which + 1).astype(F32)[:, : 2 * NODES]
    more = jnp.where(mm(choose, place_of) == kth, mm(choose, wanted), 0.0).astype(BF)
    lanes = iota((8, 2 * NODES), 1).astype(F32).astype(BF)
    chosen = mm_nt(lanes, jnp.concatenate([first, more], axis=0)).astype(I32)
    asked_row[...] = (chosen[0:1] >> 1) & (NODES - 1)
    asked_copy = pltpu.make_async_copy(asked_row, asked_place, asked_sem)
    asked_copy.start()

    new_edges = updated_rows(grid_edges, mm(hidden, held.enc_edge_w2[...]), held.enc_edge_gain[...])
    summed = mm(total_grid, new_edges).astype(BF)
    hidden = silu(enc_node_base + mm(summed, held.enc_node_w1[1])).astype(BF)
    update = norm(mm(hidden, held.enc_node_w2[...]), held.enc_node_gain[...])
    state = (state.astype(F32) + update).astype(BF)

    ready(fetch.proc_edge_w1)
    asked_copy.wait()
    for t in range(STEPS):
        outgoing = mm(state, held.proc_edge_w1[t, 1]).astype(BF)
        own_rows[...] = outgoing.reshape(NODES, 2, D)

        def fill(i, t=t):
            out_rows[t, i] = own_rows[asked_place[0, 2 * i]]

        for i in range(PAIRS, SLOTS):
            fill(i)
        for n, i in enumerate(NEAR):
            span = pl.ds(PAIRS + EXTRA * n, EXTRA)
            pltpu.make_async_remote_copy(
                src_ref=out_rows.at[t, span], dst_ref=in_rows.at[t, span],
                send_sem=more_send.at[t], recv_sem=more_recv.at[t],
                device_id=place(i // LONS, i % LONS, -1), device_id_type=MESH,
            ).start()

        def give(step_lat, step_lon, t=t):
            i = step_lat * LONS + step_lon
            pltpu.make_async_remote_copy(
                src_ref=out_rows.at[t, i], dst_ref=in_rows.at[t, i],
                send_sem=row_send.at[t], recv_sem=row_recv.at[t],
                device_id=place(step_lat, step_lon, -1), device_id_type=MESH,
            ).start()

        for step_lon in range(1, LONS):
            fill(step_lon)
        for step_lon in range(1, LONS):
            give(0, step_lon)

        def give_band(step_lat, carry, fill=fill, give=give):
            for step_lon in range(LONS):
                fill(step_lat * LONS + step_lon)
            for step_lon in range(LONS):
                give(step_lat, step_lon)
            return carry

        lax.fori_loop(1, LATS, give_band, 0)

        if t == 0:
            ready(fetch.proc_edge_b1, fetch.proc_edge_w2, fetch.proc_edge_gain)
            ready(fetch.proc_node_w1, fetch.proc_node_b1, fetch.proc_node_w2, fetch.proc_node_gain)
            owner1 = hot(iota((PAIRS, EDGES), 0) == rel)
            row1 = iota((NODES, EDGES), 0) == row
            needed = hot(mm_nt(hot(row1), owner1) > 0.5)
            below = hot(iota((NODES, NODES), 1) < iota((NODES, NODES), 0))
            order = mm(below, needed).astype(BF)
            rank = jnp.sum(jnp.where(row1, mm(order, owner1), 0.0), axis=0, keepdims=True).astype(I32)
            near = jnp.zeros_like(rel)
            for n, i in enumerate(NEAR):
                near = jnp.where(rel == i, n, near)
            nowhere = -PAIRS
            far = jnp.where((rank == 0) & (rel > 0), rel, nowhere)
            close = jnp.where(rank == 0, nowhere, 2 * NODES + EXTRA * near + rank - 1)
            close = jnp.where(rel == 0, NODES + row, close)
            receivers = held.mesh_receiver[...]
            shape = (2 * EDGES, EDGES)
            twice = hot(iota(shape, 1) == (iota(shape, 0) >> 1))
            columns = jnp.concatenate([far, close, receivers, jnp.zeros((5, EDGES), I32)], axis=0)
            columns = mm_nt(twice, columns.astype(F32).astype(BF)).astype(I32)
            shape = (2 * EDGES, 2 * PAIRS)
            gather_far[...] = hot(iota(shape, 1) == 2 * columns[:, 0:1] + (iota(shape, 0) & 1))
            shape = (2 * EDGES, CLOSE)
            lane = iota(shape, 1) - (iota(shape, 0) & 1)
            gather_close[...] = hot((lane == 2 * columns[:, 2:3]) | (lane == 2 * columns[:, 1:2]))
            shape = (2 * NODES, 2 * EDGES)
            total_mesh = hot(iota(shape, 0) == 2 * doubled_row(receivers, EDGES) + (iota(shape, 1) & 1))

            ready(fetch.mesh_edges)
            edge_state = mm(twice, held.mesh_edges[...]).astype(BF)

        close_rows[: 2 * NODES] = mm(state, held.proc_edge_w1[t, 2]).astype(BF)
        close_rows[2 * NODES : 4 * NODES] = outgoing
        node_base = mm(state, held.proc_node_w1[t, 0]) + held.proc_node_b1[t : t + 1]
        arrived = in_rows.at[t, pl.ds(PAIRS, SLOTS - PAIRS)]
        pltpu.make_async_copy(arrived, arrived, more_recv.at[t]).wait()
        close_rows[4 * NODES :] = in_rows[t, PAIRS:].reshape(2 * (SLOTS - PAIRS), D)
        edge_base[...] = (
            mm(edge_state, held.proc_edge_w1[t, 0])
            + mm(gather_close[...], close_rows[...])
            + held.proc_edge_b1[t : t + 1]
        )

        if t == 0:
            for copy in groups[0]:
                copy.wait_send()

            @pl.when(has_before)
            def _():
                for copy in groups[1]:
                    copy.wait_send()

            @pl.when(has_after)
            def _():
                for copy in groups[2]:
                    copy.wait_send()

            asked_all = req_out.at[pl.ds(1, PAIRS - 1)]
            pltpu.make_async_copy(asked_all, asked_all, req_send).wait()
        sent = out_rows.at[t, pl.ds(PAIRS, SLOTS - PAIRS)]
        pltpu.make_async_copy(sent, sent, more_send.at[t]).wait()
        sent = out_rows.at[t, pl.ds(1, PAIRS - 1)]
        pltpu.make_async_copy(sent, sent, row_send.at[t]).wait()
        arrived = in_rows.at[t, pl.ds(1, PAIRS - 1)]
        pltpu.make_async_copy(arrived, arrived, row_recv.at[t]).wait()
        table = in_rows[t, :PAIRS].reshape(2 * PAIRS, D)
        gain = held.proc_edge_gain[t : t + 1]
        hidden = silu_rows(mm(gather_far[...], table), edge_base)
        edge_state = updated_rows(edge_state, mm(hidden, held.proc_edge_w2[t]), gain)
        summed = mm(total_mesh, edge_state).astype(BF)
        hidden = silu(node_base + mm(summed, held.proc_node_w1[t, 1])).astype(BF)
        update = norm(mm(hidden, held.proc_node_w2[t]), held.proc_node_gain[t : t + 1])
        state = (state.astype(F32) + update).astype(BF)

    out_ref[...] = state


def on_device(*args):
    given = Given(*args)
    lat_rows, lon_cols, batch, width = given.grid_inputs.shape

    def flat(row):
        return row.reshape(1, row.shape[0])

    wanted = Held(
        flat(given.g2m_sender),
        flat(given.g2m_receiver),
        flat(given.mesh_sender),
        flat(given.mesh_receiver),
        given.mesh_latents,
        given.g2m_edges,
        given.enc_edge_w1,
        flat(given.enc_edge_b1),
        given.embed_w1,
        flat(given.embed_b1),
        given.embed_w2,
        flat(given.embed_gain),
        given.enc_edge_w2,
        flat(given.enc_edge_gain),
        given.enc_node_w1,
        flat(given.enc_node_b1),
        given.enc_node_w2,
        flat(given.enc_node_gain),
        given.mesh_edges,
        given.proc_edge_w1,
        given.proc_edge_b1,
        given.proc_edge_w2,
        given.proc_edge_gain,
        given.proc_node_w1,
        given.proc_node_b1,
        given.proc_node_w2,
        given.proc_node_gain,
    )
    operands = [given.grid_inputs, *wanted]
    dma = pltpu.SemaphoreType.DMA
    scratch = [pltpu.VMEM(part.shape, part.dtype) for part in wanted]
    scratch += [
        pltpu.VMEM((lat_rows + 2 * HALO, lon_cols + 2 * HALO, batch, width), BF),
        pltpu.VMEM((2, GRID_EDGES), I32),
        pltpu.SMEM((2, GRID_EDGES), I32),
        pltpu.VMEM((GRID_EDGES, batch, width), BF),
        pltpu.VMEM((1, 2 * SLOTS), I32),
        pltpu.SMEM((1, 2 * SLOTS), I32),
        pltpu.VMEM((NODES, 2, D), BF),
        pltpu.VMEM((2 * EDGES, 2 * PAIRS), BF),
        pltpu.VMEM((2 * EDGES, CLOSE), BF),
        pltpu.VMEM((CLOSE, D), BF),
        pltpu.VMEM((2 * EDGES, D), F32),
        pltpu.VMEM((PAIRS, 2, 128), BF),
        pltpu.VMEM((PAIRS, 2, 128), BF),
        pltpu.VMEM((STEPS, SLOTS, 2, D), BF),
        pltpu.VMEM((STEPS, SLOTS, 2, D), BF),
        dma((FETCHED,)),
        dma((PIECES,)),
        dma,
        dma((len(DIRECTIONS),)),
        dma((len(DIRECTIONS),)),
        dma,
        dma,
        dma((STEPS,)),
        dma((STEPS,)),
        dma((STEPS,)),
        dma((STEPS,)),
        dma,
    ]
    return pl.pallas_call(
        kernel,
        out_shape=jax.ShapeDtypeStruct((NODES * batch, D), BF),
        in_specs=[pl.BlockSpec(memory_space=pl.ANY)] * len(operands),
        out_specs=pl.BlockSpec(memory_space=pltpu.VMEM),
        scratch_shapes=scratch,
        cost_estimate=pl.CostEstimate(
            flops=4 * 10**9, bytes_accessed=15 * 10**6, transcendentals=10**6
        ),
        compiler_params=pltpu.CompilerParams(
            collective_id=0, has_side_effects=True, vmem_limit_bytes=64 * 2**20
        ),
    )(*operands).reshape(NODES, batch, D)


def solution(mesh):
    nodes = P(("lat", "lon"), None)
    edges = P(("lat", "lon"))
    split = [P("lat", "lon", None, None), nodes, nodes, edges, edges, nodes, edges, edges]
    split += [P()] * (len(Given._fields) - len(split))
    return jax.shard_map(
        on_device,
        mesh=mesh,
        in_specs=tuple(split),
        out_specs=P(("lat", "lon"), None, None),
        check_vma=False,
    )
```

```python
from typing import Any, NamedTuple

import jax
import jax.numpy as jnp
from jax import lax
from jax.experimental import pallas as pl
from jax.experimental.pallas import tpu as pltpu
from jax.sharding import PartitionSpec as P

BF = jnp.bfloat16
F32 = jnp.float32
I32 = jnp.int32
MESH = pl.DeviceIdType.MESH

BATCH = 2
D = 512
HALO = 2
STEPS = 2
CHUNK = 128
LATS = 8
LONS = 16
PAIRS = LATS * LONS
NODES = 32
GRID_EDGES = 128
EDGES = 256
NEAR = (1, 15, 16, 17, 31, 112, 113, 127)
EXTRA = 3
SLOTS = PAIRS + EXTRA * len(NEAR)
CLOSE = 4 * NODES + 2 * EXTRA * len(NEAR)
DIRECTIONS = tuple((a, b) for a in (0, -1, 1) for b in (0, -1, 1) if (a, b) != (0, 0))


class Given(NamedTuple):
    grid_inputs: Any
    mesh_latents: Any
    g2m_edges: Any
    g2m_sender: Any
    g2m_receiver: Any
    mesh_edges: Any
    mesh_sender: Any
    mesh_receiver: Any
    embed_w1: Any
    embed_b1: Any
    embed_w2: Any
    embed_gain: Any
    enc_edge_w1: Any
    enc_edge_b1: Any
    enc_edge_w2: Any
    enc_edge_gain: Any
    enc_node_w1: Any
    enc_node_b1: Any
    enc_node_w2: Any
    enc_node_gain: Any
    proc_edge_w1: Any
    proc_edge_b1: Any
    proc_edge_w2: Any
    proc_edge_gain: Any
    proc_node_w1: Any
    proc_node_b1: Any
    proc_node_w2: Any
    proc_node_gain: Any


class Held(NamedTuple):
    g2m_sender: Any
    g2m_receiver: Any
    mesh_sender: Any
    mesh_receiver: Any
    mesh_latents: Any
    g2m_edges: Any
    enc_edge_w1: Any
    enc_edge_b1: Any
    embed_w1: Any
    embed_b1: Any
    embed_w2: Any
    embed_gain: Any
    enc_edge_w2: Any
    enc_edge_gain: Any
    enc_node_w1: Any
    enc_node_b1: Any
    enc_node_w2: Any
    enc_node_gain: Any
    mesh_edges: Any
    proc_edge_w1: Any
    proc_edge_b1: Any
    proc_edge_w2: Any
    proc_edge_gain: Any
    proc_node_w1: Any
    proc_node_b1: Any
    proc_node_w2: Any
    proc_node_gain: Any


FETCHED = len(Held._fields)
BASE = 8
PIECES = 4


def mm(a, b):
    return jnp.dot(a, b, preferred_element_type=F32)


def mm_nt(a, b):
    return lax.dot_general(a, b, (((1,), (1,)), ((), ())), preferred_element_type=F32)


def iota(shape, dim):
    return lax.broadcasted_iota(I32, shape, dim)


def hot(mask):
    return jnp.where(mask, 1.0, 0.0).astype(BF)


def silu(v):
    half = 0.5 * v
    return half + half * jnp.tanh(half)


def norm(v, gain):
    count = 1.0 / v.shape[-1]
    mean = jnp.sum(v, axis=-1, keepdims=True) * count
    square = jnp.sum(v * v, axis=-1, keepdims=True) * count
    scale = lax.rsqrt(jnp.maximum(square - mean * mean, 0.0) + 1e-05)
    return (v - mean) * scale * gain


def by_rows(act, *arrays):
    count = arrays[0].shape[0]
    pieces = [act(*(v[c : c + CHUNK] for v in arrays)) for c in range(0, count, CHUNK)]
    return jnp.concatenate(pieces, axis=0)


def silu_rows(*terms):
    return by_rows(lambda *parts: silu(sum(parts[1:], parts[0])).astype(BF), *terms)


def updated_rows(rows, v, gain):
    return by_rows(lambda r, part: (r.astype(F32) + norm(part, gain)).astype(BF), rows, v)


def doubled_column(row, count):
    shape = (2 * count, count)
    spread = jnp.where(iota(shape, 1) == (iota(shape, 0) >> 1), row.astype(F32), 0.0)
    return jnp.sum(spread, axis=1, keepdims=True).astype(I32)


def doubled_row(row, count):
    shape = (count, 2 * count)
    return mm(row.astype(F32).astype(BF), hot((iota(shape, 1) >> 1) == iota(shape, 0))).astype(I32)


def kernel(*refs):
    grid_hbm = refs[0]
    hbm = refs[1 : 1 + FETCHED]
    out_ref = refs[1 + FETCHED]
    refs = refs[2 + FETCHED :]
    held = Held(*refs[:FETCHED])
    (
        cells, found, sender, picked, asked_row, asked_place, own_rows, gather_far, gather_close, close_rows, edge_base,
        req_out, req_in, out_rows, in_rows,
        fetch_sem, cells_sem, sender_sem,
        halo_send, halo_recv, req_send, req_recv, row_send, row_recv,
        more_send, more_recv, asked_sem,
    ) = refs[FETCHED:]

    lat = lax.axis_index("lat")
    lon = lax.axis_index("lon")
    lat_rows, lon_cols = grid_hbm.shape[:2]

    def place(step_lat, step_lon, sign):
        return (
            (lat + sign * step_lat + LATS) & (LATS - 1),
            (lon + sign * step_lon + LONS) & (LONS - 1),
        )

    def for_all_others(act):
        for step_lon in range(1, LONS):
            act(0, step_lon)

        def band(step_lat, carry):
            for step_lon in range(LONS):
                act(step_lat, step_lon)
            return carry

        lax.fori_loop(1, LATS, band, 0)

    fetches = [
        pltpu.make_async_copy(hbm[n], held[n], fetch_sem.at[n]) for n in range(FETCHED)
    ]
    fetch = Held(*fetches)

    def ready(*copies):
        for copy in copies:
            copy.wait()

    for copy in fetches[:4]:
        copy.start()
    cells_copies = []
    for n in range(PIECES):
        rows = lat_rows // PIECES
        cells_copies.append(
            pltpu.make_async_copy(
                grid_hbm.at[pl.ds(n * rows, rows)],
                cells.at[pl.ds(HALO + n * rows, rows), pl.ds(HALO, lon_cols)],
                cells_sem.at[n],
            )
        )
    for copy in cells_copies:
        copy.start()

    barrier = pltpu.get_barrier_semaphore()
    for i in NEAR:
        pl.semaphore_signal(
            barrier, inc=1, device_id=place(i // LONS, i % LONS, 1), device_id_type=MESH
        )

    def greet(step_lat, step_lon):
        pl.semaphore_signal(
            barrier, inc=1, device_id=place(step_lat, step_lon, 1), device_id_type=MESH
        )

    for step_lat in (0, 1, LATS - 1):
        for step_lon in range(2, LONS - 1):
            greet(step_lat, step_lon)

    def greet_band(step_lat, carry):
        for step_lon in range(LONS):
            greet(step_lat, step_lon)
        return carry

    lax.fori_loop(2, LATS - 1, greet_band, 0)

    pl.semaphore_wait(barrier, PAIRS - 1)

    spans = {0: (0, lat_rows, HALO), -1: (0, HALO, HALO + lat_rows), 1: (lat_rows - HALO, HALO, 0)}
    spans_lon = {
        0: (0, lon_cols, HALO), -1: (0, HALO, HALO + lon_cols), 1: (lon_cols - HALO, HALO, 0)
    }
    halo = []
    for n, (a, b) in enumerate(DIRECTIONS):
        row0, rows, to_row = spans[a]
        col0, cols, to_col = spans_lon[b]
        halo.append(
            pltpu.make_async_remote_copy(
                src_ref=grid_hbm.at[pl.ds(row0, rows), pl.ds(col0, cols)],
                dst_ref=cells.at[pl.ds(to_row, rows), pl.ds(to_col, cols)],
                send_sem=halo_send.at[n],
                recv_sem=halo_recv.at[n],
                device_id=((lat + a + LATS) & (LATS - 1), (lon + b + LONS) & (LONS - 1)),
                device_id_type=MESH,
            )
        )
    groups = [
        [copy for copy, (a, _) in zip(halo, DIRECTIONS) if a == which] for which in (0, -1, 1)
    ]
    has_before = lat > 0
    has_after = lat < LATS - 1

    for copy in groups[0]:
        copy.start()

    @pl.when(has_before)
    def _():
        for copy in groups[1]:
            copy.start()

    @pl.when(has_after)
    def _():
        for copy in groups[2]:
            copy.start()

    for copy in fetches[4:BASE]:
        copy.start()

    ready(fetch.g2m_sender, fetch.g2m_receiver, fetch.mesh_sender, fetch.mesh_receiver)
    cell = held.g2m_sender[...]
    cell_row = (cell >> 10) - lat * lat_rows + HALO
    cell_col = ((cell & (LONS * lon_cols - 1)) - lon * lon_cols + HALO) & (LONS * lon_cols - 1)
    found[0:1] = jnp.clip(cell_row, 0, cells.shape[0] - 1)
    found[1:2] = jnp.clip(cell_col, 0, cells.shape[1] - 1)
    sender_copy = pltpu.make_async_copy(found, sender, sender_sem)
    sender_copy.start()
    senders = held.mesh_sender[...]
    owner = senders >> 5
    row = senders & (NODES - 1)
    rel = ((((owner >> 4) - lat) & (LATS - 1)) << 4) | (((owner & 15) - lon) & (LONS - 1))
    owner2 = hot((iota((2 * PAIRS, EDGES), 0) >> 1) == rel)
    row2 = hot((iota((128, EDGES), 0) >> 1) == row)
    asked = mm_nt(owner2, row2)
    shape = (2 * PAIRS, 128)
    same = (iota(shape, 0) & 1) == (iota(shape, 1) & 1)
    asked = hot((asked > 0.5) & same & (iota(shape, 0) >= 2))
    req_out[...] = asked.reshape(PAIRS, 2, 128)
    req_in[0] = jnp.zeros((2, 128), BF)
    for t in range(STEPS):
        in_rows[t, 0] = jnp.zeros((2, D), BF)

    def ask(step_lat, step_lon):
        i = step_lat * LONS + step_lon
        pltpu.make_async_remote_copy(
            src_ref=req_out.at[i], dst_ref=req_in.at[i], send_sem=req_send, recv_sem=req_recv,
            device_id=place(step_lat, step_lon, 1), device_id_type=MESH,
        ).start()

    for_all_others(ask)

    for copy in fetches[BASE:]:
        copy.start()

    grid_receivers = held.g2m_receiver[...]
    shape = (2 * NODES, 2 * GRID_EDGES)
    total_grid = hot(
        iota(shape, 0) == 2 * doubled_row(grid_receivers, GRID_EDGES) + (iota(shape, 1) & 1)
    )
    shape = (2 * GRID_EDGES, NODES)
    gather_grid_recv = hot(iota(shape, 1) == doubled_column(grid_receivers, GRID_EDGES))

    ready(fetch.mesh_latents, fetch.g2m_edges, fetch.enc_edge_w1, fetch.enc_edge_b1)
    latents = held.mesh_latents[...]
    shape = (2 * GRID_EDGES, GRID_EDGES)
    grid_edges = mm(hot(iota(shape, 1) == (iota(shape, 0) >> 1)), held.g2m_edges[...]).astype(BF)
    mesh_recv = mm(latents, held.enc_edge_w1[2]).astype(BF)
    grid_base = (
        mm(grid_edges, held.enc_edge_w1[0])
        + mm(gather_grid_recv, mesh_recv)
        + held.enc_edge_b1[...]
    )
    shape = (2 * NODES, NODES)
    state = mm(hot(iota(shape, 1) == (iota(shape, 0) >> 1)), latents).astype(BF)

    ready(fetch.embed_w1, fetch.embed_b1, fetch.embed_w2, fetch.embed_gain)
    ready(fetch.enc_edge_w2, fetch.enc_edge_gain)
    ready(fetch.enc_node_w1, fetch.enc_node_b1, fetch.enc_node_w2, fetch.enc_node_gain)
    enc_node_base = mm(state, held.enc_node_w1[0]) + held.enc_node_b1[...]

    sender_copy.wait()
    for copy in cells_copies:
        copy.wait()
    for copy in groups[0]:
        copy.wait_recv()

    @pl.when(has_after)
    def _():
        for copy in groups[1]:
            copy.wait_recv()

    @pl.when(has_before)
    def _():
        for copy in groups[2]:
            copy.wait_recv()

    def pick(k, carry):
        picked[k] = cells[sender[0, k], sender[1, k]]
        return carry

    lax.fori_loop(0, GRID_EDGES, pick, 0, unroll=32)

    inputs = picked[...].reshape(2 * GRID_EDGES, picked.shape[2])
    bias = held.embed_b1[...]
    hidden = by_rows(lambda v: silu(v + bias).astype(BF), mm(inputs, held.embed_w1[...]))
    gain = held.embed_gain[...]
    latent = by_rows(lambda v: norm(v, gain).astype(BF), mm(hidden, held.embed_w2[...]))
    hidden = silu_rows(mm(latent, held.enc_edge_w1[1]), grid_base)
    pltpu.make_async_copy(
        req_in.at[pl.ds(1, PAIRS - 1)], req_in.at[pl.ds(1, PAIRS - 1)], req_recv
    ).wait()
    wanted = req_in[...].reshape(2 * PAIRS, 128)[:, : 2 * NODES]
    shape = (2 * NODES, 2 * NODES)
    before = hot(
        (iota(shape, 0) < iota(shape, 1)) & ((iota(shape, 0) & 1) == (iota(shape, 1) & 1))
    )
    place_of = mm(wanted, before).astype(BF)
    first = jnp.where(place_of.astype(F32) < 0.5, wanted.astype(F32), 0.0).astype(BF)
    shape = (2 * EXTRA * len(NEAR), 2 * PAIRS)
    line = iota(shape, 0)
    which = jnp.zeros_like(line)
    target = jnp.full_like(line, NEAR[0])
    for n in range(1, len(NEAR)):
        later = line >= 2 * EXTRA * n
        which = jnp.where(later, n, which)
        target = jnp.where(later, NEAR[n], target)
    choose = hot(iota(shape, 1) == 2 * target + (line & 1))
    kth = ((line >> 1) - EXTRA * which + 1).astype(F32)[:, : 2 * NODES]
    more = jnp.where(mm(choose, place_of) == kth, mm(choose, wanted), 0.0).astype(BF)
    lanes = iota((8, 2 * NODES), 1).astype(F32).astype(BF)
    chosen = mm_nt(lanes, jnp.concatenate([first, more], axis=0)).astype(I32)
    asked_row[...] = (chosen[0:1] >> 1) & (NODES - 1)
    asked_copy = pltpu.make_async_copy(asked_row, asked_place, asked_sem)
    asked_copy.start()

    new_edges = updated_rows(grid_edges, mm(hidden, held.enc_edge_w2[...]), held.enc_edge_gain[...])
    summed = mm(total_grid, new_edges).astype(BF)
    hidden = silu(enc_node_base + mm(summed, held.enc_node_w1[1])).astype(BF)
    update = norm(mm(hidden, held.enc_node_w2[...]), held.enc_node_gain[...])
    state = (state.astype(F32) + update).astype(BF)

    ready(fetch.proc_edge_w1)
    asked_copy.wait()
    for t in range(STEPS):
        outgoing = mm(state, held.proc_edge_w1[t, 1]).astype(BF)
        own_rows[...] = outgoing.reshape(NODES, 2, D)

        def fill(i, t=t):
            out_rows[t, i] = own_rows[asked_place[0, 2 * i]]

        for i in range(PAIRS, SLOTS):
            fill(i)
        for n, i in enumerate(NEAR):
            span = pl.ds(PAIRS + EXTRA * n, EXTRA)
            pltpu.make_async_remote_copy(
                src_ref=out_rows.at[t, span], dst_ref=in_rows.at[t, span],
                send_sem=more_send.at[t], recv_sem=more_recv.at[t],
                device_id=place(i // LONS, i % LONS, -1), device_id_type=MESH,
            ).start()

        def give(step_lat, step_lon, t=t):
            i = step_lat * LONS + step_lon
            pltpu.make_async_remote_copy(
                src_ref=out_rows.at[t, i], dst_ref=in_rows.at[t, i],
                send_sem=row_send.at[t], recv_sem=row_recv.at[t],
                device_id=place(step_lat, step_lon, -1), device_id_type=MESH,
            ).start()

        for step_lon in range(1, LONS):
            fill(step_lon)
        for step_lon in range(1, LONS):
            give(0, step_lon)

        def give_band(step_lat, carry, fill=fill, give=give):
            for step_lon in range(LONS):
                fill(step_lat * LONS + step_lon)
            for step_lon in range(LONS):
                give(step_lat, step_lon)
            return carry

        lax.fori_loop(1, LATS, give_band, 0)

        if t == 0:
            ready(fetch.proc_edge_b1, fetch.proc_edge_w2, fetch.proc_edge_gain)
            ready(fetch.proc_node_w1, fetch.proc_node_b1, fetch.proc_node_w2, fetch.proc_node_gain)
            owner1 = hot(iota((PAIRS, EDGES), 0) == rel)
            row1 = iota((NODES, EDGES), 0) == row
            needed = hot(mm_nt(hot(row1), owner1) > 0.5)
            below = hot(iota((NODES, NODES), 1) < iota((NODES, NODES), 0))
            order = mm(below, needed).astype(BF)
            rank = jnp.sum(jnp.where(row1, mm(order, owner1), 0.0), axis=0, keepdims=True).astype(I32)
            near = jnp.zeros_like(rel)
            for n, i in enumerate(NEAR):
                near = jnp.where(rel == i, n, near)
            nowhere = -PAIRS
            far = jnp.where((rank == 0) & (rel > 0), rel, nowhere)
            close = jnp.where(rank == 0, nowhere, 2 * NODES + EXTRA * near + rank - 1)
            close = jnp.where(rel == 0, NODES + row, close)
            receivers = held.mesh_receiver[...]
            shape = (2 * EDGES, EDGES)
            twice = hot(iota(shape, 1) == (iota(shape, 0) >> 1))
            columns = jnp.concatenate([far, close, receivers, jnp.zeros((5, EDGES), I32)], axis=0)
            columns = mm_nt(twice, columns.astype(F32).astype(BF)).astype(I32)
            shape = (2 * EDGES, 2 * PAIRS)
            gather_far[...] = hot(iota(shape, 1) == 2 * columns[:, 0:1] + (iota(shape, 0) & 1))
            shape = (2 * EDGES, CLOSE)
            lane = iota(shape, 1) - (iota(shape, 0) & 1)
            gather_close[...] = hot((lane == 2 * columns[:, 2:3]) | (lane == 2 * columns[:, 1:2]))
            shape = (2 * NODES, 2 * EDGES)
            total_mesh = hot(iota(shape, 0) == 2 * doubled_row(receivers, EDGES) + (iota(shape, 1) & 1))

            ready(fetch.mesh_edges)
            edge_state = mm(twice, held.mesh_edges[...]).astype(BF)

        close_rows[: 2 * NODES] = mm(state, held.proc_edge_w1[t, 2]).astype(BF)
        close_rows[2 * NODES : 4 * NODES] = outgoing
        node_base = mm(state, held.proc_node_w1[t, 0]) + held.proc_node_b1[t : t + 1]
        arrived = in_rows.at[t, pl.ds(PAIRS, SLOTS - PAIRS)]
        pltpu.make_async_copy(arrived, arrived, more_recv.at[t]).wait()
        close_rows[4 * NODES :] = in_rows[t, PAIRS:].reshape(2 * (SLOTS - PAIRS), D)
        edge_base[...] = (
            mm(edge_state, held.proc_edge_w1[t, 0])
            + mm(gather_close[...], close_rows[...])
            + held.proc_edge_b1[t : t + 1]
        )

        if t == 0:
            for copy in groups[0]:
                copy.wait_send()

            @pl.when(has_before)
            def _():
                for copy in groups[1]:
                    copy.wait_send()

            @pl.when(has_after)
            def _():
                for copy in groups[2]:
                    copy.wait_send()

            asked_all = req_out.at[pl.ds(1, PAIRS - 1)]
            pltpu.make_async_copy(asked_all, asked_all, req_send).wait()
        sent = out_rows.at[t, pl.ds(PAIRS, SLOTS - PAIRS)]
        pltpu.make_async_copy(sent, sent, more_send.at[t]).wait()
        sent = out_rows.at[t, pl.ds(1, PAIRS - 1)]
        pltpu.make_async_copy(sent, sent, row_send.at[t]).wait()
        arrived = in_rows.at[t, pl.ds(1, PAIRS - 1)]
        pltpu.make_async_copy(arrived, arrived, row_recv.at[t]).wait()
        table = in_rows[t, :PAIRS].reshape(2 * PAIRS, D)
        gain = held.proc_edge_gain[t : t + 1]
        hidden = silu_rows(mm(gather_far[...], table), edge_base)
        edge_state = updated_rows(edge_state, mm(hidden, held.proc_edge_w2[t]), gain)
        summed = mm(total_mesh, edge_state).astype(BF)
        hidden = silu(node_base + mm(summed, held.proc_node_w1[t, 1])).astype(BF)
        update = norm(mm(hidden, held.proc_node_w2[t]), held.proc_node_gain[t : t + 1])
        state = (state.astype(F32) + update).astype(BF)

    out_ref[...] = state


def on_device(*args):
    given = Given(*args)
    lat_rows, lon_cols, batch, width = given.grid_inputs.shape

    def flat(row):
        return row.reshape(1, row.shape[0])

    wanted = Held(
        flat(given.g2m_sender),
        flat(given.g2m_receiver),
        flat(given.mesh_sender),
        flat(given.mesh_receiver),
        given.mesh_latents,
        given.g2m_edges,
        given.enc_edge_w1,
        flat(given.enc_edge_b1),
        given.embed_w1,
        flat(given.embed_b1),
        given.embed_w2,
        flat(given.embed_gain),
        given.enc_edge_w2,
        flat(given.enc_edge_gain),
        given.enc_node_w1,
        flat(given.enc_node_b1),
        given.enc_node_w2,
        flat(given.enc_node_gain),
        given.mesh_edges,
        given.proc_edge_w1,
        given.proc_edge_b1,
        given.proc_edge_w2,
        given.proc_edge_gain,
        given.proc_node_w1,
        given.proc_node_b1,
        given.proc_node_w2,
        given.proc_node_gain,
    )
    operands = [given.grid_inputs, *wanted]
    dma = pltpu.SemaphoreType.DMA
    scratch = [pltpu.VMEM(part.shape, part.dtype) for part in wanted]
    scratch += [
        pltpu.VMEM((lat_rows + 2 * HALO, lon_cols + 2 * HALO, batch, width), BF),
        pltpu.VMEM((2, GRID_EDGES), I32),
        pltpu.SMEM((2, GRID_EDGES), I32),
        pltpu.VMEM((GRID_EDGES, batch, width), BF),
        pltpu.VMEM((1, 2 * SLOTS), I32),
        pltpu.SMEM((1, 2 * SLOTS), I32),
        pltpu.VMEM((NODES, 2, D), BF),
        pltpu.VMEM((2 * EDGES, 2 * PAIRS), BF),
        pltpu.VMEM((2 * EDGES, CLOSE), BF),
        pltpu.VMEM((CLOSE, D), BF),
        pltpu.VMEM((2 * EDGES, D), F32),
        pltpu.VMEM((PAIRS, 2, 128), BF),
        pltpu.VMEM((PAIRS, 2, 128), BF),
        pltpu.VMEM((STEPS, SLOTS, 2, D), BF),
        pltpu.VMEM((STEPS, SLOTS, 2, D), BF),
        dma((FETCHED,)),
        dma((PIECES,)),
        dma,
        dma((len(DIRECTIONS),)),
        dma((len(DIRECTIONS),)),
        dma,
        dma,
        dma((STEPS,)),
        dma((STEPS,)),
        dma((STEPS,)),
        dma((STEPS,)),
        dma,
    ]
    return pl.pallas_call(
        kernel,
        out_shape=jax.ShapeDtypeStruct((NODES * batch, D), BF),
        in_specs=[pl.BlockSpec(memory_space=pl.ANY)] * len(operands),
        out_specs=pl.BlockSpec(memory_space=pltpu.VMEM),
        scratch_shapes=scratch,
        cost_estimate=pl.CostEstimate(
            flops=4 * 10**9, bytes_accessed=15 * 10**6, transcendentals=10**6
        ),
        compiler_params=pltpu.CompilerParams(
            collective_id=0, has_side_effects=True, vmem_limit_bytes=64 * 2**20
        ),
    )(*operands).reshape(NODES, batch, D)


def solution(mesh):
    nodes = P(("lat", "lon"), None)
    edges = P(("lat", "lon"))
    split = [P("lat", "lon", None, None), nodes, nodes, edges, edges, nodes, edges, edges]
    split += [P()] * (len(Given._fields) - len(split))
    return jax.shard_map(
        on_device,
        mesh=mesh,
        in_specs=tuple(split),
        out_specs=P(("lat", "lon"), None, None),
        check_vma=False,
    )
```
